32 devices in a mesh: rec: 4 (over z), tm: 8 (over y, x, core).
Axes of the slice: x: 2, y: 2, z: 4, core: 2. Of those that a mesh axis runs over, the one named last changes fastest.
Arguments:
- mel_frames: bfloat16 [4, 16384, 80], P('rec', 'tm'), may hold values from -6 to 6
- lengths: int32 [4, 4], P('rec'), may hold values from 1 to 8192, 16384 in all within a row
- w_first: float32 [3, 3, 256], replicated, may hold values from -2 to 2
- w_second: bfloat16 [2304, 256], P(('rec', 'tm')), may hold values from -0.125 to 0.125
- w_proj: bfloat16 [5120, 1024], P(('rec', 'tm')), may hold values from -0.078125 to 0.078125
- gain_attn: float32 [1024], replicated, may hold values from 0.5 to 1.5
- w_qkv: bfloat16 [1024, 3072], P(('rec', 'tm')), may hold values from -2 to 2
- w_out: bfloat16 [1024, 1024], P(('rec', 'tm')), may hold values from -0.1875 to 0.1875
- gain_conv: float32 [1024], replicated, may hold values from 0.5 to 1.5
- w_point_in: bfloat16 [1024, 2048], P(('rec', 'tm')), may hold values from -0.1875 to 0.1875
- w_depth: float32 [9, 1024], replicated, may hold values from -6 to 6
- w_point_out: bfloat16 [1024, 1024], P(('rec', 'tm')), may hold values from -0.375 to 0.375
- gain_out: float32 [1024], replicated, may hold values from 0.5 to 1.5
Outputs:
- encoded: bfloat16 [4, 4096, 1024], P('rec', 'tm')
The draws below stay inside these ranges and needn't reach their ends.
Inputs may be any that keep to these rules, and one draw needn't show every extreme that they name: Each group's 4 lengths sum to 16384, and the largest of them is 8192.
All inputs are finite; a program needn't handle non-finite values.
Results may differ from the reference program's by a relative error of at most 0.024.
The reference program's roundings to bfloat16 on the way count: a program that leaves them out, or rounds other values in their place, can miss the bound.
Values may be sent and summed in bfloat16 or wider, within the bound.
No kernel may reach another device: no remote copies, remote signals or barrier semaphores. Data moves between devices by JAX's collectives and lax.ppermute only.
A program may use at most 128 MiB of HBM per device.

```python
import math
import jax
import jax.numpy as jnp
import numpy as np
from jax import lax

MEL_BINS = 80
CHANNELS = 256
WIDTH = 1024
HEADS = 8
KERNEL = 9
WINDOW = 128
REC_GROUP = 4
CONV_BLOCK = 64
HEAD_DIM = 128
TOK_DEV = 512
FREQ_QUARTER = 20
FRAMES = 16384
GROUPS = 4


def draw_w_qkv(key, part):
    base_key = jax.random.fold_in(key, 0)
    return (jnp.clip(jax.random.normal(base_key, (WIDTH, 3 * WIDTH), jnp.float32), -6.0, 6.0) / math.sqrt(WIDTH)).astype(jnp.bfloat16)


def levels(key, dims, pieces, low, largest):
    loudness = 1.0
    for axis_at, parts in pieces:
        heights = jax.random.uniform(jax.random.fold_in(jax.random.fold_in(key, 6), axis_at), (parts,), jnp.float32, low / len(pieces), largest / len(pieces))
        loudness = loudness * jnp.repeat(jnp.exp(heights), dims[axis_at] // parts).reshape((-1,) + (1,) * (len(dims) - 1 - axis_at))
    return loudness


def profile(number_of, total, most, slope):
    loads = [(1 << 20) // math.isqrt(grade ** slope) + 1 for grade in range(2, number_of + 1)]
    rest, counts = total - most - (number_of - 1), [1] * (number_of - 1)
    while rest > 0:
        movable = [i for i in range(number_of - 1) if counts[i] < most]
        whole, left = sum([loads[i] for i in movable]), rest
        for i in movable:
            extra = min(most - counts[i], max(1, left * loads[i] // whole), rest)
            counts[i] = counts[i] + extra
            rest = rest - extra
    return np.array([most] + counts)


def ragged(key, count, total, bound, slope):
    if count == 2:
        one = jax.random.randint(key, (), max(1, total - bound), min(bound, total - 1) + 1)
        return jnp.stack([one, total - one])
    sizes = jnp.asarray(profile(count, total, bound, slope), jnp.int32)
    couples = (count - 1) // 2
    giver, receiver = sizes[1:1 + 2 * couples:2], sizes[2:2 + 2 * couples:2]
    room = jnp.minimum(giver - 1, bound - receiver)
    moved = jax.random.randint(jax.random.fold_in(key, 1), (couples,), 0, 1 << 20) % (room + 1)
    sizes = sizes.at[1:1 + 2 * couples:2].set(giver - moved).at[2:2 + 2 * couples:2].set(receiver + moved)
    return sizes[jax.random.permutation(jax.random.fold_in(key, 2), count)]


def noise(stream_key, shape, scale, most, pieces=(), held_as=jnp.bfloat16):
    result = scale * jax.random.normal(stream_key, shape, jnp.float32)
    if pieces:
        result = result * levels(stream_key, shape, pieces, -0.22, 0.18)
    return jnp.clip(result, -most, most).astype(held_as)


def setup_inputs(seed: int = 0) -> dict:
    key_of = jax.random.split(jax.random.key(seed), 14)
    mel_frames = noise(key_of[0], (GROUPS, FRAMES, MEL_BINS), 1.0, 6.0, ((0, 4), (1, 8)))
    lengths = jax.vmap(lambda own: ragged(own, REC_GROUP, FRAMES, FRAMES // 2, 2))(jax.random.split(key_of[1], GROUPS)).reshape((GROUPS, REC_GROUP)).astype(jnp.int32)
    w_first = noise(key_of[2], (3, 3, CHANNELS), 9 ** -0.5, 2.0, (), jnp.float32)
    w_second = noise(key_of[3], (9 * CHANNELS, CHANNELS), (9 * CHANNELS) ** -0.5, 0.125, ((0, 32),))
    w_proj = noise(key_of[4], (FREQ_QUARTER * CHANNELS, WIDTH), (FREQ_QUARTER * CHANNELS) ** -0.5, 0.078125, ((0, 32),))
    gain_attn = jnp.clip(1.0 + 0.1 * jax.random.normal(key_of[5], (WIDTH,), jnp.float32), 0.5, 1.5)
    w_qkv = draw_w_qkv(jax.random.fold_in(key_of[13], 71), 0)
    w_out = noise(key_of[7], (WIDTH, WIDTH), WIDTH ** -0.5, 0.1875, ((0, 32),))
    gain_conv = jnp.clip(1.0 + 0.1 * jax.random.normal(key_of[8], (WIDTH,), jnp.float32), 0.5, 1.5)
    w_point_in = noise(key_of[9], (WIDTH, 2 * WIDTH), WIDTH ** -0.5, 0.1875, ((0, 32),))
    w_depth = noise(key_of[10], (KERNEL, WIDTH), 1 ** -0.5, 6.0, (), jnp.float32)
    w_point_out = noise(key_of[11], (WIDTH, WIDTH), (WIDTH // 4) ** -0.5, 0.375, ((0, 32),))
    gain_out = jnp.clip(1.0 + 0.1 * jax.random.normal(key_of[12], (WIDTH,), jnp.float32), 0.5, 1.5)
    return dict(mel_frames=mel_frames, lengths=lengths, w_first=w_first, w_second=w_second, w_proj=w_proj, gain_attn=gain_attn, w_qkv=w_qkv, w_out=w_out, gain_conv=gain_conv, w_point_in=w_point_in, w_depth=w_depth, w_point_out=w_point_out, gain_out=gain_out)


NORM_EPSILON = 1e-05

def layer_norm(values, gain):
    row_mean = lax.optimization_barrier(jnp.mean(values, axis=-1, keepdims=True))
    centred = values - row_mean
    variance = lax.optimization_barrier(jnp.mean(centred * centred, axis=-1, keepdims=True))
    return centred * lax.rsqrt(variance + NORM_EPSILON) * gain

def segment_ids(positions, bounds, limit):
    counted = lax.optimization_barrier(jnp.sum((positions[:, None] >= bounds[None, :-1]).astype(jnp.int32), axis=1))
    inside = (positions >= 0) & (positions < limit)
    return jnp.where(inside, counted, -1).astype(jnp.int32)

def conv_first(window, seg_rows, w_first):
    frame_count = (window.shape[0] - 1) // 2
    bins = window.shape[1]
    padded = jnp.pad(window.astype(jnp.float32), ((0, 0), (1, 1)))
    centre = seg_rows[1:2 * frame_count:2]
    total = jnp.zeros((frame_count, bins // 2, w_first.shape[-1]), jnp.float32)
    for step_t in range(3):
        taken = padded[step_t:step_t + 2 * frame_count - 1:2]
        same_seg = (seg_rows[step_t:step_t + 2 * frame_count - 1:2] == centre).astype(jnp.float32)
        taken = taken * same_seg[:, None]
        for step_f in range(3):
            columns = taken[:, step_f:step_f + bins - 1:2]
            total = total + columns[:, :, None] * w_first[step_t, step_f][None, None, :]
    return jnp.maximum(total, 0.0).astype(jnp.bfloat16)

def conv_second(first, seg_first, w_second):
    frame_count = (first.shape[0] - 1) // 2
    channels = first.shape[2]
    quarter = first.shape[1] // 2
    padded = jnp.pad(first, ((0, 0), (1, 1), (0, 0)))
    centre = seg_first[1:2 * frame_count:2]
    total = jnp.zeros((frame_count * quarter, w_second.shape[1]), jnp.float32)
    for step_t in range(3):
        taken = padded[step_t:step_t + 2 * frame_count - 1:2]
        same_seg = (seg_first[step_t:step_t + 2 * frame_count - 1:2] == centre).astype(jnp.bfloat16)
        taken = taken * same_seg[:, None, None]
        for step_f in range(3):
            columns = taken[:, step_f:step_f + 2 * quarter - 1:2].reshape(frame_count * quarter, channels)
            offset = (step_t * 3 + step_f) * channels
            total = total + jnp.dot(columns, w_second[offset:offset + channels], preferred_element_type=jnp.float32)
    return jnp.maximum(total, 0.0).astype(jnp.bfloat16).reshape(frame_count, quarter * channels)

def local_attention(q_block, kv_block, q_seg, k_seg):
    row_count = q_block.shape[0]
    span = kv_block.shape[0]
    reach = (span - row_count) // 2
    offsets = jnp.arange(span, dtype=jnp.int32)[None, :] - jnp.arange(row_count, dtype=jnp.int32)[:, None] - reach
    allowed = (jnp.abs(offsets) <= reach) & (k_seg[None, :] == q_seg[:, None])
    q_heads = q_block.reshape(row_count, HEADS, HEAD_DIM).astype(jnp.float32)
    k_heads = kv_block[:, :WIDTH].reshape(span, HEADS, HEAD_DIM).astype(jnp.float32)
    v_heads = kv_block[:, WIDTH:].reshape(span, HEADS, HEAD_DIM).astype(jnp.float32)
    scores = jnp.einsum('qhd,khd->hqk', q_heads, k_heads) * HEAD_DIM ** (-0.5)
    scores = jnp.where(allowed[None], scores, -1e+30)
    row_max = lax.optimization_barrier(jnp.max(scores, axis=-1, keepdims=True))
    exped = jnp.where(allowed[None], jnp.exp(scores - row_max), 0.0)
    probabilities = (exped / lax.optimization_barrier(jnp.sum(exped, axis=-1, keepdims=True))).astype(jnp.bfloat16)
    context = jnp.einsum('hqk,khd->qhd', probabilities.astype(jnp.float32), v_heads)
    return context.astype(jnp.bfloat16).reshape(row_count, WIDTH)

def depthwise(gated_ext, seg_ext, seg_mid, w_depth):
    length = seg_mid.shape[0]
    total = jnp.zeros((length, gated_ext.shape[1]), jnp.float32)
    for tap_index in range(w_depth.shape[0]):
        same_seg = (seg_ext[tap_index:tap_index + length] == seg_mid).astype(jnp.float32)
        total = total + gated_ext[tap_index:tap_index + length].astype(jnp.float32) * w_depth[tap_index][None, :] * same_seg[:, None]
    return jax.nn.silu(total).astype(jnp.bfloat16)

def group_forward(mel_group, length_row, w_first, w_second, w_proj, gain_attn, w_qkv, w_out, gain_conv, w_point_in, w_depth, w_point_out, gain_out):
    bounds = jnp.cumsum(length_row).astype(jnp.int32)
    frame_total = mel_group.shape[0]
    token_total = frame_total // 4
    padded_mel = jnp.concatenate([jnp.zeros((3, MEL_BINS), mel_group.dtype), mel_group], axis=0)

    def sub_block(block):
        start = (block * CONV_BLOCK).astype(jnp.int32)
        window = lax.dynamic_slice_in_dim(padded_mel, 4 * start, 4 * CONV_BLOCK + 3, 0)
        positions = 4 * start - 3 + jnp.arange(4 * CONV_BLOCK + 3, dtype=jnp.int32)
        seg_rows = segment_ids(positions, bounds, frame_total)
        first = conv_first(window, seg_rows, w_first)
        return conv_second(first, seg_rows[1::2][:first.shape[0]], w_second)
    sub = lax.map(sub_block, jnp.arange(token_total // CONV_BLOCK, dtype=jnp.int32))
    sub = sub.reshape(token_total, sub.shape[-1])
    hidden = jnp.dot(sub, w_proj, preferred_element_type=jnp.float32)
    token_pos = jnp.arange(token_total, dtype=jnp.int32)
    token_seg = segment_ids(4 * token_pos, bounds, frame_total)
    normed = layer_norm(hidden, gain_attn).astype(jnp.bfloat16)
    mixed = jnp.dot(normed, w_qkv, preferred_element_type=jnp.float32).astype(jnp.bfloat16)
    query = mixed[:, :WIDTH]
    keyval = jnp.pad(mixed[:, WIDTH:], ((WINDOW, WINDOW), (0, 0)))
    key_seg = jnp.pad(token_seg, (WINDOW, WINDOW), constant_values=-1)
    block_rows = min(512, TOK_DEV)

    def attend(block):
        start = (block * block_rows).astype(jnp.int32)
        q_block = lax.dynamic_slice_in_dim(query, start, block_rows, 0)
        kv_block = lax.dynamic_slice_in_dim(keyval, start, block_rows + 2 * WINDOW, 0)
        q_seg = lax.dynamic_slice_in_dim(token_seg, start, block_rows, 0)
        k_seg = lax.dynamic_slice_in_dim(key_seg, start, block_rows + 2 * WINDOW, 0)
        return local_attention(q_block, kv_block, q_seg, k_seg)
    context = lax.map(attend, jnp.arange(token_total // block_rows, dtype=jnp.int32)).reshape(token_total, WIDTH)
    attended = hidden + jnp.dot(context, w_out, preferred_element_type=jnp.float32)
    normed_conv = layer_norm(attended, gain_conv).astype(jnp.bfloat16)
    upward = jnp.dot(normed_conv, w_point_in, preferred_element_type=jnp.float32)
    gated = (upward[:, :WIDTH] * jax.nn.sigmoid(upward[:, WIDTH:])).astype(jnp.bfloat16)
    reach = KERNEL // 2
    gated_ext = jnp.pad(gated, ((reach, reach), (0, 0)))
    seg_ext = jnp.pad(token_seg, (reach, reach), constant_values=-1)
    acted = depthwise(gated_ext, seg_ext, token_seg, w_depth)
    combined = attended + jnp.dot(acted, w_point_out, preferred_element_type=jnp.float32)
    return layer_norm(combined, gain_out).astype(jnp.bfloat16)

def reference(mel_frames, lengths, w_first, w_second, w_proj, gain_attn, w_qkv, w_out, gain_conv, w_point_in, w_depth, w_point_out, gain_out):

    def one_group(paired):
        return group_forward(paired[0], paired[1], w_first, w_second, w_proj, gain_attn, w_qkv, w_out, gain_conv, w_point_in, w_depth, w_point_out, gain_out)
    return lax.map(one_group, (mel_frames, lengths))
```

```python
import functools

import jax
import jax.numpy as jnp
import numpy as np
from jax import lax
from jax.experimental import pallas as pl
from jax.experimental.pallas import tpu as pltpu
from jax.sharding import PartitionSpec as P

WIDTH = 1024
HEADS = 8
HEAD_DIM = 128
KERNEL = 9
WINDOW = 128
CHANNELS = 256
NORM_EPSILON = 1e-05

EDGE = 16
HALO = WINDOW + EDGE
COLS = 256


def segment_of(positions, lengths, limit):
    counted = jnp.zeros(positions.shape, jnp.int32)
    bound = 0
    for k in range(len(lengths) - 1):
        bound = bound + lengths[k]
        counted = counted + (positions >= bound).astype(jnp.int32)
    return jnp.where((positions >= 0) & (positions < limit), counted, -1)


def layer_norm(values, gain):
    row_mean = jnp.mean(values, axis=-1, keepdims=True)
    centred = values - row_mean
    variance = jnp.mean(centred * centred, axis=-1, keepdims=True)
    return centred * lax.rsqrt(variance + NORM_EPSILON) * gain


def exchange(block, axis, distance):
    size = lax.axis_size(axis)
    return lax.ppermute(block, axis, [(i, i ^ distance) for i in range(size)])


def bit_groups():
    groups = []
    for axis, lowest in (("rec", 1), ("tm", 2)):
        bits = []
        bit = lowest
        while bit < lax.axis_size(axis):
            bits.append(bit)
            bit *= 2
        groups += [(axis, bits[k : k + 2]) for k in range(0, len(bits), 2)]
    return groups + [("tm", [1])]


def distances(bits):
    return [0] + [bits[0]] if len(bits) == 1 else [0, bits[0], bits[1], bits[0] + bits[1]]


def can_exchange():
    return all(
        lax.axis_size(axis) & (lax.axis_size(axis) - 1) == 0 and lax.axis_size(axis) > 1
        for axis in ("rec", "tm")
    )


def gather_ordered(block):
    if not can_exchange():
        return lax.all_gather(block, ("rec", "tm"), axis=0, tiled=True)
    groups = bit_groups()
    names = []
    rows = block.shape[0]
    held = block[None]
    for axis, bits in groups:
        got = [held] + [exchange(held, axis, d) for d in distances(bits)[1:]]
        me = lax.axis_index(axis)
        for at, bit in enumerate(bits):
            high = (me & bit) != 0
            got = [
                jnp.where(high, got[k ^ (1 << at)], got[k]) for k in range(len(got))
            ]
        held = jnp.concatenate(got, axis=0)
        names = [(axis, bit) for bit in reversed(bits)] + names
    wanted = []
    for axis in ("rec", "tm"):
        wanted += sorted((n for n in names if n[0] == axis), key=lambda n: -n[1])
    order = [names.index(n) for n in wanted]
    dims = held.reshape((2,) * len(names) + block.shape)
    dims = jnp.transpose(dims, order + [len(names), len(names) + 1])
    return dims.reshape((-1,) + block.shape[1:])


def gather_unordered(block):
    groups = bit_groups()
    held = block[None]
    held_bits = []
    for axis, bits in groups[:-2]:
        got = [held] + [exchange(held, axis, d) for d in distances(bits)[1:]]
        held = jnp.concatenate(got, axis=0)
        held_bits = held_bits + [(axis, bit) for bit in bits]
    axis, bits = groups[-2]
    parts = [(held, [])]
    for d in distances(bits)[1:]:
        parts.append((exchange(held, axis, d), [(axis, d)]))
    axis, bits = groups[-1]
    parts += [(exchange(part, axis, 1), far + [(axis, 1)]) for part, far in parts]
    return parts, held_bits


BINS = 41


def prepare_kernel(limit, info_ref, quads_ref, lane_ref, w_ref, patches_ref, taps_ref):
    base = info_ref[0]
    lengths = [info_ref[1 + k] for k in range(4)]
    tokens = quads_ref.shape[0]
    wide = quads_ref.shape[1]
    source = lax.broadcasted_iota(jnp.int32, (wide, COLS), 0)
    token = lax.broadcasted_iota(jnp.int32, (tokens, COLS), 0)
    own = segment_of(base + 4 * (token - HALO), lengths, limit)
    frame = lane_ref[6:7, :]
    for a in range(3):
        middle = segment_of(base + 4 * (token - HALO) + 2 * a - 2, lengths, limit)
        there = segment_of(base + 4 * (token - HALO) + 2 * a - 3 + frame, lengths, limit)
        same = (middle == own) & (there == middle)
        for h in range(2):
            chosen = (source == lane_ref[2 * a + h : 2 * a + h + 1, :]).astype(jnp.float32)
            made = jnp.dot(
                quads_ref[...], chosen.astype(jnp.bfloat16), preferred_element_type=jnp.float32
            )
            patches_ref[a, h] = jnp.where(same, made, 0.0).astype(jnp.bfloat16)

    row = lax.broadcasted_iota(jnp.int32, (COLS, CHANNELS), 0)
    group = jnp.zeros((COLS, CHANNELS), jnp.int32)
    for k in range(1, 7):
        group = group + (row >= BINS * k).astype(jnp.int32)
    at_bin = row - BINS * group
    spread = []
    for b in range(3):
        total = jnp.zeros((COLS, CHANNELS), jnp.float32)
        for a in range(3):
            tap = w_ref[3 * a + b : 3 * a + b + 1, :]
            high = tap.astype(jnp.bfloat16).astype(jnp.float32)
            total = jnp.where(group == a, high, total)
            total = jnp.where(group == 3 + a, tap - high, total)
        spread.append(total)
    for f in range(20):
        total = jnp.zeros((COLS, CHANNELS), jnp.float32)
        for b in range(3):
            total = jnp.where(at_bin == 2 * f + b, spread[b], total)
        taps_ref[:, f * CHANNELS : (f + 1) * CHANNELS] = total.astype(jnp.bfloat16)


def prepare(info, mel, w_first, tokens, limit):
    bins = mel.shape[1]
    reach = 4 * (HALO + EDGE)
    tm = lax.axis_size("tm")
    forward = [(i, i + 1) for i in range(tm - 1)]
    backward = [(i + 1, i) for i in range(tm - 1)]
    low = lax.ppermute(mel[mel.shape[0] - reach :], "tm", forward)
    high = lax.ppermute(mel[:reach], "tm", backward)
    quads = jnp.concatenate([low, mel, high], axis=0).reshape(-1, 4 * bins)
    count = tokens + 2 * HALO
    quads = jnp.concatenate(
        [quads[EDGE - 1 : EDGE - 1 + count], quads[EDGE : EDGE + count]], axis=1
    )
    lane = np.arange(COLS)
    frame, at_bin = lane // BINS % 3, lane % BINS
    used = lane < 6 * BINS
    picks = np.full((8, COLS), -1, np.int32)
    for a in range(3):
        for h in range(2):
            wanted = at_bin - 1 + 40 * h
            place = bins * (2 * a + frame + 1) + wanted
            picks[2 * a + h] = np.where(used & (wanted >= 0), place, -1)
    picks[6] = frame
    whole = pl.BlockSpec(memory_space=pltpu.VMEM)
    return pl.pallas_call(
        functools.partial(prepare_kernel, limit),
        out_shape=(
            jax.ShapeDtypeStruct((3, 2, count, COLS), jnp.bfloat16),
            jax.ShapeDtypeStruct((COLS, 20 * CHANNELS), jnp.bfloat16),
        ),
        in_specs=[pl.BlockSpec(memory_space=pltpu.SMEM)] + [whole] * 3,
        out_specs=(whole, whole),
        compiler_params=pltpu.CompilerParams(vmem_limit_bytes=24 * 1024 * 1024),
        cost_estimate=pl.CostEstimate(
            flops=12 * count * 768 * COLS, bytes_accessed=6 * 1024 * 1024, transcendentals=0
        ),
        name="prepare",
    )(info, quads, jnp.asarray(picks), w_first.reshape(9, CHANNELS))


def conv_kernel(begin, count, a_ref, b_ref, w_ref, out_ref, first):
    tokens = out_ref.shape[0]
    rows_step = tokens // 2

    @pl.loop(0, 2)
    def _(r):
        rows = pl.ds(pl.multiple_of(r * rows_step, 16), rows_step)
        for a in range(3):
            for i in range(2 * count + 1):
                at = 2 * begin - 1 + i
                place = slice(i * COLS, (i + 1) * COLS)
                if at < 0:
                    first[a, :, place] = jnp.zeros((rows_step, COLS), jnp.bfloat16)
                    continue
                half, col = divmod(at, 20)
                made = jnp.dot(
                    a_ref[a, half, rows, :],
                    b_ref[:, col * COLS : (col + 1) * COLS],
                    preferred_element_type=jnp.float32,
                )
                first[a, :, place] = jnp.maximum(made, 0.0).astype(jnp.bfloat16)
        for t in range(count):
            total = None
            for a in range(3):
                made = jnp.dot(
                    first[a, :, 2 * t * COLS : (2 * t + 3) * COLS],
                    w_ref[a],
                    preferred_element_type=jnp.float32,
                )
                total = made if total is None else total + made
            out_ref[rows, t * COLS : (t + 1) * COLS] = jnp.maximum(total, 0.0).astype(jnp.bfloat16)


def subsample(patches, taps, w_second):
    tokens = patches.shape[2]
    count = 4
    weights = w_second.reshape(3, 3 * COLS, COLS)
    whole = pl.BlockSpec(memory_space=pltpu.VMEM)
    flops = 2 * tokens * COLS * COLS * (3 * (2 * count + 1) + 9 * count)
    pieces = []
    for begin in range(0, 20, count):
        pieces.append(
            pl.pallas_call(
                functools.partial(conv_kernel, begin, count),
                out_shape=jax.ShapeDtypeStruct((tokens, count * CHANNELS), jnp.bfloat16),
                in_specs=[whole] * 3,
                out_specs=whole,
                scratch_shapes=[
                    pltpu.VMEM((3, tokens // 2, (2 * count + 1) * COLS), jnp.bfloat16)
                ],
                compiler_params=pltpu.CompilerParams(vmem_limit_bytes=20 * 1024 * 1024),
                cost_estimate=pl.CostEstimate(
                    flops=flops, bytes_accessed=8 * 1024 * 1024, transcendentals=0
                ),
                name="subsample",
            )(patches, taps, weights)
        )
    return pieces


def project_kernel(places, held_bits, info_ref, gain_ref, *rest):
    subs = rest[:5]
    sources = rest[5 : 5 + len(places)]
    mid_ref, normed_ref, weights, hidden, sem = rest[5 + len(places) :]
    rec, tm, tm_size = info_ref[5], info_ref[6], info_ref[7]

    rows = sources[0].shape[-2]
    if held_bits is None:
        pltpu.make_async_copy(sources[0], weights, sem).start()
    else:
        for source, far in zip(sources, places):
            far_rec = sum(d for axis, d in far if axis == "rec")
            far_tm = sum(d for axis, d in far if axis == "tm")
            for slot in range(1 << len(held_bits)):
                own_rec, own_tm = far_rec, far_tm
                for k, (axis, bit) in enumerate(held_bits):
                    if slot >> k & 1:
                        own_rec += bit if axis == "rec" else 0
                        own_tm += bit if axis == "tm" else 0
                owner = (rec ^ own_rec) * tm_size + (tm ^ own_tm)
                place = pl.ds(pl.multiple_of(owner * rows, 16), rows)
                pltpu.make_async_copy(source.at[slot], weights.at[place, :], sem).start()
    pltpu.make_async_copy(weights, weights, sem).wait()

    depth = weights.shape[0] // len(subs)

    @pl.loop(0, WIDTH // COLS)
    def _(n):
        here = pl.ds(pl.multiple_of(n * COLS, COLS), COLS)
        total = None
        for piece, sub in enumerate(subs):
            made = jnp.dot(
                sub[...],
                weights[piece * depth : (piece + 1) * depth, here],
                preferred_element_type=jnp.float32,
            )
            total = made if total is None else total + made
        hidden[:, here] = total

    gain = gain_ref[...]
    chunk = 160

    @pl.loop(0, hidden.shape[0] // chunk)
    def _(r):
        rows = pl.ds(pl.multiple_of(r * chunk, chunk), chunk)
        normed_ref[rows, :] = layer_norm(hidden[rows, :], gain).astype(jnp.bfloat16)

    mid_ref[...] = hidden[WINDOW : WINDOW + mid_ref.shape[0], :]


def project(info, gain, subs, sources, places, held_bits, tokens):
    rows_all = tokens + 2 * HALO
    rows_mid = tokens + 2 * EDGE
    whole = pl.BlockSpec(memory_space=pltpu.VMEM)
    depth = sum(sub.shape[1] for sub in subs)
    return pl.pallas_call(
        functools.partial(project_kernel, places, held_bits),
        out_shape=(
            jax.ShapeDtypeStruct((rows_mid, WIDTH), jnp.float32),
            jax.ShapeDtypeStruct((rows_all, WIDTH), jnp.bfloat16),
        ),
        in_specs=[pl.BlockSpec(memory_space=pltpu.SMEM)]
        + [whole] * 6
        + [pl.BlockSpec(memory_space=pl.ANY)] * len(sources),
        out_specs=(whole, whole),
        scratch_shapes=[
            pltpu.VMEM((depth, WIDTH), jnp.bfloat16),
            pltpu.VMEM((rows_all, WIDTH), jnp.float32),
            pltpu.SemaphoreType.DMA(()),
        ],
        compiler_params=pltpu.CompilerParams(vmem_limit_bytes=34 * 1024 * 1024),
        cost_estimate=pl.CostEstimate(
            flops=2 * rows_all * depth * WIDTH, bytes_accessed=24 * 1024 * 1024, transcendentals=0
        ),
        name="project",
    )(info, gain, *subs, *sources)


def pack_kernel(pieces, *refs):
    out_ref = refs[-1]
    at = 0
    for source, first in pieces:
        rows = refs[source].shape[0]
        out_ref[at : at + rows, :] = refs[source][:, first : first + WIDTH]
        at += rows


def pack(arrays):
    pieces = [
        (k, first) for k, array in enumerate(arrays) for first in range(0, array.shape[1], WIDTH)
    ]
    if any(array.shape[0] % 16 for array in arrays):
        return jnp.concatenate([arrays[k][:, c : c + WIDTH] for k, c in pieces], axis=0)
    rows = sum(arrays[k].shape[0] for k, _ in pieces)
    whole = pl.BlockSpec(memory_space=pltpu.VMEM)
    return pl.pallas_call(
        functools.partial(pack_kernel, pieces),
        out_shape=jax.ShapeDtypeStruct((rows, WIDTH), jnp.bfloat16),
        in_specs=[whole] * len(arrays),
        out_specs=whole,
        compiler_params=pltpu.CompilerParams(vmem_limit_bytes=4 * 1024 * 1024),
        cost_estimate=pl.CostEstimate(
            flops=0, bytes_accessed=4 * rows * WIDTH, transcendentals=0
        ),
        name="pack",
    )(*arrays)


def block_kernel(
    tokens,
    limit,
    plan,
    count,
    info_ref,
    hidden_ref,
    normed_ref,
    gain_conv_ref,
    depth_ref,
    gain_out_ref,
    *rest,
):
    sources = rest[:count]
    out_ref = rest[count]
    scratch = rest[count + 1 :]
    buffers = scratch[: len(plan)]
    keys, values, queries, context, attended, gated, masks, biases, sems = scratch[len(plan) :]
    rows_mid = tokens + 2 * EDGE
    mid = slice(WINDOW, WINDOW + rows_mid)
    copies = []
    for at, (source, offset, rows) in enumerate(plan):
        copies.append(
            pltpu.make_async_copy(
                sources[source].at[:, pl.ds(offset, rows), :], buffers[at], sems.at[at]
            )
        )
    for copy in copies:
        copy.start()
    base = info_ref[0]
    lengths = [info_ref[1 + k] for k in range(4)]

    def columns(at, n):
        part = buffers[at][:, :, pl.ds(pl.multiple_of(n * COLS, COLS), COLS)]
        return part.reshape(-1, COLS)

    def here(n):
        return pl.ds(pl.multiple_of(n * COLS, COLS), COLS)

    blocks = []
    at_row = 0
    while at_row < rows_mid:
        size = 128 + (EDGE if at_row == 0 or at_row + 128 + EDGE == rows_mid else 0)
        blocks.append((at_row, size))
        at_row += size

    row = lax.broadcasted_iota(jnp.int32, (tokens, HEAD_DIM), 0)
    own = segment_of(base + 4 * row, lengths, limit)
    for k in range(KERNEL):
        there = segment_of(base + 4 * (row + k - KERNEL // 2), lengths, limit)
        masks[k] = (there == own).astype(jnp.float32)
    for at, (start, size) in enumerate(blocks):
        span = size + 2 * WINDOW
        q_row = lax.broadcasted_iota(jnp.int32, (size, 1), 0)
        k_row = lax.broadcasted_iota(jnp.int32, (1, span), 1)
        q_seg = segment_of(base + 4 * (q_row + start - EDGE), lengths, limit)
        k_seg = segment_of(base + 4 * (k_row + start - HALO), lengths, limit)
        apart = k_row - q_row
        allowed = (apart >= 0) & (apart <= 2 * WINDOW) & (q_seg == k_seg)
        biases[at, 0:size, 0:span] = jnp.where(allowed, 0.0, -1e30)
    for head in range(HEADS):
        values[:, (2 * head + 1) * HEAD_DIM : (2 * head + 2) * HEAD_DIM] = jnp.ones(
            (values.shape[0], HEAD_DIM), jnp.bfloat16
        )

    copies[0].wait()

    @pl.loop(0, WIDTH // COLS)
    def _(n):
        queries[:, here(n)] = jnp.dot(
            normed_ref[mid, :], columns(0, n), preferred_element_type=jnp.float32
        ).astype(jnp.bfloat16)

    copies[1].wait()

    @pl.loop(0, WIDTH // COLS)
    def _(n):
        keys[:, here(n)] = jnp.dot(
            normed_ref[...], columns(1, n), preferred_element_type=jnp.float32
        ).astype(jnp.bfloat16)

    copies[2].wait()

    @pl.loop(0, WIDTH // COLS)
    def _(n):
        made = jnp.dot(
            normed_ref[...], columns(2, n), preferred_element_type=jnp.float32
        ).astype(jnp.bfloat16)
        for k in range(COLS // HEAD_DIM):
            lanes = pl.ds(pl.multiple_of(2 * n * COLS + 2 * k * HEAD_DIM, HEAD_DIM), HEAD_DIM)
            values[:, lanes] = made[:, k * HEAD_DIM : (k + 1) * HEAD_DIM]

    scale = HEAD_DIM**-0.5 * 1.4426950408889634

    @pl.loop(0, HEADS)
    def _(head):
        lanes = pl.ds(pl.multiple_of(head * HEAD_DIM, HEAD_DIM), HEAD_DIM)
        wide = pl.ds(pl.multiple_of(head * 2 * HEAD_DIM, 2 * HEAD_DIM), 2 * HEAD_DIM)
        for at, (start, size) in enumerate(blocks):
            span = size + 2 * WINDOW
            scores = lax.dot_general(
                queries[start : start + size, lanes],
                keys[start : start + span, lanes],
                (((1,), (1,)), ((), ())),
                preferred_element_type=jnp.float32,
            )
            scores = scores * scale + biases[at, 0:size, 0:span]
            exped = jnp.exp2(scores - jnp.max(scores, axis=-1, keepdims=True))
            mixed = jnp.dot(
                exped.astype(jnp.bfloat16),
                values[start : start + span, wide],
                preferred_element_type=jnp.float32,
            )
            context[start : start + size, lanes] = (
                mixed[:, :HEAD_DIM] / mixed[:, HEAD_DIM:]
            ).astype(jnp.bfloat16)

    copies[3].wait()

    @pl.loop(0, WIDTH // COLS)
    def _(n):
        attended[:, here(n)] = hidden_ref[:, here(n)] + jnp.dot(
            context[...], columns(3, n), preferred_element_type=jnp.float32
        )

    gain_c = gain_conv_ref[...]
    step_rows = rows_mid // 2

    @pl.loop(0, 2)
    def _(r):
        rows = pl.ds(pl.multiple_of(r * step_rows, 16), step_rows)
        queries[rows, :] = layer_norm(attended[rows, :], gain_c).astype(jnp.bfloat16)

    copies[4].wait()
    copies[5].wait()

    @pl.loop(0, WIDTH // COLS)
    def _(n):
        value = jnp.dot(queries[...], columns(4, n), preferred_element_type=jnp.float32)
        gate = jnp.dot(queries[...], columns(5, n), preferred_element_type=jnp.float32)
        made = (value * jax.nn.sigmoid(gate)).astype(jnp.bfloat16).astype(jnp.float32)
        for k in range(COLS // HEAD_DIM):
            gated[n * (COLS // HEAD_DIM) + k] = made[:, k * HEAD_DIM : (k + 1) * HEAD_DIM]

    @pl.loop(0, WIDTH // HEAD_DIM)
    def _(n):
        lanes = pl.ds(pl.multiple_of(n * HEAD_DIM, HEAD_DIM), HEAD_DIM)
        total = jnp.zeros((tokens, HEAD_DIM), jnp.float32)
        for k in range(KERNEL):
            begin = EDGE - KERNEL // 2 + k
            tap = gated[n, begin : begin + tokens, :] * depth_ref[k : k + 1, lanes]
            total = total + (tap if k == KERNEL // 2 else tap * masks[k])
        context[0:tokens, lanes] = (total * jax.nn.sigmoid(total)).astype(jnp.bfloat16)

    copies[6].wait()

    @pl.loop(0, WIDTH // COLS)
    def _(n):
        attended[EDGE : EDGE + tokens, here(n)] += jnp.dot(
            context[0:tokens, :], columns(6, n), preferred_element_type=jnp.float32
        )

    gain_o = gain_out_ref[...]

    @pl.loop(0, tokens // 128)
    def _(r):
        rows = pl.ds(pl.multiple_of(r * 128, 128), 128)
        taken = attended[pl.ds(pl.multiple_of(EDGE + r * 128, 16), 128), :]
        out_ref[rows, :] = layer_norm(taken, gain_o).astype(jnp.bfloat16)


def conformer_block(info, hidden, normed, sources, plan, gain_conv, w_depth, gain_out, limit):
    rows_all = normed.shape[0]
    rows_mid = hidden.shape[0]
    tokens = rows_mid - 2 * EDGE
    whole = pl.BlockSpec(memory_space=pltpu.VMEM)
    scratch = [
        pltpu.VMEM((sources[source].shape[0], rows, WIDTH), jnp.bfloat16)
        for source, _, rows in plan
    ]
    scratch += [
        pltpu.VMEM((rows_all, WIDTH), jnp.bfloat16),
        pltpu.VMEM((rows_all, 2 * WIDTH), jnp.bfloat16),
        pltpu.VMEM((rows_mid, WIDTH), jnp.bfloat16),
        pltpu.VMEM((rows_mid, WIDTH), jnp.bfloat16),
        pltpu.VMEM((rows_mid, WIDTH), jnp.float32),
        pltpu.VMEM((WIDTH // HEAD_DIM, rows_mid, HEAD_DIM), jnp.float32),
        pltpu.VMEM((KERNEL, tokens, HEAD_DIM), jnp.float32),
        pltpu.VMEM((4, 128 + EDGE, 512), jnp.float32),
        pltpu.SemaphoreType.DMA((len(plan),)),
    ]
    flops = 2 * rows_all * WIDTH * 2 * WIDTH + 2 * rows_mid * WIDTH * WIDTH * 5
    return pl.pallas_call(
        functools.partial(block_kernel, tokens, limit, plan, len(sources)),
        out_shape=jax.ShapeDtypeStruct((tokens, WIDTH), jnp.bfloat16),
        in_specs=[pl.BlockSpec(memory_space=pltpu.SMEM)]
        + [whole] * 5
        + [pl.BlockSpec(memory_space=pl.ANY)] * len(sources),
        out_specs=whole,
        scratch_shapes=scratch,
        compiler_params=pltpu.CompilerParams(vmem_limit_bytes=44 * 1024 * 1024),
        cost_estimate=pl.CostEstimate(
            flops=flops, bytes_accessed=24 * 1024 * 1024, transcendentals=4 * 1024 * 1024
        ),
        name="conformer_block",
    )(info, hidden, normed, gain_conv, w_depth, gain_out, *sources)


def on_device(
    mel_frames,
    lengths,
    w_first,
    w_second,
    w_proj,
    gain_attn,
    w_qkv,
    w_out,
    gain_conv,
    w_point_in,
    w_depth,
    w_point_out,
    gain_out,
):
    tokens = mel_frames.shape[1] // 4
    limit = mel_frames.shape[1] * lax.axis_size("tm")
    base = lax.axis_index("tm") * mel_frames.shape[1]
    info = jnp.concatenate(
        [
            jnp.reshape(base, (1,)),
            lengths[0],
            jnp.stack([lax.axis_index("rec"), lax.axis_index("tm")]),
            jnp.full((1,), lax.axis_size("tm"), jnp.int32),
        ]
    ).astype(jnp.int32)

    packed = pack([w_qkv, w_out, w_point_in, w_point_out])
    gathered = lax.all_gather(packed, ("rec", "tm"), axis=0, tiled=False)

    w_second_all = gather_ordered(w_second)
    if can_exchange() and w_proj.shape[0] % 16 == 0:
        parts, held_bits = gather_unordered(w_proj)
        places = [far for _, far in parts]
        proj_sources = [part for part, _ in parts]
    else:
        proj_sources = [lax.all_gather(w_proj, ("rec", "tm"), axis=0, tiled=True)]
        places, held_bits = [[]], None
    patches, taps = prepare(info, mel_frames[0], w_first, tokens, limit)
    subs = subsample(patches, taps, w_second_all)
    hidden, normed = project(info, gain_attn[None], subs, proj_sources, places, held_bits, tokens)

    share = w_out.shape[0]
    if share % 16 == 0:
        sources = [gathered]
        plan = [(0, k * share, share) for k in range(7)]
    else:
        sources = [
            gathered[:, k * share : (k + 1) * share].reshape(1, -1, WIDTH) for k in range(7)
        ]
        plan = [(k, 0, WIDTH) for k in range(7)]
    encoded = conformer_block(
        info,
        hidden,
        normed,
        sources,
        plan,
        gain_conv[None],
        w_depth,
        gain_out[None],
        limit,
    )
    return encoded[None]


def solution(mesh):
    placed = (
        P("rec", "tm", None),
        P("rec", None),
        P(),
        P(("rec", "tm"), None),
        P(("rec", "tm"), None),
        P(),
        P(("rec", "tm"), None),
        P(("rec", "tm"), None),
        P(),
        P(("rec", "tm"), None),
        P(),
        P(("rec", "tm"), None),
        P(),
    )
    return jax.shard_map(
        on_device, mesh=mesh, in_specs=placed, out_specs=P("rec", "tm", None), check_vma=False
    )
```

```python
import functools

import jax
import jax.numpy as jnp
import numpy as np
from jax import lax
from jax.experimental import pallas as pl
from jax.experimental.pallas import tpu as pltpu
from jax.sharding import PartitionSpec as P

WIDTH = 1024
HEADS = 8
HEAD_DIM = 128
KERNEL = 9
WINDOW = 128
CHANNELS = 256
NORM_EPSILON = 1e-05

EDGE = 16
HALO = WINDOW + EDGE
COLS = 256


def segment_of(positions, lengths, limit):
    counted = jnp.zeros(positions.shape, jnp.int32)
    bound = 0
    for k in range(len(lengths) - 1):
        bound = bound + lengths[k]
        counted = counted + (positions >= bound).astype(jnp.int32)
    return jnp.where((positions >= 0) & (positions < limit), counted, -1)


def layer_norm(values, gain):
    row_mean = jnp.mean(values, axis=-1, keepdims=True)
    centred = values - row_mean
    variance = jnp.mean(centred * centred, axis=-1, keepdims=True)
    return centred * lax.rsqrt(variance + NORM_EPSILON) * gain


def exchange(block, axis, distance):
    size = lax.axis_size(axis)
    return lax.ppermute(block, axis, [(i, i ^ distance) for i in range(size)])


def bit_groups():
    groups = []
    for axis, lowest in (("rec", 1), ("tm", 2)):
        bits = []
        bit = lowest
        while bit < lax.axis_size(axis):
            bits.append(bit)
            bit *= 2
        groups += [(axis, bits[k : k + 2]) for k in range(0, len(bits), 2)]
    return groups + [("tm", [1])]


def distances(bits):
    return [0] + [bits[0]] if len(bits) == 1 else [0, bits[0], bits[1], bits[0] + bits[1]]


def can_exchange():
    return all(
        lax.axis_size(axis) & (lax.axis_size(axis) - 1) == 0 and lax.axis_size(axis) > 1
        for axis in ("rec", "tm")
    )


def gather_ordered(block):
    if not can_exchange():
        return lax.all_gather(block, ("rec", "tm"), axis=0, tiled=True)
    groups = bit_groups()
    names = []
    rows = block.shape[0]
    held = block[None]
    for axis, bits in groups:
        got = [held] + [exchange(held, axis, d) for d in distances(bits)[1:]]
        me = lax.axis_index(axis)
        for at, bit in enumerate(bits):
            high = (me & bit) != 0
            got = [
                jnp.where(high, got[k ^ (1 << at)], got[k]) for k in range(len(got))
            ]
        held = jnp.concatenate(got, axis=0)
        names = [(axis, bit) for bit in reversed(bits)] + names
    wanted = []
    for axis in ("rec", "tm"):
        wanted += sorted((n for n in names if n[0] == axis), key=lambda n: -n[1])
    order = [names.index(n) for n in wanted]
    dims = held.reshape((2,) * len(names) + block.shape)
    dims = jnp.transpose(dims, order + [len(names), len(names) + 1])
    return dims.reshape((-1,) + block.shape[1:])


def gather_relayed(block, whole_rec, after):
    if whole_rec:
        held = lax.all_gather(block, "rec", axis=0, tiled=True)
    else:
        held = jnp.concatenate([block] + [exchange(block, "rec", d) for d in (1, 2, 3)], axis=0)
    if after:
        held = lax.optimization_barrier((held, *after))[0]
    half = held.shape[0] // 2
    beside = exchange(held, "tm", 2)
    above = exchange(held, "tm", 4)
    low = exchange(beside[:half], "tm", 4)
    high = exchange(above[half:], "tm", 2)
    pieces = [(held, 0, 0, 4), (beside, 2, 0, 4), (above, 4, 0, 4), (low, 6, 0, 2), (high, 6, 2, 2)]
    pieces += [(exchange(p, "tm", 1), far ^ 1, slot, n) for p, far, slot, n in pieces]
    return [p[0] for p in pieces], [p[1:] + (whole_rec,) for p in pieces], [low, high]


def copies_in(info_ref, sources, places, target, sem):
    if places is None:
        pltpu.make_async_copy(sources[0], target, sem).start()
        return
    rec, tm, tm_size = info_ref[5], info_ref[6], info_ref[7]
    for source, (far, first, number, indices) in zip(sources, places):
        rows = source.shape[0] // number
        for slot in range(number):
            owner_rec = first + slot if indices else rec ^ (first + slot)
            owner = owner_rec * tm_size + (tm ^ far)
            if len(target.shape) == 3:
                place = target.at[owner]
            else:
                place = target.at[pl.ds(pl.multiple_of(owner * rows, 16), rows), :]
            pltpu.make_async_copy(source.at[pl.ds(slot * rows, rows), :], place, sem).start()


BINS = 41


def prepare_kernel(limit, info_ref, quads_ref, lane_ref, w_ref, patches_ref, taps_ref):
    base = info_ref[0]
    lengths = [info_ref[1 + k] for k in range(4)]
    tokens = quads_ref.shape[0]
    wide = quads_ref.shape[1]
    source = lax.broadcasted_iota(jnp.int32, (wide, COLS), 0)
    token = lax.broadcasted_iota(jnp.int32, (tokens, COLS), 0)
    own = segment_of(base + 4 * (token - HALO), lengths, limit)
    frame = lane_ref[6:7, :]
    for a in range(3):
        middle = segment_of(base + 4 * (token - HALO) + 2 * a - 2, lengths, limit)
        there = segment_of(base + 4 * (token - HALO) + 2 * a - 3 + frame, lengths, limit)
        same = (middle == own) & (there == middle)
        for h in range(2):
            chosen = (source == lane_ref[2 * a + h : 2 * a + h + 1, :]).astype(jnp.float32)
            made = jnp.dot(
                quads_ref[...], chosen.astype(jnp.bfloat16), preferred_element_type=jnp.float32
            )
            patches_ref[a, h] = jnp.where(same, made, 0.0).astype(jnp.bfloat16)

    row = lax.broadcasted_iota(jnp.int32, (COLS, CHANNELS), 0)
    group = jnp.zeros((COLS, CHANNELS), jnp.int32)
    for k in range(1, 7):
        group = group + (row >= BINS * k).astype(jnp.int32)
    at_bin = row - BINS * group
    spread = []
    for b in range(3):
        total = jnp.zeros((COLS, CHANNELS), jnp.float32)
        for a in range(3):
            tap = w_ref[3 * a + b : 3 * a + b + 1, :]
            high = tap.astype(jnp.bfloat16).astype(jnp.float32)
            total = jnp.where(group == a, high, total)
            total = jnp.where(group == 3 + a, tap - high, total)
        spread.append(total)
    for f in range(20):
        total = jnp.zeros((COLS, CHANNELS), jnp.float32)
        for b in range(3):
            total = jnp.where(at_bin == 2 * f + b, spread[b], total)
        taps_ref[:, f * CHANNELS : (f + 1) * CHANNELS] = total.astype(jnp.bfloat16)


def prepare(info, mel, w_first, tokens, limit):
    bins = mel.shape[1]
    reach = 4 * (HALO + EDGE)
    tm = lax.axis_size("tm")
    forward = [(i, i + 1) for i in range(tm - 1)]
    backward = [(i + 1, i) for i in range(tm - 1)]
    low = lax.ppermute(mel[mel.shape[0] - reach :], "tm", forward)
    high = lax.ppermute(mel[:reach], "tm", backward)
    quads = jnp.concatenate([low, mel, high], axis=0).reshape(-1, 4 * bins)
    count = tokens + 2 * HALO
    quads = jnp.concatenate(
        [quads[EDGE - 1 : EDGE - 1 + count], quads[EDGE : EDGE + count]], axis=1
    )
    lane = np.arange(COLS)
    frame, at_bin = lane // BINS % 3, lane % BINS
    used = lane < 6 * BINS
    picks = np.full((8, COLS), -1, np.int32)
    for a in range(3):
        for h in range(2):
            wanted = at_bin - 1 + 40 * h
            place = bins * (2 * a + frame + 1) + wanted
            picks[2 * a + h] = np.where(used & (wanted >= 0), place, -1)
    picks[6] = frame
    whole = pl.BlockSpec(memory_space=pltpu.VMEM)
    return pl.pallas_call(
        functools.partial(prepare_kernel, limit),
        out_shape=(
            jax.ShapeDtypeStruct((3, 2, count, COLS), jnp.bfloat16),
            jax.ShapeDtypeStruct((COLS, 20 * CHANNELS), jnp.bfloat16),
        ),
        in_specs=[pl.BlockSpec(memory_space=pltpu.SMEM)] + [whole] * 3,
        out_specs=(whole, whole),
        compiler_params=pltpu.CompilerParams(vmem_limit_bytes=24 * 1024 * 1024),
        cost_estimate=pl.CostEstimate(
            flops=12 * count * 768 * COLS, bytes_accessed=6 * 1024 * 1024, transcendentals=0
        ),
        name="prepare",
    )(info, quads, jnp.asarray(picks), w_first.reshape(9, CHANNELS))


def conv_kernel(begin, count, a_ref, b_ref, w_ref, out_ref, first):
    tokens = out_ref.shape[0]
    rows_step = tokens // 2

    @pl.loop(0, 2)
    def _(r):
        rows = pl.ds(pl.multiple_of(r * rows_step, 16), rows_step)
        for a in range(3):
            for i in range(2 * count + 1):
                at = 2 * begin - 1 + i
                place = slice(i * COLS, (i + 1) * COLS)
                if at < 0:
                    first[a, :, place] = jnp.zeros((rows_step, COLS), jnp.bfloat16)
                    continue
                half, col = divmod(at, 20)
                made = jnp.dot(
                    a_ref[a, half, rows, :],
                    b_ref[:, col * COLS : (col + 1) * COLS],
                    preferred_element_type=jnp.float32,
                )
                first[a, :, place] = jnp.maximum(made, 0.0).astype(jnp.bfloat16)
        for t in range(count):
            total = None
            for a in range(3):
                made = jnp.dot(
                    first[a, :, 2 * t * COLS : (2 * t + 3) * COLS],
                    w_ref[a],
                    preferred_element_type=jnp.float32,
                )
                total = made if total is None else total + made
            out_ref[rows, t * COLS : (t + 1) * COLS] = jnp.maximum(total, 0.0).astype(jnp.bfloat16)


def subsample(patches, taps, w_second):
    tokens = patches.shape[2]
    count = 4
    weights = w_second.reshape(3, 3 * COLS, COLS)
    whole = pl.BlockSpec(memory_space=pltpu.VMEM)
    flops = 2 * tokens * COLS * COLS * (3 * (2 * count + 1) + 9 * count)
    pieces = []
    for begin in range(0, 20, count):
        pieces.append(
            pl.pallas_call(
                functools.partial(conv_kernel, begin, count),
                out_shape=jax.ShapeDtypeStruct((tokens, count * CHANNELS), jnp.bfloat16),
                in_specs=[whole] * 3,
                out_specs=whole,
                scratch_shapes=[
                    pltpu.VMEM((3, tokens // 2, (2 * count + 1) * COLS), jnp.bfloat16)
                ],
                compiler_params=pltpu.CompilerParams(vmem_limit_bytes=20 * 1024 * 1024),
                cost_estimate=pl.CostEstimate(
                    flops=flops, bytes_accessed=8 * 1024 * 1024, transcendentals=0
                ),
                name="subsample",
            )(patches, taps, weights)
        )
    return pieces


def project_kernel(places, info_ref, gain_ref, *rest):
    subs = rest[:5]
    sources = rest[5:-5]
    mid_ref, normed_ref, weights, hidden, sem = rest[-5:]
    copies_in(info_ref, sources, places, weights, sem)
    pltpu.make_async_copy(weights, weights, sem).wait()

    depth = weights.shape[0] // len(subs)

    @pl.loop(0, WIDTH // COLS)
    def _(n):
        here = pl.ds(pl.multiple_of(n * COLS, COLS), COLS)
        total = None
        for piece, sub in enumerate(subs):
            made = jnp.dot(
                sub[...],
                weights[piece * depth : (piece + 1) * depth, here],
                preferred_element_type=jnp.float32,
            )
            total = made if total is None else total + made
        hidden[:, here] = total

    gain = gain_ref[...]
    chunk = 160

    @pl.loop(0, hidden.shape[0] // chunk)
    def _(r):
        rows = pl.ds(pl.multiple_of(r * chunk, chunk), chunk)
        normed_ref[rows, :] = layer_norm(hidden[rows, :], gain).astype(jnp.bfloat16)

    mid_ref[...] = hidden[WINDOW : WINDOW + mid_ref.shape[0], :]


def project(info, gain, subs, sources, places, tokens):
    rows_all = tokens + 2 * HALO
    rows_mid = tokens + 2 * EDGE
    whole = pl.BlockSpec(memory_space=pltpu.VMEM)
    depth = sum(sub.shape[1] for sub in subs)
    return pl.pallas_call(
        functools.partial(project_kernel, places),
        out_shape=(
            jax.ShapeDtypeStruct((rows_mid, WIDTH), jnp.float32),
            jax.ShapeDtypeStruct((rows_all, WIDTH), jnp.bfloat16),
        ),
        in_specs=[pl.BlockSpec(memory_space=pltpu.SMEM)]
        + [whole] * 6
        + [pl.BlockSpec(memory_space=pl.ANY)] * len(sources),
        out_specs=(whole, whole),
        scratch_shapes=[
            pltpu.VMEM((depth, WIDTH), jnp.bfloat16),
            pltpu.VMEM((rows_all, WIDTH), jnp.float32),
            pltpu.SemaphoreType.DMA(()),
        ],
        compiler_params=pltpu.CompilerParams(vmem_limit_bytes=34 * 1024 * 1024),
        cost_estimate=pl.CostEstimate(
            flops=2 * rows_all * depth * WIDTH, bytes_accessed=24 * 1024 * 1024, transcendentals=0
        ),
        name="project",
    )(info, gain, *subs, *sources)


def pack_kernel(pieces, *refs):
    out_ref = refs[-1]
    at = 0
    for source, first in pieces:
        rows = refs[source].shape[0]
        out_ref[at : at + rows, :] = refs[source][:, first : first + WIDTH]
        at += rows


def pack(arrays):
    pieces = [
        (k, first) for k, array in enumerate(arrays) for first in range(0, array.shape[1], WIDTH)
    ]
    if any(array.shape[0] % 16 for array in arrays):
        return jnp.concatenate([arrays[k][:, c : c + WIDTH] for k, c in pieces], axis=0)
    rows = sum(arrays[k].shape[0] for k, _ in pieces)
    whole = pl.BlockSpec(memory_space=pltpu.VMEM)
    return pl.pallas_call(
        functools.partial(pack_kernel, pieces),
        out_shape=jax.ShapeDtypeStruct((rows, WIDTH), jnp.bfloat16),
        in_specs=[whole] * len(arrays),
        out_specs=whole,
        compiler_params=pltpu.CompilerParams(vmem_limit_bytes=4 * 1024 * 1024),
        cost_estimate=pl.CostEstimate(
            flops=0, bytes_accessed=4 * rows * WIDTH, transcendentals=0
        ),
        name="pack",
    )(*arrays)


def columns(weights, part, parts, n):
    rows = weights.shape[1] // parts
    here = pl.ds(pl.multiple_of(n * COLS, COLS), COLS)
    return weights[:, part * rows : (part + 1) * rows, here].reshape(-1, COLS)


def attention_kernel(tokens, limit, places, info_ref, normed_ref, *rest):
    sources = rest[:-7]
    context_ref, weights, keys, values, queries, biases, sem = rest[-7:]
    rows_mid = tokens + 2 * EDGE
    copies_in(info_ref, sources, places, weights, sem)
    base = info_ref[0]
    lengths = [info_ref[1 + k] for k in range(4)]

    blocks = []
    at_row = 0
    while at_row < rows_mid:
        size = 128 + (EDGE if at_row == 0 or at_row + 128 + EDGE == rows_mid else 0)
        blocks.append((at_row, size))
        at_row += size

    for at, (start, size) in enumerate(blocks):
        span = size + 2 * WINDOW
        q_row = lax.broadcasted_iota(jnp.int32, (size, 1), 0)
        k_row = lax.broadcasted_iota(jnp.int32, (1, span), 1)
        q_seg = segment_of(base + 4 * (q_row + start - EDGE), lengths, limit)
        k_seg = segment_of(base + 4 * (k_row + start - HALO), lengths, limit)
        apart = k_row - q_row
        allowed = (apart >= 0) & (apart <= 2 * WINDOW) & (q_seg == k_seg)
        biases[at, 0:size, 0:span] = jnp.where(allowed, 0.0, -1e30)
    for head in range(HEADS):
        values[:, (2 * head + 1) * HEAD_DIM : (2 * head + 2) * HEAD_DIM] = jnp.ones(
            (values.shape[0], HEAD_DIM), jnp.bfloat16
        )

    pltpu.make_async_copy(weights, weights, sem).wait()

    @pl.loop(0, WIDTH // COLS)
    def _(n):
        here = pl.ds(pl.multiple_of(n * COLS, COLS), COLS)
        queries[:, here] = jnp.dot(
            normed_ref[WINDOW : WINDOW + rows_mid, :],
            columns(weights, 0, 3, n),
            preferred_element_type=jnp.float32,
        ).astype(jnp.bfloat16)
        keys[:, here] = jnp.dot(
            normed_ref[...], columns(weights, 1, 3, n), preferred_element_type=jnp.float32
        ).astype(jnp.bfloat16)
        made = jnp.dot(
            normed_ref[...], columns(weights, 2, 3, n), preferred_element_type=jnp.float32
        ).astype(jnp.bfloat16)
        for k in range(COLS // HEAD_DIM):
            lanes = pl.ds(pl.multiple_of(2 * n * COLS + 2 * k * HEAD_DIM, HEAD_DIM), HEAD_DIM)
            values[:, lanes] = made[:, k * HEAD_DIM : (k + 1) * HEAD_DIM]

    scale = HEAD_DIM**-0.5 * 1.4426950408889634

    @pl.loop(0, HEADS)
    def _(head):
        lanes = pl.ds(pl.multiple_of(head * HEAD_DIM, HEAD_DIM), HEAD_DIM)
        wide = pl.ds(pl.multiple_of(head * 2 * HEAD_DIM, 2 * HEAD_DIM), 2 * HEAD_DIM)
        for at, (start, size) in enumerate(blocks):
            span = size + 2 * WINDOW
            scores = lax.dot_general(
                queries[start : start + size, lanes],
                keys[start : start + span, lanes],
                (((1,), (1,)), ((), ())),
                preferred_element_type=jnp.float32,
            )
            scores = scores * scale + biases[at, 0:size, 0:span]
            exped = jnp.exp2(scores - jnp.max(scores, axis=-1, keepdims=True))
            mixed = jnp.dot(
                exped.astype(jnp.bfloat16),
                values[start : start + span, wide],
                preferred_element_type=jnp.float32,
            )
            context_ref[start : start + size, lanes] = (
                mixed[:, :HEAD_DIM] / mixed[:, HEAD_DIM:]
            ).astype(jnp.bfloat16)


def attend(info, normed, sources, places, limit):
    rows_all = normed.shape[0]
    tokens = rows_all - 2 * HALO
    rows_mid = tokens + 2 * EDGE
    whole = pl.BlockSpec(memory_space=pltpu.VMEM)
    flops = 2 * WIDTH * (rows_all * 2 * WIDTH + rows_mid * WIDTH + 3 * rows_mid * 400)
    return pl.pallas_call(
        functools.partial(attention_kernel, tokens, limit, places),
        out_shape=jax.ShapeDtypeStruct((rows_mid, WIDTH), jnp.bfloat16),
        in_specs=[pl.BlockSpec(memory_space=pltpu.SMEM), whole]
        + [pl.BlockSpec(memory_space=pl.ANY)] * len(sources),
        out_specs=whole,
        scratch_shapes=[
            pltpu.VMEM((32, 3 * WIDTH // 32, WIDTH), jnp.bfloat16),
            pltpu.VMEM((rows_all, WIDTH), jnp.bfloat16),
            pltpu.VMEM((rows_all, 2 * WIDTH), jnp.bfloat16),
            pltpu.VMEM((rows_mid, WIDTH), jnp.bfloat16),
            pltpu.VMEM((4, 128 + EDGE, 512), jnp.float32),
            pltpu.SemaphoreType.DMA(()),
        ],
        compiler_params=pltpu.CompilerParams(vmem_limit_bytes=26 * 1024 * 1024),
        cost_estimate=pl.CostEstimate(
            flops=flops, bytes_accessed=10 * 1024 * 1024, transcendentals=2 * 1024 * 1024
        ),
        name="attend",
    )(info, normed, *sources)


def final_kernel(
    tokens,
    limit,
    places,
    info_ref,
    hidden_ref,
    context_ref,
    gain_conv_ref,
    depth_ref,
    gain_out_ref,
    *rest,
):
    sources = rest[:-8]
    out_ref, weights, attended, normed, gated, acted, masks, sem = rest[-8:]
    rows_mid = tokens + 2 * EDGE
    copies_in(info_ref, sources, places, weights, sem)
    base = info_ref[0]
    lengths = [info_ref[1 + k] for k in range(4)]

    row = lax.broadcasted_iota(jnp.int32, (tokens, HEAD_DIM), 0)
    own = segment_of(base + 4 * row, lengths, limit)
    for k in range(KERNEL):
        there = segment_of(base + 4 * (row + k - KERNEL // 2), lengths, limit)
        masks[k] = (there == own).astype(jnp.float32)

    pltpu.make_async_copy(weights, weights, sem).wait()

    @pl.loop(0, WIDTH // COLS)
    def _(n):
        here = pl.ds(pl.multiple_of(n * COLS, COLS), COLS)
        attended[:, here] = hidden_ref[:, here] + jnp.dot(
            context_ref[...], columns(weights, 0, 4, n), preferred_element_type=jnp.float32
        )

    gain_c = gain_conv_ref[...]
    step_rows = rows_mid // 2

    @pl.loop(0, 2)
    def _(r):
        rows = pl.ds(pl.multiple_of(r * step_rows, 16), step_rows)
        normed[rows, :] = layer_norm(attended[rows, :], gain_c).astype(jnp.bfloat16)

    @pl.loop(0, WIDTH // COLS)
    def _(n):
        value = jnp.dot(normed[...], columns(weights, 1, 4, n), preferred_element_type=jnp.float32)
        gate = jnp.dot(normed[...], columns(weights, 2, 4, n), preferred_element_type=jnp.float32)
        made = (value * jax.nn.sigmoid(gate)).astype(jnp.bfloat16).astype(jnp.float32)
        for j in range(COLS // HEAD_DIM):
            gated[...] = made[:, j * HEAD_DIM : (j + 1) * HEAD_DIM]
            lanes = pl.ds(pl.multiple_of(n * COLS + j * HEAD_DIM, HEAD_DIM), HEAD_DIM)
            total = jnp.zeros((tokens, HEAD_DIM), jnp.float32)
            for k in range(KERNEL):
                begin = EDGE - KERNEL // 2 + k
                tap = gated[begin : begin + tokens, :] * depth_ref[k : k + 1, lanes]
                total = total + (tap if k == KERNEL // 2 else tap * masks[k])
            acted[:, lanes] = (total * jax.nn.sigmoid(total)).astype(jnp.bfloat16)

    @pl.loop(0, WIDTH // COLS)
    def _(n):
        here = pl.ds(pl.multiple_of(n * COLS, COLS), COLS)
        attended[EDGE : EDGE + tokens, here] += jnp.dot(
            acted[...], columns(weights, 3, 4, n), preferred_element_type=jnp.float32
        )

    gain_o = gain_out_ref[...]

    @pl.loop(0, tokens // 128)
    def _(r):
        rows = pl.ds(pl.multiple_of(r * 128, 128), 128)
        taken = attended[pl.ds(pl.multiple_of(EDGE + r * 128, 16), 128), :]
        out_ref[rows, :] = layer_norm(taken, gain_o).astype(jnp.bfloat16)


def finish(info, hidden, context, sources, places, gain_conv, w_depth, gain_out, limit):
    rows_mid = hidden.shape[0]
    tokens = rows_mid - 2 * EDGE
    whole = pl.BlockSpec(memory_space=pltpu.VMEM)
    return pl.pallas_call(
        functools.partial(final_kernel, tokens, limit, places),
        out_shape=jax.ShapeDtypeStruct((tokens, WIDTH), jnp.bfloat16),
        in_specs=[pl.BlockSpec(memory_space=pltpu.SMEM)]
        + [whole] * 5
        + [pl.BlockSpec(memory_space=pl.ANY)] * len(sources),
        out_specs=whole,
        scratch_shapes=[
            pltpu.VMEM((32, 4 * WIDTH // 32, WIDTH), jnp.bfloat16),
            pltpu.VMEM((rows_mid, WIDTH), jnp.float32),
            pltpu.VMEM((rows_mid, WIDTH), jnp.bfloat16),
            pltpu.VMEM((rows_mid, HEAD_DIM), jnp.float32),
            pltpu.VMEM((tokens, WIDTH), jnp.bfloat16),
            pltpu.VMEM((KERNEL, tokens, HEAD_DIM), jnp.float32),
            pltpu.SemaphoreType.DMA(()),
        ],
        compiler_params=pltpu.CompilerParams(vmem_limit_bytes=30 * 1024 * 1024),
        cost_estimate=pl.CostEstimate(
            flops=8 * rows_mid * WIDTH * WIDTH,
            bytes_accessed=14 * 1024 * 1024,
            transcendentals=2 * 1024 * 1024,
        ),
        name="finish",
    )(info, hidden, context, gain_conv, w_depth, gain_out, *sources)


def on_device(
    mel_frames,
    lengths,
    w_first,
    w_second,
    w_proj,
    gain_attn,
    w_qkv,
    w_out,
    gain_conv,
    w_point_in,
    w_depth,
    w_point_out,
    gain_out,
):
    tokens = mel_frames.shape[1] // 4
    limit = mel_frames.shape[1] * lax.axis_size("tm")
    base = lax.axis_index("tm") * mel_frames.shape[1]
    info = jnp.concatenate(
        [
            jnp.reshape(base, (1,)),
            lengths[0],
            jnp.stack([lax.axis_index("rec"), lax.axis_index("tm")]),
            jnp.full((1,), lax.axis_size("tm"), jnp.int32),
        ]
    ).astype(jnp.int32)

    w_second_all = gather_ordered(w_second)
    rest = [w_qkv], [w_out, w_point_in, w_point_out]
    relayed = lax.axis_size("rec") == 4 and lax.axis_size("tm") == 8
    if relayed:
        gathered = [gather_relayed(w_proj, False, [])]
        for arrays in rest:
            gathered.append(gather_relayed(pack(arrays), True, gathered[-1][2]))
    else:
        full = lax.all_gather(w_proj, ("rec", "tm"), axis=0, tiled=True)
        gathered = [([full], None)]
        for arrays in rest:
            packed = pack(arrays)
            parts = packed.shape[0] // w_out.shape[0]
            full = lax.all_gather(packed, ("rec", "tm"), axis=0, tiled=False)
            full = full.reshape(full.shape[0], parts, -1, WIDTH).transpose(1, 0, 2, 3)
            full = full.reshape(parts, 32, -1, WIDTH).transpose(1, 0, 2, 3)
            gathered.append(([full.reshape(32, -1, WIDTH)], None))

    patches, taps = prepare(info, mel_frames[0], w_first, tokens, limit)
    subs = subsample(patches, taps, w_second_all)
    hidden, normed = project(info, gain_attn[None], subs, *gathered[0][:2], tokens)
    context = attend(info, normed, *gathered[1][:2], limit)
    encoded = finish(
        info,
        hidden,
        context,
        *gathered[2][:2],
        gain_conv[None],
        w_depth,
        gain_out[None],
        limit,
    )
    return encoded[None]


def solution(mesh):
    placed = (
        P("rec", "tm", None),
        P("rec", None),
        P(),
        P(("rec", "tm"), None),
        P(("rec", "tm"), None),
        P(),
        P(("rec", "tm"), None),
        P(("rec", "tm"), None),
        P(),
        P(("rec", "tm"), None),
        P(),
        P(("rec", "tm"), None),
        P(),
    )
    return jax.shard_map(
        on_device, mesh=mesh, in_specs=placed, out_specs=P("rec", "tm", None), check_vma=False
    )
```

```python
import functools

import jax
import jax.numpy as jnp
import numpy as np
from jax import lax
from jax.experimental import pallas as pl
from jax.experimental.pallas import tpu as pltpu
from jax.sharding import PartitionSpec as P

WIDTH = 1024
HEADS = 8
HEAD_DIM = 128
KERNEL = 9
WINDOW = 128
CHANNELS = 256
NORM_EPSILON = 1e-05

EDGE = 16
HALO = WINDOW + EDGE
COLS = 256


def segment_of(positions, lengths, limit):
    counted = jnp.zeros(positions.shape, jnp.int32)
    bound = 0
    for k in range(len(lengths) - 1):
        bound = bound + lengths[k]
        counted = counted + (positions >= bound).astype(jnp.int32)
    return jnp.where((positions >= 0) & (positions < limit), counted, -1)


def layer_norm(values, gain):
    row_mean = jnp.mean(values, axis=-1, keepdims=True)
    centred = values - row_mean
    variance = jnp.mean(centred * centred, axis=-1, keepdims=True)
    return centred * lax.rsqrt(variance + NORM_EPSILON) * gain


def exchange(block, axis, distance):
    size = lax.axis_size(axis)
    return lax.ppermute(block, axis, [(i, i ^ distance) for i in range(size)])


def bit_groups():
    groups = []
    for axis, lowest in (("rec", 1), ("tm", 2)):
        bits = []
        bit = lowest
        while bit < lax.axis_size(axis):
            bits.append(bit)
            bit *= 2
        groups += [(axis, bits[k : k + 2]) for k in range(0, len(bits), 2)]
    return groups + [("tm", [1])]


def distances(bits):
    return [0] + [bits[0]] if len(bits) == 1 else [0, bits[0], bits[1], bits[0] + bits[1]]


def can_exchange():
    return all(
        lax.axis_size(axis) & (lax.axis_size(axis) - 1) == 0 and lax.axis_size(axis) > 1
        for axis in ("rec", "tm")
    )


def behind(value, *others):
    return lax.optimization_barrier((value, *others))[0]


def gather_ordered(block):
    if not can_exchange():
        return lax.all_gather(block, ("rec", "tm"), axis=0, tiled=True), []
    names = []
    held = block[None]
    rounds = []
    for axis, bits in bit_groups():
        got = [held] + [exchange(held, axis, d) for d in distances(bits)[1:]]
        rounds.append(got[1:])
        me = lax.axis_index(axis)
        for at, bit in enumerate(bits):
            high = (me & bit) != 0
            got = [jnp.where(high, got[k ^ (1 << at)], got[k]) for k in range(len(got))]
        held = jnp.concatenate(got, axis=0)
        names = [(axis, bit) for bit in reversed(bits)] + names
    wanted = []
    for axis in ("rec", "tm"):
        wanted += sorted((n for n in names if n[0] == axis), key=lambda n: -n[1])
    order = [names.index(n) for n in wanted]
    dims = held.reshape((2,) * len(names) + block.shape)
    dims = jnp.transpose(dims, order + [len(names), len(names) + 1])
    return dims.reshape((-1,) + block.shape[1:]), rounds


def along_rec(block):
    return [block] + [exchange(block, "rec", d) for d in (1, 2, 3)]


def to_neighbours(held):
    return held, exchange(held, "tm", 2), exchange(held, "tm", 4)


def relayed(held, beside, above):
    half = held.shape[0] // 2
    return exchange(beside[:half], "tm", 4), exchange(above[half:], "tm", 2)


def to_other_core(held, beside, above, low, high):
    pieces = [(held, 0, 0, 4), (beside, 2, 0, 4), (above, 4, 0, 4), (low, 6, 0, 2), (high, 6, 2, 2)]
    pieces += [(exchange(p, "tm", 1), far ^ 1, slot, n) for p, far, slot, n in pieces]
    return [p[0] for p in pieces], [p[1:] for p in pieces]


def copies_in(info_ref, sources, places, target, sem):
    if places is None:
        pltpu.make_async_copy(sources[0], target, sem).start()
        return
    rec, tm, tm_size = info_ref[5], info_ref[6], info_ref[7]
    for source, (far, first, number) in zip(sources, places):
        rows = source.shape[0] // number
        for slot in range(number):
            owner = (rec ^ (first + slot)) * tm_size + (tm ^ far)
            if len(target.shape) == 3:
                place = target.at[owner]
            else:
                place = target.at[pl.ds(pl.multiple_of(owner * rows, 16), rows), :]
            pltpu.make_async_copy(source.at[pl.ds(slot * rows, rows), :], place, sem).start()


BINS = 41


def prepare_kernel(limit, info_ref, quads_ref, lane_ref, w_ref, patches_ref, taps_ref):
    base = info_ref[0]
    lengths = [info_ref[1 + k] for k in range(4)]
    tokens = quads_ref.shape[0]
    wide = quads_ref.shape[1]
    source = lax.broadcasted_iota(jnp.int32, (wide, COLS), 0)
    token = lax.broadcasted_iota(jnp.int32, (tokens, COLS), 0)
    own = segment_of(base + 4 * (token - HALO), lengths, limit)
    frame = lane_ref[6:7, :]
    for a in range(3):
        middle = segment_of(base + 4 * (token - HALO) + 2 * a - 2, lengths, limit)
        there = segment_of(base + 4 * (token - HALO) + 2 * a - 3 + frame, lengths, limit)
        same = (middle == own) & (there == middle)
        for h in range(2):
            chosen = (source == lane_ref[2 * a + h : 2 * a + h + 1, :]).astype(jnp.float32)
            made = jnp.dot(
                quads_ref[...], chosen.astype(jnp.bfloat16), preferred_element_type=jnp.float32
            )
            patches_ref[a, h] = jnp.where(same, made, 0.0).astype(jnp.bfloat16)

    row = lax.broadcasted_iota(jnp.int32, (COLS, CHANNELS), 0)
    group = jnp.zeros((COLS, CHANNELS), jnp.int32)
    for k in range(1, 7):
        group = group + (row >= BINS * k).astype(jnp.int32)
    at_bin = row - BINS * group
    spread = []
    for b in range(3):
        total = jnp.zeros((COLS, CHANNELS), jnp.float32)
        for a in range(3):
            tap = w_ref[3 * a + b : 3 * a + b + 1, :]
            high = tap.astype(jnp.bfloat16).astype(jnp.float32)
            total = jnp.where(group == a, high, total)
            total = jnp.where(group == 3 + a, tap - high, total)
        spread.append(total)
    for f in range(20):
        total = jnp.zeros((COLS, CHANNELS), jnp.float32)
        for b in range(3):
            total = jnp.where(at_bin == 2 * f + b, spread[b], total)
        taps_ref[:, f * CHANNELS : (f + 1) * CHANNELS] = total.astype(jnp.bfloat16)


def prepare(info, mel, w_first, tokens, limit):
    bins = mel.shape[1]
    reach = 4 * (HALO + EDGE)
    tm = lax.axis_size("tm")
    forward = [(i, i + 1) for i in range(tm - 1)]
    backward = [(i + 1, i) for i in range(tm - 1)]
    low = lax.ppermute(mel[mel.shape[0] - reach :], "tm", forward)
    high = lax.ppermute(mel[:reach], "tm", backward)
    quads = jnp.concatenate([low, mel, high], axis=0).reshape(-1, 4 * bins)
    count = tokens + 2 * HALO
    quads = jnp.concatenate(
        [quads[EDGE - 1 : EDGE - 1 + count], quads[EDGE : EDGE + count]], axis=1
    )
    lane = np.arange(COLS)
    frame, at_bin = lane // BINS % 3, lane % BINS
    used = lane < 6 * BINS
    picks = np.full((8, COLS), -1, np.int32)
    for a in range(3):
        for h in range(2):
            wanted = at_bin - 1 + 40 * h
            place = bins * (2 * a + frame + 1) + wanted
            picks[2 * a + h] = np.where(used & (wanted >= 0), place, -1)
    picks[6] = frame
    whole = pl.BlockSpec(memory_space=pltpu.VMEM)
    return pl.pallas_call(
        functools.partial(prepare_kernel, limit),
        out_shape=(
            jax.ShapeDtypeStruct((3, 2, count, COLS), jnp.bfloat16),
            jax.ShapeDtypeStruct((COLS, 20 * CHANNELS), jnp.bfloat16),
        ),
        in_specs=[pl.BlockSpec(memory_space=pltpu.SMEM)] + [whole] * 3,
        out_specs=(whole, whole),
        compiler_params=pltpu.CompilerParams(vmem_limit_bytes=24 * 1024 * 1024),
        cost_estimate=pl.CostEstimate(
            flops=12 * count * 768 * COLS, bytes_accessed=6 * 1024 * 1024, transcendentals=0
        ),
        name="prepare",
    )(info, quads, jnp.asarray(picks), w_first.reshape(9, CHANNELS))


def conv_kernel(begin, count, a_ref, b_ref, w_ref, out_ref, first):
    tokens = out_ref.shape[0]
    rows_step = tokens // 2

    @pl.loop(0, 2)
    def _(r):
        rows = pl.ds(pl.multiple_of(r * rows_step, 16), rows_step)
        for a in range(3):
            for i in range(2 * count + 1):
                at = 2 * begin - 1 + i
                place = slice(i * COLS, (i + 1) * COLS)
                if at < 0:
                    first[a, :, place] = jnp.zeros((rows_step, COLS), jnp.bfloat16)
                    continue
                half, col = divmod(at, 20)
                made = jnp.dot(
                    a_ref[a, half, rows, :],
                    b_ref[:, col * COLS : (col + 1) * COLS],
                    preferred_element_type=jnp.float32,
                )
                first[a, :, place] = jnp.maximum(made, 0.0).astype(jnp.bfloat16)
        for t in range(count):
            total = None
            for a in range(3):
                made = jnp.dot(
                    first[a, :, 2 * t * COLS : (2 * t + 3) * COLS],
                    w_ref[a],
                    preferred_element_type=jnp.float32,
                )
                total = made if total is None else total + made
            out_ref[rows, t * COLS : (t + 1) * COLS] = jnp.maximum(total, 0.0).astype(jnp.bfloat16)


def subsample(patches, taps, w_second):
    tokens = patches.shape[2]
    count = 4
    weights = w_second.reshape(3, 3 * COLS, COLS)
    whole = pl.BlockSpec(memory_space=pltpu.VMEM)
    flops = 2 * tokens * COLS * COLS * (3 * (2 * count + 1) + 9 * count)
    pieces = []
    for begin in range(0, 20, count):
        pieces.append(
            pl.pallas_call(
                functools.partial(conv_kernel, begin, count),
                out_shape=jax.ShapeDtypeStruct((tokens, count * CHANNELS), jnp.bfloat16),
                in_specs=[whole] * 3,
                out_specs=whole,
                scratch_shapes=[
                    pltpu.VMEM((3, tokens // 2, (2 * count + 1) * COLS), jnp.bfloat16)
                ],
                compiler_params=pltpu.CompilerParams(vmem_limit_bytes=20 * 1024 * 1024),
                cost_estimate=pl.CostEstimate(
                    flops=flops, bytes_accessed=8 * 1024 * 1024, transcendentals=0
                ),
                name="subsample",
            )(patches, taps, weights)
        )
    return pieces


def project_kernel(places, info_ref, gain_ref, *rest):
    subs = rest[:5]
    sources = rest[5:-5]
    mid_ref, normed_ref, weights, hidden, sem = rest[-5:]
    copies_in(info_ref, sources, places, weights, sem)
    pltpu.make_async_copy(weights, weights, sem).wait()

    depth = weights.shape[0] // len(subs)

    @pl.loop(0, WIDTH // COLS)
    def _(n):
        here = pl.ds(pl.multiple_of(n * COLS, COLS), COLS)
        total = None
        for piece, sub in enumerate(subs):
            made = jnp.dot(
                sub[...],
                weights[piece * depth : (piece + 1) * depth, here],
                preferred_element_type=jnp.float32,
            )
            total = made if total is None else total + made
        hidden[:, here] = total

    gain = gain_ref[...]
    chunk = 160

    @pl.loop(0, hidden.shape[0] // chunk)
    def _(r):
        rows = pl.ds(pl.multiple_of(r * chunk, chunk), chunk)
        normed_ref[rows, :] = layer_norm(hidden[rows, :], gain).astype(jnp.bfloat16)

    mid_ref[...] = hidden[WINDOW : WINDOW + mid_ref.shape[0], :]


def project(info, gain, subs, sources, places, tokens):
    rows_all = tokens + 2 * HALO
    rows_mid = tokens + 2 * EDGE
    whole = pl.BlockSpec(memory_space=pltpu.VMEM)
    depth = sum(sub.shape[1] for sub in subs)
    return pl.pallas_call(
        functools.partial(project_kernel, places),
        out_shape=(
            jax.ShapeDtypeStruct((rows_mid, WIDTH), jnp.float32),
            jax.ShapeDtypeStruct((rows_all, WIDTH), jnp.bfloat16),
        ),
        in_specs=[pl.BlockSpec(memory_space=pltpu.SMEM)]
        + [whole] * 6
        + [pl.BlockSpec(memory_space=pl.ANY)] * len(sources),
        out_specs=(whole, whole),
        scratch_shapes=[
            pltpu.VMEM((depth, WIDTH), jnp.bfloat16),
            pltpu.VMEM((rows_all, WIDTH), jnp.float32),
            pltpu.SemaphoreType.DMA(()),
        ],
        compiler_params=pltpu.CompilerParams(vmem_limit_bytes=34 * 1024 * 1024),
        cost_estimate=pl.CostEstimate(
            flops=2 * rows_all * depth * WIDTH, bytes_accessed=24 * 1024 * 1024, transcendentals=0
        ),
        name="project",
    )(info, gain, *subs, *sources)


def pack_kernel(pieces, *refs):
    out_ref = refs[-1]
    at = 0
    for source, first in pieces:
        rows = refs[source].shape[0]
        out_ref[at : at + rows, :] = refs[source][:, first : first + WIDTH]
        at += rows


def pack(arrays):
    pieces = [
        (k, first) for k, array in enumerate(arrays) for first in range(0, array.shape[1], WIDTH)
    ]
    if any(array.shape[0] % 16 for array in arrays):
        return jnp.concatenate([arrays[k][:, c : c + WIDTH] for k, c in pieces], axis=0)
    rows = sum(arrays[k].shape[0] for k, _ in pieces)
    whole = pl.BlockSpec(memory_space=pltpu.VMEM)
    return pl.pallas_call(
        functools.partial(pack_kernel, pieces),
        out_shape=jax.ShapeDtypeStruct((rows, WIDTH), jnp.bfloat16),
        in_specs=[whole] * len(arrays),
        out_specs=whole,
        compiler_params=pltpu.CompilerParams(vmem_limit_bytes=4 * 1024 * 1024),
        cost_estimate=pl.CostEstimate(
            flops=0, bytes_accessed=4 * rows * WIDTH, transcendentals=0
        ),
        name="pack",
    )(*arrays)


def columns(weights, part, parts, n):
    rows = weights.shape[1] // parts
    here = pl.ds(pl.multiple_of(n * COLS, COLS), COLS)
    return weights[:, part * rows : (part + 1) * rows, here].reshape(-1, COLS)


def block_kernel(
    tokens,
    limit,
    info_ref,
    hidden_ref,
    normed_ref,
    gain_conv_ref,
    depth_ref,
    gain_out_ref,
    *rest,
):
    late, out_ref, early_w, late_w, keys, values, queries, context, attended, gated, masks = rest[
        :11
    ]
    biases, sems = rest[11:]
    rows_mid = tokens + 2 * EDGE
    mid = slice(WINDOW, WINDOW + rows_mid)
    early_rows, late_rows = early_w.shape[1], late_w.shape[1]
    early_copy = pltpu.make_async_copy(late.at[:, pl.ds(0, early_rows), :], early_w, sems.at[0])
    late_copy = pltpu.make_async_copy(
        late.at[:, pl.ds(early_rows, late_rows), :], late_w, sems.at[1]
    )
    early_copy.start()
    late_copy.start()
    base = info_ref[0]
    lengths = [info_ref[1 + k] for k in range(4)]

    def here(n):
        return pl.ds(pl.multiple_of(n * COLS, COLS), COLS)

    blocks = []
    at_row = 0
    while at_row < rows_mid:
        size = 128 + (EDGE if at_row == 0 or at_row + 128 + EDGE == rows_mid else 0)
        blocks.append((at_row, size))
        at_row += size

    row = lax.broadcasted_iota(jnp.int32, (tokens, HEAD_DIM), 0)
    own = segment_of(base + 4 * row, lengths, limit)
    for k in range(KERNEL):
        there = segment_of(base + 4 * (row + k - KERNEL // 2), lengths, limit)
        masks[k] = (there == own).astype(jnp.float32)
    for at, (start, size) in enumerate(blocks):
        span = size + 2 * WINDOW
        q_row = lax.broadcasted_iota(jnp.int32, (size, 1), 0)
        k_row = lax.broadcasted_iota(jnp.int32, (1, span), 1)
        q_seg = segment_of(base + 4 * (q_row + start - EDGE), lengths, limit)
        k_seg = segment_of(base + 4 * (k_row + start - HALO), lengths, limit)
        apart = k_row - q_row
        allowed = (apart >= 0) & (apart <= 2 * WINDOW) & (q_seg == k_seg)
        biases[at, 0:size, 0:span] = jnp.where(allowed, 0.0, -1e30)
    for head in range(HEADS):
        values[:, (2 * head + 1) * HEAD_DIM : (2 * head + 2) * HEAD_DIM] = jnp.ones(
            (values.shape[0], HEAD_DIM), jnp.bfloat16
        )

    early_copy.wait()

    @pl.loop(0, WIDTH // COLS)
    def _(n):
        queries[:, here(n)] = jnp.dot(
            normed_ref[mid, :], columns(early_w, 0, 3, n), preferred_element_type=jnp.float32
        ).astype(jnp.bfloat16)
        keys[:, here(n)] = jnp.dot(
            normed_ref[...], columns(early_w, 1, 3, n), preferred_element_type=jnp.float32
        ).astype(jnp.bfloat16)
        made = jnp.dot(
            normed_ref[...], columns(early_w, 2, 3, n), preferred_element_type=jnp.float32
        ).astype(jnp.bfloat16)
        for k in range(COLS // HEAD_DIM):
            lanes = pl.ds(pl.multiple_of(2 * n * COLS + 2 * k * HEAD_DIM, HEAD_DIM), HEAD_DIM)
            values[:, lanes] = made[:, k * HEAD_DIM : (k + 1) * HEAD_DIM]

    scale = HEAD_DIM**-0.5 * 1.4426950408889634

    @pl.loop(0, HEADS)
    def _(head):
        lanes = pl.ds(pl.multiple_of(head * HEAD_DIM, HEAD_DIM), HEAD_DIM)
        wide = pl.ds(pl.multiple_of(head * 2 * HEAD_DIM, 2 * HEAD_DIM), 2 * HEAD_DIM)
        for at, (start, size) in enumerate(blocks):
            span = size + 2 * WINDOW
            scores = lax.dot_general(
                queries[start : start + size, lanes],
                keys[start : start + span, lanes],
                (((1,), (1,)), ((), ())),
                preferred_element_type=jnp.float32,
            )
            scores = scores * scale + biases[at, 0:size, 0:span]
            exped = jnp.exp2(scores - jnp.max(scores, axis=-1, keepdims=True))
            mixed = jnp.dot(
                exped.astype(jnp.bfloat16),
                values[start : start + span, wide],
                preferred_element_type=jnp.float32,
            )
            context[start : start + size, lanes] = (
                mixed[:, :HEAD_DIM] / mixed[:, HEAD_DIM:]
            ).astype(jnp.bfloat16)

    late_copy.wait()

    @pl.loop(0, WIDTH // COLS)
    def _(n):
        attended[:, here(n)] = hidden_ref[:, here(n)] + jnp.dot(
            context[...], columns(late_w, 0, 4, n), preferred_element_type=jnp.float32
        )

    gain_c = gain_conv_ref[...]
    step_rows = rows_mid // 2

    @pl.loop(0, 2)
    def _(r):
        rows = pl.ds(pl.multiple_of(r * step_rows, 16), step_rows)
        queries[rows, :] = layer_norm(attended[rows, :], gain_c).astype(jnp.bfloat16)


    @pl.loop(0, WIDTH // COLS)
    def _(n):
        value = jnp.dot(queries[...], columns(late_w, 1, 4, n), preferred_element_type=jnp.float32)
        gate = jnp.dot(queries[...], columns(late_w, 2, 4, n), preferred_element_type=jnp.float32)
        made = (value * jax.nn.sigmoid(gate)).astype(jnp.bfloat16).astype(jnp.float32)
        for j in range(COLS // HEAD_DIM):
            gated[...] = made[:, j * HEAD_DIM : (j + 1) * HEAD_DIM]
            lanes = pl.ds(pl.multiple_of(n * COLS + j * HEAD_DIM, HEAD_DIM), HEAD_DIM)
            total = jnp.zeros((tokens, HEAD_DIM), jnp.float32)
            for k in range(KERNEL):
                begin = EDGE - KERNEL // 2 + k
                tap = gated[begin : begin + tokens, :] * depth_ref[k : k + 1, lanes]
                total = total + (tap if k == KERNEL // 2 else tap * masks[k])
            context[0:tokens, lanes] = (total * jax.nn.sigmoid(total)).astype(jnp.bfloat16)

    @pl.loop(0, WIDTH // COLS)
    def _(n):
        attended[EDGE : EDGE + tokens, here(n)] += jnp.dot(
            context[0:tokens, :], columns(late_w, 3, 4, n), preferred_element_type=jnp.float32
        )

    gain_o = gain_out_ref[...]

    @pl.loop(0, tokens // 128)
    def _(r):
        rows = pl.ds(pl.multiple_of(r * 128, 128), 128)
        taken = attended[pl.ds(pl.multiple_of(EDGE + r * 128, 16), 128), :]
        out_ref[rows, :] = layer_norm(taken, gain_o).astype(jnp.bfloat16)


def conformer_block(info, hidden, normed, late, gain_conv, w_depth, gain_out, limit):
    rows_all = normed.shape[0]
    rows_mid = hidden.shape[0]
    tokens = rows_mid - 2 * EDGE
    whole = pl.BlockSpec(memory_space=pltpu.VMEM)
    flops = 2 * rows_all * WIDTH * 2 * WIDTH + 2 * rows_mid * WIDTH * WIDTH * 5
    return pl.pallas_call(
        functools.partial(block_kernel, tokens, limit),
        out_shape=jax.ShapeDtypeStruct((tokens, WIDTH), jnp.bfloat16),
        in_specs=[pl.BlockSpec(memory_space=pltpu.SMEM)]
        + [whole] * 5
        + [pl.BlockSpec(memory_space=pl.ANY)],
        out_specs=whole,
        scratch_shapes=[
            pltpu.VMEM((32, 3 * WIDTH // 32, WIDTH), jnp.bfloat16),
            pltpu.VMEM((32, 4 * WIDTH // 32, WIDTH), jnp.bfloat16),
            pltpu.VMEM((rows_all, WIDTH), jnp.bfloat16),
            pltpu.VMEM((rows_all, 2 * WIDTH), jnp.bfloat16),
            pltpu.VMEM((rows_mid, WIDTH), jnp.bfloat16),
            pltpu.VMEM((rows_mid, WIDTH), jnp.bfloat16),
            pltpu.VMEM((rows_mid, WIDTH), jnp.float32),
            pltpu.VMEM((rows_mid, HEAD_DIM), jnp.float32),
            pltpu.VMEM((KERNEL, tokens, HEAD_DIM), jnp.float32),
            pltpu.VMEM((4, 128 + EDGE, 512), jnp.float32),
            pltpu.SemaphoreType.DMA((2,)),
        ],
        compiler_params=pltpu.CompilerParams(vmem_limit_bytes=44 * 1024 * 1024),
        cost_estimate=pl.CostEstimate(
            flops=flops, bytes_accessed=24 * 1024 * 1024, transcendentals=4 * 1024 * 1024
        ),
        name="conformer_block",
    )(info, hidden, normed, gain_conv, w_depth, gain_out, late)


def on_device(
    mel_frames,
    lengths,
    w_first,
    w_second,
    w_proj,
    gain_attn,
    w_qkv,
    w_out,
    gain_conv,
    w_point_in,
    w_depth,
    w_point_out,
    gain_out,
):
    tokens = mel_frames.shape[1] // 4
    limit = mel_frames.shape[1] * lax.axis_size("tm")
    base = lax.axis_index("tm") * mel_frames.shape[1]
    info = jnp.concatenate(
        [
            jnp.reshape(base, (1,)),
            lengths[0],
            jnp.stack([lax.axis_index("rec"), lax.axis_index("tm")]),
            jnp.full((1,), lax.axis_size("tm"), jnp.int32),
        ]
    ).astype(jnp.int32)

    def gather_packed(arrays):
        packed = pack(arrays)
        full = lax.all_gather(packed, ("rec", "tm"), axis=0, tiled=False)
        if full.shape[0] == 32:
            return full
        parts = packed.shape[0] // w_out.shape[0]
        full = full.reshape(full.shape[0], parts, -1, WIDTH).transpose(1, 0, 2, 3)
        full = full.reshape(parts, 32, -1, WIDTH).transpose(1, 0, 2, 3)
        return full.reshape(32, -1, WIDTH)

    late = gather_packed([w_qkv, w_out, w_point_in, w_point_out])
    w_second_all, rounds = gather_ordered(w_second)
    patches, taps = prepare(info, mel_frames[0], w_first, tokens, limit)
    subs = subsample(patches, taps, w_second_all)
    if lax.axis_size("rec") == 4 and lax.axis_size("tm") == 8:
        proj = along_rec(behind(w_proj, *rounds[0]))
        proj = behind(tuple(proj), patches, *rounds[1], *subs[:2])
        proj = to_neighbours(jnp.concatenate(proj, axis=0))
        proj_late = relayed(*behind(proj, *subs))
        proj, places = to_other_core(*proj, *proj_late)
    else:
        proj, places = [lax.all_gather(w_proj, ("rec", "tm"), axis=0, tiled=True)], None
    hidden, normed = project(info, gain_attn[None], subs, proj, places, tokens)
    encoded = conformer_block(
        info,
        hidden,
        normed,
        late,
        gain_conv[None],
        w_depth,
        gain_out[None],
        limit,
    )
    return encoded[None]


def solution(mesh):
    placed = (
        P("rec", "tm", None),
        P("rec", None),
        P(),
        P(("rec", "tm"), None),
        P(("rec", "tm"), None),
        P(),
        P(("rec", "tm"), None),
        P(("rec", "tm"), None),
        P(),
        P(("rec", "tm"), None),
        P(),
        P(("rec", "tm"), None),
        P(),
    )
    return jax.shard_map(
        on_device, mesh=mesh, in_specs=placed, out_specs=P("rec", "tm", None), check_vma=False
    )
```

```python
import functools

import jax
import jax.numpy as jnp
import numpy as np
from jax import lax
from jax.experimental import pallas as pl
from jax.experimental.pallas import tpu as pltpu
from jax.sharding import PartitionSpec as P

WIDTH = 1024
HEADS = 8
HEAD_DIM = 128
KERNEL = 9
WINDOW = 128
CHANNELS = 256
NORM_EPSILON = 1e-05

EDGE = 16
HALO = WINDOW + EDGE
COLS = 256


def segment_of(positions, lengths, limit):
    counted = jnp.zeros(positions.shape, jnp.int32)
    bound = 0
    for k in range(len(lengths) - 1):
        bound = bound + lengths[k]
        counted = counted + (positions >= bound).astype(jnp.int32)
    return jnp.where((positions >= 0) & (positions < limit), counted, -1)


def layer_norm(values, gain):
    row_mean = jnp.mean(values, axis=-1, keepdims=True)
    centred = values - row_mean
    variance = jnp.mean(centred * centred, axis=-1, keepdims=True)
    return centred * lax.rsqrt(variance + NORM_EPSILON) * gain


def exchange(block, axis, distance):
    size = lax.axis_size(axis)
    return lax.ppermute(block, axis, [(i, i ^ distance) for i in range(size)])


def bit_groups():
    groups = []
    for axis, lowest in (("rec", 1), ("tm", 2)):
        bits = []
        bit = lowest
        while bit < lax.axis_size(axis):
            bits.append(bit)
            bit *= 2
        groups += [(axis, bits[k : k + 2]) for k in range(0, len(bits), 2)]
    return groups + [("tm", [1])]


def distances(bits):
    return [0] + [bits[0]] if len(bits) == 1 else [0, bits[0], bits[1], bits[0] + bits[1]]


def can_exchange():
    return all(
        lax.axis_size(axis) & (lax.axis_size(axis) - 1) == 0 and lax.axis_size(axis) > 1
        for axis in ("rec", "tm")
    )


def behind(value, *others):
    return lax.optimization_barrier((value, *others))[0]


def gather_ordered(block):
    if not can_exchange():
        return lax.all_gather(block, ("rec", "tm"), axis=0, tiled=True), []
    names = []
    held = block[None]
    rounds = []
    for axis, bits in bit_groups():
        got = [held] + [exchange(held, axis, d) for d in distances(bits)[1:]]
        rounds.append(got[1:])
        me = lax.axis_index(axis)
        for at, bit in enumerate(bits):
            high = (me & bit) != 0
            got = [jnp.where(high, got[k ^ (1 << at)], got[k]) for k in range(len(got))]
        held = jnp.concatenate(got, axis=0)
        names = [(axis, bit) for bit in reversed(bits)] + names
    wanted = []
    for axis in ("rec", "tm"):
        wanted += sorted((n for n in names if n[0] == axis), key=lambda n: -n[1])
    order = [names.index(n) for n in wanted]
    dims = held.reshape((2,) * len(names) + block.shape)
    dims = jnp.transpose(dims, order + [len(names), len(names) + 1])
    return dims.reshape((-1,) + block.shape[1:]), rounds


def along_rec(block):
    return [block] + [exchange(block, "rec", d) for d in (1, 2, 3)]


def to_neighbours(held):
    return held, exchange(held, "tm", 2), exchange(held, "tm", 4)


def relayed(held, beside, above):
    half = held.shape[0] // 2
    return exchange(beside[:half], "tm", 4), exchange(above[half:], "tm", 2)


def to_other_core(held, beside, above, low, high):
    pieces = [(held, 0, 0, 4), (beside, 2, 0, 4), (above, 4, 0, 4), (low, 6, 0, 2), (high, 6, 2, 2)]
    pieces += [(exchange(p, "tm", 1), far ^ 1, slot, n) for p, far, slot, n in pieces]
    return [p[0] for p in pieces], [p[1:] for p in pieces]


def copies_in(info_ref, sources, places, target, sem):
    if places is None:
        pltpu.make_async_copy(sources[0], target, sem).start()
        return
    rec, tm, tm_size = info_ref[5], info_ref[6], info_ref[7]
    for source, (far, first, number) in zip(sources, places):
        rows = source.shape[0] // number
        for slot in range(number):
            owner = (rec ^ (first + slot)) * tm_size + (tm ^ far)
            if len(target.shape) == 3:
                place = target.at[owner]
            else:
                place = target.at[pl.ds(pl.multiple_of(owner * rows, 16), rows), :]
            pltpu.make_async_copy(source.at[pl.ds(slot * rows, rows), :], place, sem).start()


BINS = 41


def prepare_kernel(limit, info_ref, quads_ref, lane_ref, w_ref, patches_ref, taps_ref):
    base = info_ref[0]
    lengths = [info_ref[1 + k] for k in range(4)]
    tokens = quads_ref.shape[0]
    wide = quads_ref.shape[1]
    source = lax.broadcasted_iota(jnp.int32, (wide, COLS), 0)
    token = lax.broadcasted_iota(jnp.int32, (tokens, COLS), 0)
    own = segment_of(base + 4 * (token - HALO), lengths, limit)
    frame = lane_ref[6:7, :]
    for a in range(3):
        middle = segment_of(base + 4 * (token - HALO) + 2 * a - 2, lengths, limit)
        there = segment_of(base + 4 * (token - HALO) + 2 * a - 3 + frame, lengths, limit)
        same = (middle == own) & (there == middle)
        for h in range(2):
            chosen = (source == lane_ref[2 * a + h : 2 * a + h + 1, :]).astype(jnp.float32)
            made = jnp.dot(
                quads_ref[...], chosen.astype(jnp.bfloat16), preferred_element_type=jnp.float32
            )
            patches_ref[a, h] = jnp.where(same, made, 0.0).astype(jnp.bfloat16)

    row = lax.broadcasted_iota(jnp.int32, (COLS, CHANNELS), 0)
    group = jnp.zeros((COLS, CHANNELS), jnp.int32)
    for k in range(1, 7):
        group = group + (row >= BINS * k).astype(jnp.int32)
    at_bin = row - BINS * group
    spread = []
    for b in range(3):
        total = jnp.zeros((COLS, CHANNELS), jnp.float32)
        for a in range(3):
            tap = w_ref[3 * a + b : 3 * a + b + 1, :]
            high = tap.astype(jnp.bfloat16).astype(jnp.float32)
            total = jnp.where(group == a, high, total)
            total = jnp.where(group == 3 + a, tap - high, total)
        spread.append(total)
    for f in range(20):
        total = jnp.zeros((COLS, CHANNELS), jnp.float32)
        for b in range(3):
            total = jnp.where(at_bin == 2 * f + b, spread[b], total)
        taps_ref[:, f * CHANNELS : (f + 1) * CHANNELS] = total.astype(jnp.bfloat16)


def prepare(info, mel, w_first, tokens, limit):
    bins = mel.shape[1]
    reach = 4 * (HALO + EDGE)
    tm = lax.axis_size("tm")
    forward = [(i, i + 1) for i in range(tm - 1)]
    backward = [(i + 1, i) for i in range(tm - 1)]
    low = lax.ppermute(mel[mel.shape[0] - reach :], "tm", forward)
    high = lax.ppermute(mel[:reach], "tm", backward)
    quads = jnp.concatenate([low, mel, high], axis=0).reshape(-1, 4 * bins)
    count = tokens + 2 * HALO
    quads = jnp.concatenate(
        [quads[EDGE - 1 : EDGE - 1 + count], quads[EDGE : EDGE + count]], axis=1
    )
    lane = np.arange(COLS)
    frame, at_bin = lane // BINS % 3, lane % BINS
    used = lane < 6 * BINS
    picks = np.full((8, COLS), -1, np.int32)
    for a in range(3):
        for h in range(2):
            wanted = at_bin - 1 + 40 * h
            place = bins * (2 * a + frame + 1) + wanted
            picks[2 * a + h] = np.where(used & (wanted >= 0), place, -1)
    picks[6] = frame
    whole = pl.BlockSpec(memory_space=pltpu.VMEM)
    return pl.pallas_call(
        functools.partial(prepare_kernel, limit),
        out_shape=(
            jax.ShapeDtypeStruct((3, 2, count, COLS), jnp.bfloat16),
            jax.ShapeDtypeStruct((COLS, 20 * CHANNELS), jnp.bfloat16),
        ),
        in_specs=[pl.BlockSpec(memory_space=pltpu.SMEM)] + [whole] * 3,
        out_specs=(whole, whole),
        compiler_params=pltpu.CompilerParams(vmem_limit_bytes=24 * 1024 * 1024),
        cost_estimate=pl.CostEstimate(
            flops=12 * count * 768 * COLS, bytes_accessed=6 * 1024 * 1024, transcendentals=0
        ),
        name="prepare",
    )(info, quads, jnp.asarray(picks), w_first.reshape(9, CHANNELS))


def conv_kernel(begin, count, a_ref, b_ref, w_ref, out_ref, first):
    tokens = out_ref.shape[0]
    rows_step = tokens // 2

    @pl.loop(0, 2)
    def _(r):
        rows = pl.ds(pl.multiple_of(r * rows_step, 16), rows_step)
        for a in range(3):
            for i in range(2 * count + 1):
                at = 2 * begin - 1 + i
                place = slice(i * COLS, (i + 1) * COLS)
                if at < 0:
                    first[a, :, place] = jnp.zeros((rows_step, COLS), jnp.bfloat16)
                    continue
                half, col = divmod(at, 20)
                made = jnp.dot(
                    a_ref[a, half, rows, :],
                    b_ref[:, col * COLS : (col + 1) * COLS],
                    preferred_element_type=jnp.float32,
                )
                first[a, :, place] = jnp.maximum(made, 0.0).astype(jnp.bfloat16)
        for t in range(count):
            total = None
            for a in range(3):
                made = jnp.dot(
                    first[a, :, 2 * t * COLS : (2 * t + 3) * COLS],
                    w_ref[a],
                    preferred_element_type=jnp.float32,
                )
                total = made if total is None else total + made
            out_ref[rows, t * COLS : (t + 1) * COLS] = jnp.maximum(total, 0.0).astype(jnp.bfloat16)


def subsample(patches, taps, w_second):
    tokens = patches.shape[2]
    count = 4
    weights = w_second.reshape(3, 3 * COLS, COLS)
    whole = pl.BlockSpec(memory_space=pltpu.VMEM)
    flops = 2 * tokens * COLS * COLS * (3 * (2 * count + 1) + 9 * count)
    pieces = []
    for begin in range(0, 20, count):
        pieces.append(
            pl.pallas_call(
                functools.partial(conv_kernel, begin, count),
                out_shape=jax.ShapeDtypeStruct((tokens, count * CHANNELS), jnp.bfloat16),
                in_specs=[whole] * 3,
                out_specs=whole,
                scratch_shapes=[
                    pltpu.VMEM((3, tokens // 2, (2 * count + 1) * COLS), jnp.bfloat16)
                ],
                compiler_params=pltpu.CompilerParams(vmem_limit_bytes=20 * 1024 * 1024),
                cost_estimate=pl.CostEstimate(
                    flops=flops, bytes_accessed=8 * 1024 * 1024, transcendentals=0
                ),
                name="subsample",
            )(patches, taps, weights)
        )
    return pieces


def project_kernel(places, info_ref, gain_ref, *rest):
    subs = rest[:5]
    sources = rest[5:-5]
    mid_ref, normed_ref, weights, hidden, sem = rest[-5:]
    copies_in(info_ref, sources, places, weights, sem)
    pltpu.make_async_copy(weights, weights, sem).wait()

    depth = weights.shape[0] // len(subs)

    @pl.loop(0, WIDTH // COLS)
    def _(n):
        here = pl.ds(pl.multiple_of(n * COLS, COLS), COLS)
        total = None
        for piece, sub in enumerate(subs):
            made = jnp.dot(
                sub[...],
                weights[piece * depth : (piece + 1) * depth, here],
                preferred_element_type=jnp.float32,
            )
            total = made if total is None else total + made
        hidden[:, here] = total

    gain = gain_ref[...]
    chunk = 160

    @pl.loop(0, hidden.shape[0] // chunk)
    def _(r):
        rows = pl.ds(pl.multiple_of(r * chunk, chunk), chunk)
        normed_ref[rows, :] = layer_norm(hidden[rows, :], gain).astype(jnp.bfloat16)

    mid_ref[...] = hidden[WINDOW : WINDOW + mid_ref.shape[0], :]


def project(info, gain, subs, sources, places, tokens):
    rows_all = tokens + 2 * HALO
    rows_mid = tokens + 2 * EDGE
    whole = pl.BlockSpec(memory_space=pltpu.VMEM)
    depth = sum(sub.shape[1] for sub in subs)
    return pl.pallas_call(
        functools.partial(project_kernel, places),
        out_shape=(
            jax.ShapeDtypeStruct((rows_mid, WIDTH), jnp.float32),
            jax.ShapeDtypeStruct((rows_all, WIDTH), jnp.bfloat16),
        ),
        in_specs=[pl.BlockSpec(memory_space=pltpu.SMEM)]
        + [whole] * 6
        + [pl.BlockSpec(memory_space=pl.ANY)] * len(sources),
        out_specs=(whole, whole),
        scratch_shapes=[
            pltpu.VMEM((depth, WIDTH), jnp.bfloat16),
            pltpu.VMEM((rows_all, WIDTH), jnp.float32),
            pltpu.SemaphoreType.DMA(()),
        ],
        compiler_params=pltpu.CompilerParams(vmem_limit_bytes=34 * 1024 * 1024),
        cost_estimate=pl.CostEstimate(
            flops=2 * rows_all * depth * WIDTH, bytes_accessed=24 * 1024 * 1024, transcendentals=0
        ),
        name="project",
    )(info, gain, *subs, *sources)


def pack_kernel(pieces, *refs):
    *sources, out_ref, held, sems = refs
    at = 0
    copies = []
    for source, first in pieces:
        rows = sources[source].shape[0]
        copies.append(
            pltpu.make_async_copy(
                sources[source].at[:, pl.ds(first, WIDTH)],
                held.at[pl.ds(at, rows), :],
                sems.at[len(copies)],
            )
        )
        at += rows
    for copy in copies:
        copy.start()
    for copy in copies:
        copy.wait()
    out = pltpu.make_async_copy(held, out_ref, sems.at[len(copies)])
    out.start()
    out.wait()


def pack(arrays):
    pieces = [
        (k, first) for k, array in enumerate(arrays) for first in range(0, array.shape[1], WIDTH)
    ]
    if any(array.shape[0] % 16 for array in arrays):
        return jnp.concatenate([arrays[k][:, c : c + WIDTH] for k, c in pieces], axis=0)
    rows = sum(arrays[k].shape[0] for k, _ in pieces)
    far = pl.BlockSpec(memory_space=pltpu.HBM)
    return pl.pallas_call(
        functools.partial(pack_kernel, pieces),
        out_shape=jax.ShapeDtypeStruct((rows, WIDTH), jnp.bfloat16),
        in_specs=[far] * len(arrays),
        out_specs=far,
        scratch_shapes=[
            pltpu.VMEM((rows, WIDTH), jnp.bfloat16),
            pltpu.SemaphoreType.DMA((len(pieces) + 1,)),
        ],
        compiler_params=pltpu.CompilerParams(vmem_limit_bytes=60 * 1024 * 1024),
        cost_estimate=pl.CostEstimate(
            flops=0, bytes_accessed=4 * rows * WIDTH, transcendentals=0
        ),
        name="pack",
    )(*arrays)


def columns(weights, part, parts, n):
    rows = weights.shape[1] // parts
    return weights[:, part * rows : (part + 1) * rows, n * COLS : (n + 1) * COLS].reshape(-1, COLS)


def block_kernel(
    tokens,
    limit,
    info_ref,
    normed_ref,
    gain_conv_ref,
    depth_ref,
    gain_out_ref,
    hidden_ref,
    weights_ref,
    out_ref,
    early_w,
    late_w,
    keys,
    values,
    queries,
    context,
    attended,
    gated,
    masks,
    biases,
    sems,
):
    rows_mid = tokens + 2 * EDGE
    share = early_w.shape[1] // 3
    early_copies = []
    for k in range(3):
        part = pl.ds(k * share, share)
        early_copies.append(
            pltpu.make_async_copy(
                weights_ref.at[:, part, :], early_w.at[:, part, :], sems.at[k]
            )
        )
    late_copies = []
    for k in range(4):
        late_copies.append(
            pltpu.make_async_copy(
                weights_ref.at[:, pl.ds((3 + k) * share, share), :],
                late_w.at[:, pl.ds(k * share, share), :],
                sems.at[3 + k],
            )
        )
    hidden_copy = pltpu.make_async_copy(hidden_ref, attended, sems.at[7])
    for copy in early_copies:
        copy.start()
    base = info_ref[0]
    lengths = [info_ref[1 + k] for k in range(4)]

    blocks = []
    at_row = 0
    while at_row < rows_mid:
        size = 128 + (EDGE if at_row == 0 or at_row + 128 + EDGE == rows_mid else 0)
        blocks.append((at_row, size))
        at_row += size

    for at, (start, size) in enumerate(blocks):
        span = size + 2 * WINDOW
        q_row = lax.broadcasted_iota(jnp.int32, (size, 1), 0)
        k_row = lax.broadcasted_iota(jnp.int32, (1, span), 1)
        q_seg = segment_of(base + 4 * (q_row + start - EDGE), lengths, limit)
        k_seg = segment_of(base + 4 * (k_row + start - HALO), lengths, limit)
        apart = k_row - q_row
        allowed = (apart >= 0) & (apart <= 2 * WINDOW) & (q_seg == k_seg)
        biases[at, 0:size, 0:span] = jnp.where(allowed, 0.0, -1e30)
    for head in range(HEADS):
        values[:, (2 * head + 1) * HEAD_DIM : (2 * head + 2) * HEAD_DIM] = jnp.ones(
            (values.shape[0], HEAD_DIM), jnp.bfloat16
        )

    early_copies[0].wait()
    hidden_copy.start()
    for copy in late_copies:
        copy.start()
    for n in range(WIDTH // COLS):
        queries[:, n * COLS : (n + 1) * COLS] = jnp.dot(
            normed_ref[WINDOW : WINDOW + rows_mid, :],
            columns(early_w, 0, 3, n),
            preferred_element_type=jnp.float32,
        ).astype(jnp.bfloat16)
    row = lax.broadcasted_iota(jnp.int32, (tokens, HEAD_DIM), 0)
    own = segment_of(base + 4 * row, lengths, limit)
    for k in range(KERNEL):
        there = segment_of(base + 4 * (row + k - KERNEL // 2), lengths, limit)
        masks[k] = (there == own).astype(jnp.float32)
    early_copies[1].wait()
    for n in range(WIDTH // COLS):
        keys[:, n * COLS : (n + 1) * COLS] = jnp.dot(
            normed_ref[...], columns(early_w, 1, 3, n), preferred_element_type=jnp.float32
        ).astype(jnp.bfloat16)
    early_copies[2].wait()
    for n in range(WIDTH // COLS):
        made = jnp.dot(
            normed_ref[...], columns(early_w, 2, 3, n), preferred_element_type=jnp.float32
        ).astype(jnp.bfloat16)
        for k in range(COLS // HEAD_DIM):
            first = 2 * n * COLS + 2 * k * HEAD_DIM
            values[:, first : first + HEAD_DIM] = made[:, k * HEAD_DIM : (k + 1) * HEAD_DIM]

    scale = HEAD_DIM**-0.5 * 1.4426950408889634

    @pl.loop(0, HEADS // 2)
    def _(pair):
        for at, (start, size) in enumerate(blocks):
            span = size + 2 * WINDOW
            for side in range(2):
                head = 2 * pair + side
                lanes = pl.ds(pl.multiple_of(head * HEAD_DIM, HEAD_DIM), HEAD_DIM)
                wide = pl.ds(pl.multiple_of(head * 2 * HEAD_DIM, 2 * HEAD_DIM), 2 * HEAD_DIM)
                scores = lax.dot_general(
                    queries[start : start + size, lanes],
                    keys[start : start + span, lanes],
                    (((1,), (1,)), ((), ())),
                    preferred_element_type=jnp.float32,
                )
                scores = scores * scale + biases[at, 0:size, 0:span]
                exped = jnp.exp2(scores - jnp.max(scores, axis=-1, keepdims=True))
                mixed = jnp.dot(
                    exped.astype(jnp.bfloat16),
                    values[start : start + span, wide],
                    preferred_element_type=jnp.float32,
                )
                context[start : start + size, lanes] = (
                    mixed[:, :HEAD_DIM] / mixed[:, HEAD_DIM:]
                ).astype(jnp.bfloat16)

    hidden_copy.wait()
    late_copies[0].wait()
    gain_c = gain_conv_ref[...]
    half = rows_mid // 2
    for r in range(2):
        rows = slice(r * half, (r + 1) * half)
        for n in range(WIDTH // COLS):
            attended[rows, n * COLS : (n + 1) * COLS] += jnp.dot(
                context[rows, :], columns(late_w, 0, 4, n), preferred_element_type=jnp.float32
            )
        queries[rows, :] = layer_norm(attended[rows, :], gain_c).astype(jnp.bfloat16)

    late_copies[1].wait()
    late_copies[2].wait()
    for n in range(WIDTH // COLS):
        value = jnp.dot(queries[...], columns(late_w, 1, 4, n), preferred_element_type=jnp.float32)
        gate = jnp.dot(queries[...], columns(late_w, 2, 4, n), preferred_element_type=jnp.float32)
        made = (value * jax.nn.sigmoid(gate)).astype(jnp.bfloat16).astype(jnp.float32)
        for j in range(COLS // HEAD_DIM):
            at = n * (COLS // HEAD_DIM) + j
            gated[at] = made[:, j * HEAD_DIM : (j + 1) * HEAD_DIM]
            lanes = slice(at * HEAD_DIM, (at + 1) * HEAD_DIM)
            total = jnp.zeros((tokens, HEAD_DIM), jnp.float32)
            for k in range(KERNEL):
                begin = EDGE - KERNEL // 2 + k
                tap = gated[at, begin : begin + tokens, :] * depth_ref[k : k + 1, lanes]
                total = total + (tap if k == KERNEL // 2 else tap * masks[k])
            context[0:tokens, lanes] = (total * jax.nn.sigmoid(total)).astype(jnp.bfloat16)

    late_copies[3].wait()
    gain_o = gain_out_ref[...]
    half = tokens // 2
    for r in range(2):
        rows = slice(r * half, (r + 1) * half)
        mid = slice(EDGE + r * half, EDGE + (r + 1) * half)
        for n in range(WIDTH // COLS):
            attended[mid, n * COLS : (n + 1) * COLS] += jnp.dot(
                context[rows, :], columns(late_w, 3, 4, n), preferred_element_type=jnp.float32
            )
        out_ref[rows, :] = layer_norm(attended[mid, :], gain_o).astype(jnp.bfloat16)


def conformer_block(info, hidden, normed, weights, gain_conv, w_depth, gain_out, limit):
    rows_all = normed.shape[0]
    rows_mid = hidden.shape[0]
    tokens = rows_mid - 2 * EDGE
    whole = pl.BlockSpec(memory_space=pltpu.VMEM)
    far = pl.BlockSpec(memory_space=pltpu.HBM)
    flops = 2 * rows_all * WIDTH * 2 * WIDTH + 2 * rows_mid * WIDTH * WIDTH * 5
    return pl.pallas_call(
        functools.partial(block_kernel, tokens, limit),
        out_shape=jax.ShapeDtypeStruct((tokens, WIDTH), jnp.bfloat16),
        in_specs=[pl.BlockSpec(memory_space=pltpu.SMEM)] + [whole] * 4 + [far] * 2,
        out_specs=whole,
        scratch_shapes=[
            pltpu.VMEM((32, 3 * WIDTH // 32, WIDTH), jnp.bfloat16),
            pltpu.VMEM((32, 4 * WIDTH // 32, WIDTH), jnp.bfloat16),
            pltpu.VMEM((rows_all, WIDTH), jnp.bfloat16),
            pltpu.VMEM((rows_all, 2 * WIDTH), jnp.bfloat16),
            pltpu.VMEM((rows_mid, WIDTH), jnp.bfloat16),
            pltpu.VMEM((rows_mid, WIDTH), jnp.bfloat16),
            pltpu.VMEM((rows_mid, WIDTH), jnp.float32),
            pltpu.VMEM((WIDTH // HEAD_DIM, rows_mid, HEAD_DIM), jnp.float32),
            pltpu.VMEM((KERNEL, tokens, HEAD_DIM), jnp.float32),
            pltpu.VMEM((4, 128 + EDGE, 512), jnp.float32),
            pltpu.SemaphoreType.DMA((8,)),
        ],
        compiler_params=pltpu.CompilerParams(vmem_limit_bytes=60 * 1024 * 1024),
        cost_estimate=pl.CostEstimate(
            flops=flops, bytes_accessed=24 * 1024 * 1024, transcendentals=4 * 1024 * 1024
        ),
        name="conformer_block",
    )(info, normed, gain_conv, w_depth, gain_out, hidden, weights)


def on_device(
    mel_frames,
    lengths,
    w_first,
    w_second,
    w_proj,
    gain_attn,
    w_qkv,
    w_out,
    gain_conv,
    w_point_in,
    w_depth,
    w_point_out,
    gain_out,
):
    tokens = mel_frames.shape[1] // 4
    limit = mel_frames.shape[1] * lax.axis_size("tm")
    base = lax.axis_index("tm") * mel_frames.shape[1]
    info = jnp.concatenate(
        [
            jnp.reshape(base, (1,)),
            lengths[0],
            jnp.stack([lax.axis_index("rec"), lax.axis_index("tm")]),
            jnp.full((1,), lax.axis_size("tm"), jnp.int32),
        ]
    ).astype(jnp.int32)

    def gather_packed(arrays):
        packed = pack(arrays)
        full = lax.all_gather(packed, ("rec", "tm"), axis=0, tiled=False)
        if full.shape[0] == 32:
            return full
        parts = packed.shape[0] // w_out.shape[0]
        full = full.reshape(full.shape[0], parts, -1, WIDTH).transpose(1, 0, 2, 3)
        full = full.reshape(parts, 32, -1, WIDTH).transpose(1, 0, 2, 3)
        return full.reshape(32, -1, WIDTH)

    late = gather_packed([w_qkv, w_out, w_point_in, w_point_out])
    w_second_all, rounds = gather_ordered(w_second)
    patches, taps = prepare(info, mel_frames[0], w_first, tokens, limit)
    subs = subsample(patches, taps, w_second_all)
    if lax.axis_size("rec") == 4 and lax.axis_size("tm") == 8:
        proj = along_rec(behind(w_proj, *rounds[0]))
        proj = behind(tuple(proj), patches, *rounds[1], *subs[:2])
        proj = to_neighbours(jnp.concatenate(proj, axis=0))
        proj_late = relayed(*behind(proj, *subs))
        proj, places = to_other_core(*proj, *proj_late)
    else:
        proj, places = [lax.all_gather(w_proj, ("rec", "tm"), axis=0, tiled=True)], None
    hidden, normed = project(info, gain_attn[None], subs, proj, places, tokens)
    encoded = conformer_block(
        info,
        hidden,
        normed,
        late,
        gain_conv[None],
        w_depth,
        gain_out[None],
        limit,
    )
    return encoded[None]


def solution(mesh):
    placed = (
        P("rec", "tm", None),
        P("rec", None),
        P(),
        P(("rec", "tm"), None),
        P(("rec", "tm"), None),
        P(),
        P(("rec", "tm"), None),
        P(("rec", "tm"), None),
        P(),
        P(("rec", "tm"), None),
        P(),
        P(("rec", "tm"), None),
        P(),
    )
    return jax.shard_map(
        on_device, mesh=mesh, in_specs=placed, out_specs=P("rec", "tm", None), check_vma=False
    )
```

```python
import functools

import jax
import jax.numpy as jnp
import numpy as np
from jax import lax
from jax.experimental import pallas as pl
from jax.experimental.pallas import tpu as pltpu
from jax.sharding import PartitionSpec as P

WIDTH = 1024
HEADS = 8
HEAD_DIM = 128
KERNEL = 9
WINDOW = 128
CHANNELS = 256
NORM_EPSILON = 1e-05

EDGE = 16
HALO = WINDOW + EDGE
COLS = 256


def segment_of(positions, lengths, limit):
    counted = jnp.zeros(positions.shape, jnp.int32)
    bound = 0
    for k in range(len(lengths) - 1):
        bound = bound + lengths[k]
        counted = counted + (positions >= bound).astype(jnp.int32)
    return jnp.where((positions >= 0) & (positions < limit), counted, -1)


def layer_norm(values, gain):
    row_mean = jnp.mean(values, axis=-1, keepdims=True)
    centred = values - row_mean
    variance = jnp.mean(centred * centred, axis=-1, keepdims=True)
    return centred * lax.rsqrt(variance + NORM_EPSILON) * gain


def exchange(block, axis, distance):
    size = lax.axis_size(axis)
    return lax.ppermute(block, axis, [(i, i ^ distance) for i in range(size)])


def bit_groups():
    groups = []
    for axis, lowest in (("rec", 1), ("tm", 2)):
        bits = []
        bit = lowest
        while bit < lax.axis_size(axis):
            bits.append(bit)
            bit *= 2
        groups += [(axis, bits[k : k + 2]) for k in range(0, len(bits), 2)]
    return groups + [("tm", [1])]


def distances(bits):
    return [0] + [bits[0]] if len(bits) == 1 else [0, bits[0], bits[1], bits[0] + bits[1]]


def can_exchange():
    return all(
        lax.axis_size(axis) & (lax.axis_size(axis) - 1) == 0 and lax.axis_size(axis) > 1
        for axis in ("rec", "tm")
    )


def behind(value, *others):
    return lax.optimization_barrier((value, *others))[0]


def gather_ordered(block, along=None, hold=None):
    if not can_exchange():
        return lax.all_gather(block, ("rec", "tm"), axis=0, tiled=True)
    names = []
    held = block[None]
    for axis, bits in bit_groups():
        if along is not None and axis == "rec":
            got = [piece[None] for piece in along]
        else:
            got = [held] + [exchange(held, axis, d) for d in distances(bits)[1:]]
        if hold is not None and axis == "tm" and bits[0] > 1:
            got = list(behind(tuple(got), hold))
        me = lax.axis_index(axis)
        for at, bit in enumerate(bits):
            high = (me & bit) != 0
            got = [jnp.where(high, got[k ^ (1 << at)], got[k]) for k in range(len(got))]
        held = jnp.concatenate(got, axis=0)
        names = [(axis, bit) for bit in reversed(bits)] + names
    wanted = []
    for axis in ("rec", "tm"):
        wanted += sorted((n for n in names if n[0] == axis), key=lambda n: -n[1])
    order = [names.index(n) for n in wanted]
    dims = held.reshape((2,) * len(names) + block.shape)
    dims = jnp.transpose(dims, order + [len(names), len(names) + 1])
    return dims.reshape((-1,) + block.shape[1:])


def along_rec(block):
    return [block] + [exchange(block, "rec", d) for d in (1, 2, 3)]


def to_neighbours(held):
    return held, exchange(held, "tm", 2), exchange(held, "tm", 4)


def relayed(held, beside, above):
    half = held.shape[0] // 2
    return exchange(beside[:half], "tm", 4), exchange(above[half:], "tm", 2)


def to_other_core(held, beside, above, low, high):
    pieces = [(held, 0, 0, 4), (beside, 2, 0, 4), (above, 4, 0, 4), (low, 6, 0, 2), (high, 6, 2, 2)]
    pieces += [(exchange(p, "tm", 1), far ^ 1, slot, n) for p, far, slot, n in pieces]
    return [p[0] for p in pieces], [p[1:] for p in pieces]


def copies_in(info_ref, sources, places, target, sem):
    if places is None:
        pltpu.make_async_copy(sources[0], target, sem).start()
        return
    rec, tm, tm_size = info_ref[5], info_ref[6], info_ref[7]
    for source, (far, first, number) in zip(sources, places):
        rows = source.shape[0] // number
        for slot in range(number):
            owner = (rec ^ (first + slot)) * tm_size + (tm ^ far)
            if len(target.shape) == 3:
                place = target.at[owner]
            else:
                place = target.at[pl.ds(pl.multiple_of(owner * rows, 16), rows), :]
            pltpu.make_async_copy(source.at[pl.ds(slot * rows, rows), :], place, sem).start()


BINS = 41


def prepare_kernel(limit, info_ref, quads_ref, lane_ref, w_ref, patches_ref, taps_ref):
    base = info_ref[0]
    lengths = [info_ref[1 + k] for k in range(4)]
    tokens = quads_ref.shape[0]
    wide = quads_ref.shape[1]
    source = lax.broadcasted_iota(jnp.int32, (wide, COLS), 0)
    token = lax.broadcasted_iota(jnp.int32, (tokens, COLS), 0)
    own = segment_of(base + 4 * (token - HALO), lengths, limit)
    frame = lane_ref[6:7, :]
    for a in range(3):
        middle = segment_of(base + 4 * (token - HALO) + 2 * a - 2, lengths, limit)
        there = segment_of(base + 4 * (token - HALO) + 2 * a - 3 + frame, lengths, limit)
        same = (middle == own) & (there == middle)
        for h in range(2):
            chosen = (source == lane_ref[2 * a + h : 2 * a + h + 1, :]).astype(jnp.float32)
            made = jnp.dot(
                quads_ref[...], chosen.astype(jnp.bfloat16), preferred_element_type=jnp.float32
            )
            patches_ref[a, h] = jnp.where(same, made, 0.0).astype(jnp.bfloat16)

    row = lax.broadcasted_iota(jnp.int32, (COLS, CHANNELS), 0)
    group = jnp.zeros((COLS, CHANNELS), jnp.int32)
    for k in range(1, 7):
        group = group + (row >= BINS * k).astype(jnp.int32)
    at_bin = row - BINS * group
    spread = []
    for b in range(3):
        total = jnp.zeros((COLS, CHANNELS), jnp.float32)
        for a in range(3):
            tap = w_ref[3 * a + b : 3 * a + b + 1, :]
            high = tap.astype(jnp.bfloat16).astype(jnp.float32)
            total = jnp.where(group == a, high, total)
            total = jnp.where(group == 3 + a, tap - high, total)
        spread.append(total)
    for f in range(20):
        total = jnp.zeros((COLS, CHANNELS), jnp.float32)
        for b in range(3):
            total = jnp.where(at_bin == 2 * f + b, spread[b], total)
        taps_ref[:, f * CHANNELS : (f + 1) * CHANNELS] = total.astype(jnp.bfloat16)


def mel_halos(mel):
    reach = 4 * (HALO + EDGE)
    tm = lax.axis_size("tm")
    forward = [(i, i + 1) for i in range(tm - 1)]
    backward = [(i + 1, i) for i in range(tm - 1)]
    low = lax.ppermute(mel[mel.shape[0] - reach :], "tm", forward)
    return low, lax.ppermute(mel[:reach], "tm", backward)


def prepare(info, mel, low, high, w_first, tokens, limit):
    bins = mel.shape[1]
    quads = jnp.concatenate([low, mel, high], axis=0).reshape(-1, 4 * bins)
    count = tokens + 2 * HALO
    quads = jnp.concatenate(
        [quads[EDGE - 1 : EDGE - 1 + count], quads[EDGE : EDGE + count]], axis=1
    )
    lane = np.arange(COLS)
    frame, at_bin = lane // BINS % 3, lane % BINS
    used = lane < 6 * BINS
    picks = np.full((8, COLS), -1, np.int32)
    for a in range(3):
        for h in range(2):
            wanted = at_bin - 1 + 40 * h
            place = bins * (2 * a + frame + 1) + wanted
            picks[2 * a + h] = np.where(used & (wanted >= 0), place, -1)
    picks[6] = frame
    whole = pl.BlockSpec(memory_space=pltpu.VMEM)
    return pl.pallas_call(
        functools.partial(prepare_kernel, limit),
        out_shape=(
            jax.ShapeDtypeStruct((3, 2, count, COLS), jnp.bfloat16),
            jax.ShapeDtypeStruct((COLS, 20 * CHANNELS), jnp.bfloat16),
        ),
        in_specs=[pl.BlockSpec(memory_space=pltpu.SMEM)] + [whole] * 3,
        out_specs=(whole, whole),
        compiler_params=pltpu.CompilerParams(vmem_limit_bytes=24 * 1024 * 1024),
        cost_estimate=pl.CostEstimate(flops=1024, bytes_accessed=1024, transcendentals=0),
        name="prepare",
    )(info, quads, jnp.asarray(picks), w_first.reshape(9, CHANNELS))


def conv_kernel(begin, count, a_ref, b_ref, w_ref, out_ref, first):
    tokens = out_ref.shape[0]
    rows_step = tokens // 2

    @pl.loop(0, 2)
    def _(r):
        rows = pl.ds(pl.multiple_of(r * rows_step, 16), rows_step)
        for a in range(3):
            for i in range(2 * count + 1):
                at = 2 * begin - 1 + i
                place = slice(i * COLS, (i + 1) * COLS)
                if at < 0:
                    first[a, :, place] = jnp.zeros((rows_step, COLS), jnp.bfloat16)
                    continue
                half, col = divmod(at, 20)
                made = jnp.dot(
                    a_ref[a, half, rows, :],
                    b_ref[:, col * COLS : (col + 1) * COLS],
                    preferred_element_type=jnp.float32,
                )
                first[a, :, place] = jnp.maximum(made, 0.0).astype(jnp.bfloat16)
        for t in range(count):
            total = None
            for a in range(3):
                made = jnp.dot(
                    first[a, :, 2 * t * COLS : (2 * t + 3) * COLS],
                    w_ref[a],
                    preferred_element_type=jnp.float32,
                )
                total = made if total is None else total + made
            out_ref[rows, t * COLS : (t + 1) * COLS] = jnp.maximum(total, 0.0).astype(jnp.bfloat16)


def subsample(patches, taps, w_second):
    tokens = patches.shape[2]
    count = 4
    weights = w_second.reshape(3, 3 * COLS, COLS)
    whole = pl.BlockSpec(memory_space=pltpu.VMEM)
    flops = 2 * tokens * COLS * COLS * (3 * (2 * count + 1) + 9 * count)
    pieces = []
    for begin in range(0, 20, count):
        pieces.append(
            pl.pallas_call(
                functools.partial(conv_kernel, begin, count),
                out_shape=jax.ShapeDtypeStruct((tokens, count * CHANNELS), jnp.bfloat16),
                in_specs=[whole] * 3,
                out_specs=whole,
                scratch_shapes=[
                    pltpu.VMEM((3, tokens // 2, (2 * count + 1) * COLS), jnp.bfloat16)
                ],
                compiler_params=pltpu.CompilerParams(vmem_limit_bytes=20 * 1024 * 1024),
                cost_estimate=pl.CostEstimate(flops=1024, bytes_accessed=1024, transcendentals=0),
                name="subsample",
            )(patches, taps, weights)
        )
    return pieces


def project_kernel(places, info_ref, gain_ref, *rest):
    subs = rest[:5]
    sources = rest[5:-5]
    mid_ref, normed_ref, weights, hidden, sem = rest[-5:]
    copies_in(info_ref, sources, places, weights, sem)
    pltpu.make_async_copy(weights, weights, sem).wait()

    depth = weights.shape[0] // len(subs)

    @pl.loop(0, WIDTH // COLS)
    def _(n):
        here = pl.ds(pl.multiple_of(n * COLS, COLS), COLS)
        total = None
        for piece, sub in enumerate(subs):
            made = jnp.dot(
                sub[...],
                weights[piece * depth : (piece + 1) * depth, here],
                preferred_element_type=jnp.float32,
            )
            total = made if total is None else total + made
        hidden[:, here] = total

    gain = gain_ref[...]
    chunk = 160

    @pl.loop(0, hidden.shape[0] // chunk)
    def _(r):
        rows = pl.ds(pl.multiple_of(r * chunk, chunk), chunk)
        normed_ref[rows, :] = layer_norm(hidden[rows, :], gain).astype(jnp.bfloat16)

    mid_ref[...] = hidden[WINDOW : WINDOW + mid_ref.shape[0], :]


def project(info, gain, subs, sources, places, tokens):
    rows_all = tokens + 2 * HALO
    rows_mid = tokens + 2 * EDGE
    whole = pl.BlockSpec(memory_space=pltpu.VMEM)
    depth = sum(sub.shape[1] for sub in subs)
    return pl.pallas_call(
        functools.partial(project_kernel, places),
        out_shape=(
            jax.ShapeDtypeStruct((rows_mid, WIDTH), jnp.float32),
            jax.ShapeDtypeStruct((rows_all, WIDTH), jnp.bfloat16),
        ),
        in_specs=[pl.BlockSpec(memory_space=pltpu.SMEM)]
        + [whole] * 6
        + [pl.BlockSpec(memory_space=pl.ANY)] * len(sources),
        out_specs=(whole, whole),
        scratch_shapes=[
            pltpu.VMEM((depth, WIDTH), jnp.bfloat16),
            pltpu.VMEM((rows_all, WIDTH), jnp.float32),
            pltpu.SemaphoreType.DMA(()),
        ],
        compiler_params=pltpu.CompilerParams(vmem_limit_bytes=34 * 1024 * 1024),
        cost_estimate=pl.CostEstimate(flops=1024, bytes_accessed=1024, transcendentals=0),
        name="project",
    )(info, gain, *subs, *sources)


def join_kernel(proj_ref, second_ref, out_ref):
    rows = proj_ref.shape[0]
    out_ref[0:rows, :] = proj_ref[...]
    second = second_ref[...].astype(jnp.float32)
    spare = jnp.zeros((8, CHANNELS), jnp.float32)
    for k in range(3):
        part = jnp.concatenate([second[24 * k : 24 * k + 24], spare], axis=0)
        out_ref[rows : rows + 32, k * CHANNELS : (k + 1) * CHANNELS] = part.astype(jnp.bfloat16)
    out_ref[rows : rows + 32, 3 * CHANNELS :] = jnp.zeros(
        (32, WIDTH - 3 * CHANNELS), jnp.bfloat16
    )


def join(w_proj, w_second):
    whole = pl.BlockSpec(memory_space=pltpu.VMEM)
    rows = w_proj.shape[0] + 32
    return pl.pallas_call(
        join_kernel,
        out_shape=jax.ShapeDtypeStruct((rows, WIDTH), jnp.bfloat16),
        in_specs=[whole] * 2,
        out_specs=whole,
        compiler_params=pltpu.CompilerParams(vmem_limit_bytes=4 * 1024 * 1024),
        cost_estimate=pl.CostEstimate(flops=1024, bytes_accessed=1024, transcendentals=0),
        name="join",
    )(w_proj, w_second)


def second_part(joined):
    part = joined[-32:-8, : 3 * CHANNELS].reshape(24, 3, CHANNELS)
    return part.transpose(1, 0, 2).reshape(72, CHANNELS)


def pack_kernel(pieces, *refs):
    *sources, out_ref, held, sems = refs
    at = 0
    copies = []
    for source, first in pieces:
        rows = sources[source].shape[0]
        copies.append(
            pltpu.make_async_copy(
                sources[source].at[:, pl.ds(first, WIDTH)],
                held.at[pl.ds(at, rows), :],
                sems.at[len(copies)],
            )
        )
        at += rows
    for copy in copies:
        copy.start()
    for copy in copies:
        copy.wait()
    out = pltpu.make_async_copy(held, out_ref, sems.at[len(copies)])
    out.start()
    out.wait()


def pack(arrays):
    pieces = [
        (k, first) for k, array in enumerate(arrays) for first in range(0, array.shape[1], WIDTH)
    ]
    if any(array.shape[0] % 16 for array in arrays):
        return jnp.concatenate([arrays[k][:, c : c + WIDTH] for k, c in pieces], axis=0)
    rows = sum(arrays[k].shape[0] for k, _ in pieces)
    far = pl.BlockSpec(memory_space=pltpu.HBM)
    return pl.pallas_call(
        functools.partial(pack_kernel, pieces),
        out_shape=jax.ShapeDtypeStruct((rows, WIDTH), jnp.bfloat16),
        in_specs=[far] * len(arrays),
        out_specs=far,
        scratch_shapes=[
            pltpu.VMEM((rows, WIDTH), jnp.bfloat16),
            pltpu.SemaphoreType.DMA((len(pieces) + 1,)),
        ],
        compiler_params=pltpu.CompilerParams(vmem_limit_bytes=60 * 1024 * 1024),
        cost_estimate=pl.CostEstimate(flops=1024, bytes_accessed=1024, transcendentals=0),
        name="pack",
    )(*arrays)


def columns(weights, part, parts, n):
    rows = weights.shape[1] // parts
    return weights[:, part * rows : (part + 1) * rows, n * COLS : (n + 1) * COLS].reshape(-1, COLS)


def block_kernel(
    tokens,
    limit,
    places,
    info_ref,
    normed_ref,
    gain_conv_ref,
    depth_ref,
    gain_out_ref,
    hidden_ref,
    *rest,
):
    sources, late_ref = rest[:-13], rest[-13]
    out_ref, early_w, late_w, keys, values, queries, context, attended, gated, masks, biases = rest[
        -12:-1
    ]
    sems = rest[-1]
    rows_mid = tokens + 2 * EDGE
    share = late_w.shape[1] // 4
    copies_in(info_ref, sources, places, early_w, sems.at[0])
    late_copies = []
    for k in range(4):
        late_copies.append(
            pltpu.make_async_copy(
                late_ref.at[:, pl.ds(k * share, share), :],
                late_w.at[:, pl.ds(k * share, share), :],
                sems.at[3 + k],
            )
        )
    hidden_copy = pltpu.make_async_copy(hidden_ref, attended, sems.at[7])
    base = info_ref[0]
    lengths = [info_ref[1 + k] for k in range(4)]

    blocks = []
    at_row = 0
    while at_row < rows_mid:
        size = 128 + (EDGE if at_row == 0 or at_row + 128 + EDGE == rows_mid else 0)
        blocks.append((at_row, size))
        at_row += size

    for at, (start, size) in enumerate(blocks):
        span = size + 2 * WINDOW
        q_row = lax.broadcasted_iota(jnp.int32, (size, 1), 0)
        k_row = lax.broadcasted_iota(jnp.int32, (1, span), 1)
        q_seg = segment_of(base + 4 * (q_row + start - EDGE), lengths, limit)
        k_seg = segment_of(base + 4 * (k_row + start - HALO), lengths, limit)
        apart = k_row - q_row
        allowed = (apart >= 0) & (apart <= 2 * WINDOW) & (q_seg == k_seg)
        biases[at, 0:size, 0:span] = jnp.where(allowed, 0.0, -1e30)
    for head in range(HEADS):
        values[:, (2 * head + 1) * HEAD_DIM : (2 * head + 2) * HEAD_DIM] = jnp.ones(
            (values.shape[0], HEAD_DIM), jnp.bfloat16
        )

    pltpu.make_async_copy(early_w, early_w, sems.at[0]).wait()
    hidden_copy.start()
    for copy in late_copies:
        copy.start()
    for n in range(WIDTH // COLS):
        queries[:, n * COLS : (n + 1) * COLS] = jnp.dot(
            normed_ref[WINDOW : WINDOW + rows_mid, :],
            early_w[:, :, n * COLS : (n + 1) * COLS].reshape(-1, COLS),
            preferred_element_type=jnp.float32,
        ).astype(jnp.bfloat16)
    row = lax.broadcasted_iota(jnp.int32, (tokens, HEAD_DIM), 0)
    own = segment_of(base + 4 * row, lengths, limit)
    for k in range(KERNEL):
        there = segment_of(base + 4 * (row + k - KERNEL // 2), lengths, limit)
        masks[k] = (there == own).astype(jnp.float32)
    for n in range(WIDTH // COLS):
        keys[:, n * COLS : (n + 1) * COLS] = jnp.dot(
            normed_ref[...], early_w[:, :, 1 * WIDTH + n * COLS : 1 * WIDTH + (n + 1) * COLS].reshape(-1, COLS), preferred_element_type=jnp.float32
        ).astype(jnp.bfloat16)
    for n in range(WIDTH // COLS):
        made = jnp.dot(
            normed_ref[...], early_w[:, :, 2 * WIDTH + n * COLS : 2 * WIDTH + (n + 1) * COLS].reshape(-1, COLS), preferred_element_type=jnp.float32
        ).astype(jnp.bfloat16)
        for k in range(COLS // HEAD_DIM):
            first = 2 * n * COLS + 2 * k * HEAD_DIM
            values[:, first : first + HEAD_DIM] = made[:, k * HEAD_DIM : (k + 1) * HEAD_DIM]

    scale = HEAD_DIM**-0.5 * 1.4426950408889634

    @pl.loop(0, HEADS // 2)
    def _(pair):
        for at, (start, size) in enumerate(blocks):
            span = size + 2 * WINDOW
            for side in range(2):
                head = 2 * pair + side
                lanes = pl.ds(pl.multiple_of(head * HEAD_DIM, HEAD_DIM), HEAD_DIM)
                wide = pl.ds(pl.multiple_of(head * 2 * HEAD_DIM, 2 * HEAD_DIM), 2 * HEAD_DIM)
                scores = lax.dot_general(
                    queries[start : start + size, lanes],
                    keys[start : start + span, lanes],
                    (((1,), (1,)), ((), ())),
                    preferred_element_type=jnp.float32,
                )
                scores = scores * scale + biases[at, 0:size, 0:span]
                exped = jnp.exp2(scores - jnp.max(scores, axis=-1, keepdims=True))
                mixed = jnp.dot(
                    exped.astype(jnp.bfloat16),
                    values[start : start + span, wide],
                    preferred_element_type=jnp.float32,
                )
                context[start : start + size, lanes] = (
                    mixed[:, :HEAD_DIM] / mixed[:, HEAD_DIM:]
                ).astype(jnp.bfloat16)

    hidden_copy.wait()
    late_copies[0].wait()
    gain_c = gain_conv_ref[...]
    half = rows_mid // 2
    for r in range(2):
        rows = slice(r * half, (r + 1) * half)
        for n in range(WIDTH // COLS):
            attended[rows, n * COLS : (n + 1) * COLS] += jnp.dot(
                context[rows, :], columns(late_w, 0, 4, n), preferred_element_type=jnp.float32
            )
        queries[rows, :] = layer_norm(attended[rows, :], gain_c).astype(jnp.bfloat16)

    late_copies[1].wait()
    late_copies[2].wait()
    for n in range(WIDTH // COLS):
        value = jnp.dot(queries[...], columns(late_w, 1, 4, n), preferred_element_type=jnp.float32)
        gate = jnp.dot(queries[...], columns(late_w, 2, 4, n), preferred_element_type=jnp.float32)
        made = (value * jax.nn.sigmoid(gate)).astype(jnp.bfloat16).astype(jnp.float32)
        for j in range(COLS // HEAD_DIM):
            at = n * (COLS // HEAD_DIM) + j
            gated[at] = made[:, j * HEAD_DIM : (j + 1) * HEAD_DIM]
            lanes = slice(at * HEAD_DIM, (at + 1) * HEAD_DIM)
            total = jnp.zeros((tokens, HEAD_DIM), jnp.float32)
            for k in range(KERNEL):
                begin = EDGE - KERNEL // 2 + k
                tap = gated[at, begin : begin + tokens, :] * depth_ref[k : k + 1, lanes]
                total = total + (tap if k == KERNEL // 2 else tap * masks[k])
            context[0:tokens, lanes] = (total * jax.nn.sigmoid(total)).astype(jnp.bfloat16)

    late_copies[3].wait()
    gain_o = gain_out_ref[...]
    half = tokens // 2
    for r in range(2):
        rows = slice(r * half, (r + 1) * half)
        mid = slice(EDGE + r * half, EDGE + (r + 1) * half)
        for n in range(WIDTH // COLS):
            attended[mid, n * COLS : (n + 1) * COLS] += jnp.dot(
                context[rows, :], columns(late_w, 3, 4, n), preferred_element_type=jnp.float32
            )
        out_ref[rows, :] = layer_norm(attended[mid, :], gain_o).astype(jnp.bfloat16)


def conformer_block(
    info, hidden, normed, sources, places, late, gain_conv, w_depth, gain_out, limit
):
    rows_all = normed.shape[0]
    rows_mid = hidden.shape[0]
    tokens = rows_mid - 2 * EDGE
    whole = pl.BlockSpec(memory_space=pltpu.VMEM)
    far = pl.BlockSpec(memory_space=pltpu.HBM)
    flops = 2 * rows_all * WIDTH * 2 * WIDTH + 2 * rows_mid * WIDTH * WIDTH * 5
    return pl.pallas_call(
        functools.partial(block_kernel, tokens, limit, places),
        out_shape=jax.ShapeDtypeStruct((tokens, WIDTH), jnp.bfloat16),
        in_specs=[pl.BlockSpec(memory_space=pltpu.SMEM)] + [whole] * 4 + [far] * (len(sources) + 2),
        out_specs=whole,
        scratch_shapes=[
            pltpu.VMEM((32, WIDTH // 32, 3 * WIDTH), jnp.bfloat16),
            pltpu.VMEM((32, 4 * WIDTH // 32, WIDTH), jnp.bfloat16),
            pltpu.VMEM((rows_all, WIDTH), jnp.bfloat16),
            pltpu.VMEM((rows_all, 2 * WIDTH), jnp.bfloat16),
            pltpu.VMEM((rows_mid, WIDTH), jnp.bfloat16),
            pltpu.VMEM((rows_mid, WIDTH), jnp.bfloat16),
            pltpu.VMEM((rows_mid, WIDTH), jnp.float32),
            pltpu.VMEM((WIDTH // HEAD_DIM, rows_mid, HEAD_DIM), jnp.float32),
            pltpu.VMEM((KERNEL, tokens, HEAD_DIM), jnp.float32),
            pltpu.VMEM((4, 128 + EDGE, 512), jnp.float32),
            pltpu.SemaphoreType.DMA((8,)),
        ],
        compiler_params=pltpu.CompilerParams(vmem_limit_bytes=60 * 1024 * 1024),
        cost_estimate=pl.CostEstimate(flops=1024, bytes_accessed=1024, transcendentals=0),
        name="conformer_block",
    )(info, normed, gain_conv, w_depth, gain_out, hidden, *sources, late)


def on_device(
    mel_frames,
    lengths,
    w_first,
    w_second,
    w_proj,
    gain_attn,
    w_qkv,
    w_out,
    gain_conv,
    w_point_in,
    w_depth,
    w_point_out,
    gain_out,
):
    tokens = mel_frames.shape[1] // 4
    limit = mel_frames.shape[1] * lax.axis_size("tm")
    base = lax.axis_index("tm") * mel_frames.shape[1]
    info = jnp.concatenate(
        [
            jnp.reshape(base, (1,)),
            lengths[0],
            jnp.stack([lax.axis_index("rec"), lax.axis_index("tm")]),
            jnp.full((1,), lax.axis_size("tm"), jnp.int32),
        ]
    ).astype(jnp.int32)

    def gather_packed(packed, share):
        full = lax.all_gather(packed, ("rec", "tm"), axis=0, tiled=False)
        if full.shape[0] == 32:
            return full
        parts = packed.shape[0] // share
        full = full.reshape(full.shape[0], parts, -1, WIDTH).transpose(1, 0, 2, 3)
        full = full.reshape(parts, 32, -1, WIDTH).transpose(1, 0, 2, 3)
        return full.reshape(32, -1, WIDTH)

    late_packed = pack([w_out, w_point_in, w_point_out])
    late = gather_packed(late_packed, w_out.shape[0])
    low, high = mel_halos(mel_frames[0])
    patches, taps = prepare(info, mel_frames[0], low, high, w_first, tokens, limit)
    if lax.axis_size("rec") == 4 and lax.axis_size("tm") == 8 and w_proj.shape[0] == 160:
        joined = join(behind(w_proj, late_packed), w_second)
        qkv = along_rec(behind(w_qkv, low, high))
        joined = behind(tuple(along_rec(joined)), patches)
        proj = jnp.concatenate([piece[:-32] for piece in joined], axis=0)
        second = [second_part(piece) for piece in joined]
        second = gather_ordered(w_second, second, proj)
        subs = subsample(patches, taps, second)
        proj = to_neighbours(proj)
        qkv = behind(tuple(qkv), *proj[1:], *subs[:2])
        qkv = to_neighbours(jnp.concatenate(qkv, axis=0))
        proj_late = relayed(*behind(proj, *subs[:2]))
        proj, places = to_other_core(*proj, *behind(proj_late, *subs))
        hidden, normed = project(info, gain_attn[None], subs, proj, places, tokens)
        qkv_late = behind(relayed(*qkv), normed)
        qkv, places = to_other_core(*qkv, *qkv_late)
    else:
        subs = subsample(patches, taps, gather_ordered(w_second))
        proj = [lax.all_gather(w_proj, ("rec", "tm"), axis=0, tiled=True)]
        hidden, normed = project(info, gain_attn[None], subs, proj, None, tokens)
        qkv = lax.all_gather(w_qkv, ("rec", "tm"), axis=0, tiled=True)
        qkv, places = [qkv.reshape(32, WIDTH // 32, 3 * WIDTH)], None
    encoded = conformer_block(
        info,
        hidden,
        normed,
        qkv,
        places,
        late,
        gain_conv[None],
        w_depth,
        gain_out[None],
        limit,
    )
    return encoded[None]


def solution(mesh):
    placed = (
        P("rec", "tm", None),
        P("rec", None),
        P(),
        P(("rec", "tm"), None),
        P(("rec", "tm"), None),
        P(),
        P(("rec", "tm"), None),
        P(("rec", "tm"), None),
        P(),
        P(("rec", "tm"), None),
        P(),
        P(("rec", "tm"), None),
        P(),
    )
    return jax.shard_map(
        on_device, mesh=mesh, in_specs=placed, out_specs=P("rec", "tm", None), check_vma=False
    )
```

```python
import functools

import jax
import jax.numpy as jnp
import numpy as np
from jax import lax
from jax.experimental import pallas as pl
from jax.experimental.pallas import tpu as pltpu
from jax.sharding import PartitionSpec as P

WIDTH = 1024
HEADS = 8
HEAD_DIM = 128
KERNEL = 9
WINDOW = 128
CHANNELS = 256
NORM_EPSILON = 1e-05

EDGE = 16
HALO = WINDOW + EDGE
COLS = 256


def segment_of(positions, lengths, limit):
    counted = jnp.zeros(positions.shape, jnp.int32)
    bound = 0
    for k in range(len(lengths) - 1):
        bound = bound + lengths[k]
        counted = counted + (positions >= bound).astype(jnp.int32)
    return jnp.where((positions >= 0) & (positions < limit), counted, -1)


def layer_norm(values, gain):
    row_mean = jnp.mean(values, axis=-1, keepdims=True)
    centred = values - row_mean
    variance = jnp.mean(centred * centred, axis=-1, keepdims=True)
    return centred * lax.rsqrt(variance + NORM_EPSILON) * gain


def exchange(block, axis, distance):
    size = lax.axis_size(axis)
    return lax.ppermute(block, axis, [(i, i ^ distance) for i in range(size)])


def bit_groups():
    groups = []
    for axis, lowest in (("rec", 1), ("tm", 2)):
        bits = []
        bit = lowest
        while bit < lax.axis_size(axis):
            bits.append(bit)
            bit *= 2
        groups += [(axis, bits[k : k + 2]) for k in range(0, len(bits), 2)]
    return groups + [("tm", [1])]


def distances(bits):
    return [0] + [bits[0]] if len(bits) == 1 else [0, bits[0], bits[1], bits[0] + bits[1]]


def can_exchange():
    return all(
        lax.axis_size(axis) & (lax.axis_size(axis) - 1) == 0 and lax.axis_size(axis) > 1
        for axis in ("rec", "tm")
    )


def behind(value, *others):
    return lax.optimization_barrier((value, *others))[0]


def gather_ordered(block):
    if not can_exchange():
        return lax.all_gather(block, ("rec", "tm"), axis=0, tiled=True), []
    names = []
    held = block[None]
    rounds = []
    for axis, bits in bit_groups():
        got = [held] + [exchange(held, axis, d) for d in distances(bits)[1:]]
        rounds.append(got[1:])
        me = lax.axis_index(axis)
        for at, bit in enumerate(bits):
            high = (me & bit) != 0
            got = [jnp.where(high, got[k ^ (1 << at)], got[k]) for k in range(len(got))]
        held = jnp.concatenate(got, axis=0)
        names = [(axis, bit) for bit in reversed(bits)] + names
    wanted = []
    for axis in ("rec", "tm"):
        wanted += sorted((n for n in names if n[0] == axis), key=lambda n: -n[1])
    order = [names.index(n) for n in wanted]
    dims = held.reshape((2,) * len(names) + block.shape)
    dims = jnp.transpose(dims, order + [len(names), len(names) + 1])
    return dims.reshape((-1,) + block.shape[1:]), rounds


def along_rec(block):
    return [block] + [exchange(block, "rec", d) for d in (1, 2, 3)]


def to_neighbours(held):
    return held, exchange(held, "tm", 2), exchange(held, "tm", 4)


def relayed(held, beside, above):
    half = held.shape[0] // 2
    return exchange(beside[:half], "tm", 4), exchange(above[half:], "tm", 2)


def to_other_core(held, beside, above, low, high):
    pieces = [(held, 0, 0, 4), (beside, 2, 0, 4), (above, 4, 0, 4), (low, 6, 0, 2), (high, 6, 2, 2)]
    pieces += [(exchange(p, "tm", 1), far ^ 1, slot, n) for p, far, slot, n in pieces]
    return [p[0] for p in pieces], [p[1:] for p in pieces]


def copies_in(info_ref, sources, places, target, sem):
    if places is None:
        pltpu.make_async_copy(sources[0], target, sem).start()
        return
    rec, tm, tm_size = info_ref[5], info_ref[6], info_ref[7]
    for source, (far, first, number) in zip(sources, places):
        rows = source.shape[0] // number
        for slot in range(number):
            owner = (rec ^ (first + slot)) * tm_size + (tm ^ far)
            if len(target.shape) == 3:
                place = target.at[owner]
            else:
                place = target.at[pl.ds(pl.multiple_of(owner * rows, 16), rows), :]
            pltpu.make_async_copy(source.at[pl.ds(slot * rows, rows), :], place, sem).start()


BINS = 41


def prepare_kernel(limit, info_ref, quads_ref, lane_ref, w_ref, patches_ref, taps_ref):
    base = info_ref[0]
    lengths = [info_ref[1 + k] for k in range(4)]
    tokens = quads_ref.shape[0]
    wide = quads_ref.shape[1]
    source = lax.broadcasted_iota(jnp.int32, (wide, COLS), 0)
    token = lax.broadcasted_iota(jnp.int32, (tokens, COLS), 0)
    own = segment_of(base + 4 * (token - HALO), lengths, limit)
    frame = lane_ref[6:7, :]
    for a in range(3):
        middle = segment_of(base + 4 * (token - HALO) + 2 * a - 2, lengths, limit)
        there = segment_of(base + 4 * (token - HALO) + 2 * a - 3 + frame, lengths, limit)
        same = (middle == own) & (there == middle)
        for h in range(2):
            chosen = (source == lane_ref[2 * a + h : 2 * a + h + 1, :]).astype(jnp.float32)
            made = jnp.dot(
                quads_ref[...], chosen.astype(jnp.bfloat16), preferred_element_type=jnp.float32
            )
            patches_ref[a, h] = jnp.where(same, made, 0.0).astype(jnp.bfloat16)

    row = lax.broadcasted_iota(jnp.int32, (COLS, CHANNELS), 0)
    group = jnp.zeros((COLS, CHANNELS), jnp.int32)
    for k in range(1, 7):
        group = group + (row >= BINS * k).astype(jnp.int32)
    at_bin = row - BINS * group
    spread = []
    for b in range(3):
        total = jnp.zeros((COLS, CHANNELS), jnp.float32)
        for a in range(3):
            tap = w_ref[3 * a + b : 3 * a + b + 1, :]
            high = tap.astype(jnp.bfloat16).astype(jnp.float32)
            total = jnp.where(group == a, high, total)
            total = jnp.where(group == 3 + a, tap - high, total)
        spread.append(total)
    for f in range(20):
        total = jnp.zeros((COLS, CHANNELS), jnp.float32)
        for b in range(3):
            total = jnp.where(at_bin == 2 * f + b, spread[b], total)
        taps_ref[:, f * CHANNELS : (f + 1) * CHANNELS] = total.astype(jnp.bfloat16)


def mel_halos(mel):
    reach = 4 * (HALO + EDGE)
    tm = lax.axis_size("tm")
    forward = [(i, i + 1) for i in range(tm - 1)]
    backward = [(i + 1, i) for i in range(tm - 1)]
    low = lax.ppermute(mel[mel.shape[0] - reach :], "tm", forward)
    return low, lax.ppermute(mel[:reach], "tm", backward)


def prepare(info, mel, low, high, w_first, tokens, limit):
    bins = mel.shape[1]
    quads = jnp.concatenate([low, mel, high], axis=0).reshape(-1, 4 * bins)
    count = tokens + 2 * HALO
    quads = jnp.concatenate(
        [quads[EDGE - 1 : EDGE - 1 + count], quads[EDGE : EDGE + count]], axis=1
    )
    lane = np.arange(COLS)
    frame, at_bin = lane // BINS % 3, lane % BINS
    used = lane < 6 * BINS
    picks = np.full((8, COLS), -1, np.int32)
    for a in range(3):
        for h in range(2):
            wanted = at_bin - 1 + 40 * h
            place = bins * (2 * a + frame + 1) + wanted
            picks[2 * a + h] = np.where(used & (wanted >= 0), place, -1)
    picks[6] = frame
    whole = pl.BlockSpec(memory_space=pltpu.VMEM)
    return pl.pallas_call(
        functools.partial(prepare_kernel, limit),
        out_shape=(
            jax.ShapeDtypeStruct((3, 2, count, COLS), jnp.bfloat16),
            jax.ShapeDtypeStruct((COLS, 20 * CHANNELS), jnp.bfloat16),
        ),
        in_specs=[pl.BlockSpec(memory_space=pltpu.SMEM)] + [whole] * 3,
        out_specs=(whole, whole),
        compiler_params=pltpu.CompilerParams(vmem_limit_bytes=24 * 1024 * 1024),
        cost_estimate=pl.CostEstimate(flops=1024, bytes_accessed=1024, transcendentals=0),
        name="prepare",
    )(info, quads, jnp.asarray(picks), w_first.reshape(9, CHANNELS))


def conv_kernel(begin, count, a_ref, b_ref, w_ref, out_ref, first):
    tokens = out_ref.shape[0]
    rows_step = tokens // 2

    @pl.loop(0, 2)
    def _(r):
        rows = pl.ds(pl.multiple_of(r * rows_step, 16), rows_step)
        for a in range(3):
            for i in range(2 * count + 1):
                at = 2 * begin - 1 + i
                place = slice(i * COLS, (i + 1) * COLS)
                if at < 0:
                    first[a, :, place] = jnp.zeros((rows_step, COLS), jnp.bfloat16)
                    continue
                half, col = divmod(at, 20)
                made = jnp.dot(
                    a_ref[a, half, rows, :],
                    b_ref[:, col * COLS : (col + 1) * COLS],
                    preferred_element_type=jnp.float32,
                )
                first[a, :, place] = jnp.maximum(made, 0.0).astype(jnp.bfloat16)
        for t in range(count):
            total = None
            for a in range(3):
                made = jnp.dot(
                    first[a, :, 2 * t * COLS : (2 * t + 3) * COLS],
                    w_ref[a],
                    preferred_element_type=jnp.float32,
                )
                total = made if total is None else total + made
            out_ref[rows, t * COLS : (t + 1) * COLS] = jnp.maximum(total, 0.0).astype(jnp.bfloat16)


def subsample(patches, taps, w_second):
    tokens = patches.shape[2]
    count = 4
    weights = w_second.reshape(3, 3 * COLS, COLS)
    whole = pl.BlockSpec(memory_space=pltpu.VMEM)
    flops = 2 * tokens * COLS * COLS * (3 * (2 * count + 1) + 9 * count)
    pieces = []
    for begin in range(0, 20, count):
        pieces.append(
            pl.pallas_call(
                functools.partial(conv_kernel, begin, count),
                out_shape=jax.ShapeDtypeStruct((tokens, count * CHANNELS), jnp.bfloat16),
                in_specs=[whole] * 3,
                out_specs=whole,
                scratch_shapes=[
                    pltpu.VMEM((3, tokens // 2, (2 * count + 1) * COLS), jnp.bfloat16)
                ],
                compiler_params=pltpu.CompilerParams(vmem_limit_bytes=20 * 1024 * 1024),
                cost_estimate=pl.CostEstimate(flops=1024, bytes_accessed=1024, transcendentals=0),
                name="subsample",
            )(patches, taps, weights)
        )
    return pieces


def project_kernel(places, info_ref, gain_ref, *rest):
    subs = rest[:5]
    sources = rest[5:-5]
    mid_ref, normed_ref, weights, hidden, sem = rest[-5:]
    copies_in(info_ref, sources, places, weights, sem)
    pltpu.make_async_copy(weights, weights, sem).wait()

    depth = weights.shape[0] // len(subs)

    @pl.loop(0, WIDTH // COLS)
    def _(n):
        here = pl.ds(pl.multiple_of(n * COLS, COLS), COLS)
        total = None
        for piece, sub in enumerate(subs):
            made = jnp.dot(
                sub[...],
                weights[piece * depth : (piece + 1) * depth, here],
                preferred_element_type=jnp.float32,
            )
            total = made if total is None else total + made
        hidden[:, here] = total

    gain = gain_ref[...]
    chunk = 160

    @pl.loop(0, hidden.shape[0] // chunk)
    def _(r):
        rows = pl.ds(pl.multiple_of(r * chunk, chunk), chunk)
        normed_ref[rows, :] = layer_norm(hidden[rows, :], gain).astype(jnp.bfloat16)

    mid_ref[...] = hidden[WINDOW : WINDOW + mid_ref.shape[0], :]


def project(info, gain, subs, sources, places, tokens):
    rows_all = tokens + 2 * HALO
    rows_mid = tokens + 2 * EDGE
    whole = pl.BlockSpec(memory_space=pltpu.VMEM)
    depth = sum(sub.shape[1] for sub in subs)
    return pl.pallas_call(
        functools.partial(project_kernel, places),
        out_shape=(
            jax.ShapeDtypeStruct((rows_mid, WIDTH), jnp.float32),
            jax.ShapeDtypeStruct((rows_all, WIDTH), jnp.bfloat16),
        ),
        in_specs=[pl.BlockSpec(memory_space=pltpu.SMEM)]
        + [whole] * 6
        + [pl.BlockSpec(memory_space=pl.ANY)] * len(sources),
        out_specs=(whole, whole),
        scratch_shapes=[
            pltpu.VMEM((depth, WIDTH), jnp.bfloat16),
            pltpu.VMEM((rows_all, WIDTH), jnp.float32),
            pltpu.SemaphoreType.DMA(()),
        ],
        compiler_params=pltpu.CompilerParams(vmem_limit_bytes=34 * 1024 * 1024),
        cost_estimate=pl.CostEstimate(flops=1024, bytes_accessed=1024, transcendentals=0),
        name="project",
    )(info, gain, *subs, *sources)


def pack_kernel(pieces, *refs):
    *sources, out_ref, held, sems = refs
    at = 0
    copies = []
    for source, first in pieces:
        rows = sources[source].shape[0]
        copies.append(
            pltpu.make_async_copy(
                sources[source].at[:, pl.ds(first, WIDTH)],
                held.at[pl.ds(at, rows), :],
                sems.at[len(copies)],
            )
        )
        at += rows
    for copy in copies:
        copy.start()
    for copy in copies:
        copy.wait()
    out = pltpu.make_async_copy(held, out_ref, sems.at[len(copies)])
    out.start()
    out.wait()


def pack(arrays):
    pieces = [
        (k, first) for k, array in enumerate(arrays) for first in range(0, array.shape[1], WIDTH)
    ]
    if any(array.shape[0] % 16 for array in arrays):
        return jnp.concatenate([arrays[k][:, c : c + WIDTH] for k, c in pieces], axis=0)
    rows = sum(arrays[k].shape[0] for k, _ in pieces)
    far = pl.BlockSpec(memory_space=pltpu.HBM)
    return pl.pallas_call(
        functools.partial(pack_kernel, pieces),
        out_shape=jax.ShapeDtypeStruct((rows, WIDTH), jnp.bfloat16),
        in_specs=[far] * len(arrays),
        out_specs=far,
        scratch_shapes=[
            pltpu.VMEM((rows, WIDTH), jnp.bfloat16),
            pltpu.SemaphoreType.DMA((len(pieces) + 1,)),
        ],
        compiler_params=pltpu.CompilerParams(vmem_limit_bytes=60 * 1024 * 1024),
        cost_estimate=pl.CostEstimate(flops=1024, bytes_accessed=1024, transcendentals=0),
        name="pack",
    )(*arrays)


def columns(weights, part, parts, n):
    rows = weights.shape[1] // parts
    return weights[:, part * rows : (part + 1) * rows, n * COLS : (n + 1) * COLS].reshape(-1, COLS)


def block_kernel(
    tokens,
    limit,
    info_ref,
    normed_ref,
    gain_conv_ref,
    depth_ref,
    gain_out_ref,
    hidden_ref,
    weights_ref,
    out_ref,
    early_w,
    late_w,
    keys,
    values,
    queries,
    context,
    attended,
    gated,
    masks,
    biases,
    sems,
):
    rows_mid = tokens + 2 * EDGE
    share = early_w.shape[1] // 3
    early_copies = []
    for k in range(3):
        part = pl.ds(k * share, share)
        early_copies.append(
            pltpu.make_async_copy(
                weights_ref.at[:, part, :], early_w.at[:, part, :], sems.at[k]
            )
        )
    late_copies = []
    for k in range(4):
        late_copies.append(
            pltpu.make_async_copy(
                weights_ref.at[:, pl.ds((3 + k) * share, share), :],
                late_w.at[:, pl.ds(k * share, share), :],
                sems.at[3 + k],
            )
        )
    hidden_copy = pltpu.make_async_copy(hidden_ref, attended, sems.at[7])
    for copy in early_copies:
        copy.start()
    base = info_ref[0]
    lengths = [info_ref[1 + k] for k in range(4)]

    blocks = []
    at_row = 0
    while at_row < rows_mid:
        size = 128 + (EDGE if at_row == 0 or at_row + 128 + EDGE == rows_mid else 0)
        blocks.append((at_row, size))
        at_row += size

    for at, (start, size) in enumerate(blocks):
        span = size + 2 * WINDOW
        q_row = lax.broadcasted_iota(jnp.int32, (size, 1), 0)
        k_row = lax.broadcasted_iota(jnp.int32, (1, span), 1)
        q_seg = segment_of(base + 4 * (q_row + start - EDGE), lengths, limit)
        k_seg = segment_of(base + 4 * (k_row + start - HALO), lengths, limit)
        apart = k_row - q_row
        allowed = (apart >= 0) & (apart <= 2 * WINDOW) & (q_seg == k_seg)
        biases[at, 0:size, 0:span] = jnp.where(allowed, 0.0, -1e30)
    for head in range(HEADS):
        values[:, (2 * head + 1) * HEAD_DIM : (2 * head + 2) * HEAD_DIM] = jnp.ones(
            (values.shape[0], HEAD_DIM), jnp.bfloat16
        )

    early_copies[0].wait()
    hidden_copy.start()
    for copy in late_copies:
        copy.start()
    for n in range(WIDTH // COLS):
        queries[:, n * COLS : (n + 1) * COLS] = jnp.dot(
            normed_ref[WINDOW : WINDOW + rows_mid, :],
            columns(early_w, 0, 3, n),
            preferred_element_type=jnp.float32,
        ).astype(jnp.bfloat16)
    row = lax.broadcasted_iota(jnp.int32, (tokens, HEAD_DIM), 0)
    own = segment_of(base + 4 * row, lengths, limit)
    for k in range(KERNEL):
        there = segment_of(base + 4 * (row + k - KERNEL // 2), lengths, limit)
        masks[k] = (there == own).astype(jnp.float32)
    early_copies[1].wait()
    for n in range(WIDTH // COLS):
        keys[:, n * COLS : (n + 1) * COLS] = jnp.dot(
            normed_ref[...], columns(early_w, 1, 3, n), preferred_element_type=jnp.float32
        ).astype(jnp.bfloat16)
    early_copies[2].wait()
    for n in range(WIDTH // COLS):
        made = jnp.dot(
            normed_ref[...], columns(early_w, 2, 3, n), preferred_element_type=jnp.float32
        ).astype(jnp.bfloat16)
        for k in range(COLS // HEAD_DIM):
            first = 2 * n * COLS + 2 * k * HEAD_DIM
            values[:, first : first + HEAD_DIM] = made[:, k * HEAD_DIM : (k + 1) * HEAD_DIM]

    scale = HEAD_DIM**-0.5 * 1.4426950408889634

    @pl.loop(0, HEADS // 2)
    def _(pair):
        for at, (start, size) in enumerate(blocks):
            span = size + 2 * WINDOW
            for side in range(2):
                head = 2 * pair + side
                lanes = pl.ds(pl.multiple_of(head * HEAD_DIM, HEAD_DIM), HEAD_DIM)
                wide = pl.ds(pl.multiple_of(head * 2 * HEAD_DIM, 2 * HEAD_DIM), 2 * HEAD_DIM)
                scores = lax.dot_general(
                    queries[start : start + size, lanes],
                    keys[start : start + span, lanes],
                    (((1,), (1,)), ((), ())),
                    preferred_element_type=jnp.float32,
                )
                scores = scores * scale + biases[at, 0:size, 0:span]
                exped = jnp.exp2(scores - jnp.max(scores, axis=-1, keepdims=True))
                mixed = jnp.dot(
                    exped.astype(jnp.bfloat16),
                    values[start : start + span, wide],
                    preferred_element_type=jnp.float32,
                )
                context[start : start + size, lanes] = (
                    mixed[:, :HEAD_DIM] / mixed[:, HEAD_DIM:]
                ).astype(jnp.bfloat16)

    hidden_copy.wait()
    late_copies[0].wait()
    gain_c = gain_conv_ref[...]
    half = rows_mid // 2
    for r in range(2):
        rows = slice(r * half, (r + 1) * half)
        for n in range(WIDTH // COLS):
            attended[rows, n * COLS : (n + 1) * COLS] += jnp.dot(
                context[rows, :], columns(late_w, 0, 4, n), preferred_element_type=jnp.float32
            )
        queries[rows, :] = layer_norm(attended[rows, :], gain_c).astype(jnp.bfloat16)

    late_copies[1].wait()
    late_copies[2].wait()
    for n in range(WIDTH // COLS):
        value = jnp.dot(queries[...], columns(late_w, 1, 4, n), preferred_element_type=jnp.float32)
        gate = jnp.dot(queries[...], columns(late_w, 2, 4, n), preferred_element_type=jnp.float32)
        made = (value * jax.nn.sigmoid(gate)).astype(jnp.bfloat16).astype(jnp.float32)
        for j in range(COLS // HEAD_DIM):
            at = n * (COLS // HEAD_DIM) + j
            gated[at] = made[:, j * HEAD_DIM : (j + 1) * HEAD_DIM]
            lanes = slice(at * HEAD_DIM, (at + 1) * HEAD_DIM)
            total = jnp.zeros((tokens, HEAD_DIM), jnp.float32)
            for k in range(KERNEL):
                begin = EDGE - KERNEL // 2 + k
                tap = gated[at, begin : begin + tokens, :] * depth_ref[k : k + 1, lanes]
                total = total + (tap if k == KERNEL // 2 else tap * masks[k])
            context[0:tokens, lanes] = (total * jax.nn.sigmoid(total)).astype(jnp.bfloat16)

    late_copies[3].wait()
    gain_o = gain_out_ref[...]
    half = tokens // 2
    for r in range(2):
        rows = slice(r * half, (r + 1) * half)
        mid = slice(EDGE + r * half, EDGE + (r + 1) * half)
        for n in range(WIDTH // COLS):
            attended[mid, n * COLS : (n + 1) * COLS] += jnp.dot(
                context[rows, :], columns(late_w, 3, 4, n), preferred_element_type=jnp.float32
            )
        out_ref[rows, :] = layer_norm(attended[mid, :], gain_o).astype(jnp.bfloat16)


def conformer_block(info, hidden, normed, weights, gain_conv, w_depth, gain_out, limit):
    rows_all = normed.shape[0]
    rows_mid = hidden.shape[0]
    tokens = rows_mid - 2 * EDGE
    whole = pl.BlockSpec(memory_space=pltpu.VMEM)
    far = pl.BlockSpec(memory_space=pltpu.HBM)
    flops = 2 * rows_all * WIDTH * 2 * WIDTH + 2 * rows_mid * WIDTH * WIDTH * 5
    return pl.pallas_call(
        functools.partial(block_kernel, tokens, limit),
        out_shape=jax.ShapeDtypeStruct((tokens, WIDTH), jnp.bfloat16),
        in_specs=[pl.BlockSpec(memory_space=pltpu.SMEM)] + [whole] * 4 + [far] * 2,
        out_specs=whole,
        scratch_shapes=[
            pltpu.VMEM((32, 3 * WIDTH // 32, WIDTH), jnp.bfloat16),
            pltpu.VMEM((32, 4 * WIDTH // 32, WIDTH), jnp.bfloat16),
            pltpu.VMEM((rows_all, WIDTH), jnp.bfloat16),
            pltpu.VMEM((rows_all, 2 * WIDTH), jnp.bfloat16),
            pltpu.VMEM((rows_mid, WIDTH), jnp.bfloat16),
            pltpu.VMEM((rows_mid, WIDTH), jnp.bfloat16),
            pltpu.VMEM((rows_mid, WIDTH), jnp.float32),
            pltpu.VMEM((WIDTH // HEAD_DIM, rows_mid, HEAD_DIM), jnp.float32),
            pltpu.VMEM((KERNEL, tokens, HEAD_DIM), jnp.float32),
            pltpu.VMEM((4, 128 + EDGE, 512), jnp.float32),
            pltpu.SemaphoreType.DMA((8,)),
        ],
        compiler_params=pltpu.CompilerParams(vmem_limit_bytes=60 * 1024 * 1024),
        cost_estimate=pl.CostEstimate(flops=1024, bytes_accessed=1024, transcendentals=0),
        name="conformer_block",
    )(info, normed, gain_conv, w_depth, gain_out, hidden, weights)


def on_device(
    mel_frames,
    lengths,
    w_first,
    w_second,
    w_proj,
    gain_attn,
    w_qkv,
    w_out,
    gain_conv,
    w_point_in,
    w_depth,
    w_point_out,
    gain_out,
):
    tokens = mel_frames.shape[1] // 4
    limit = mel_frames.shape[1] * lax.axis_size("tm")
    base = lax.axis_index("tm") * mel_frames.shape[1]
    info = jnp.concatenate(
        [
            jnp.reshape(base, (1,)),
            lengths[0],
            jnp.stack([lax.axis_index("rec"), lax.axis_index("tm")]),
            jnp.full((1,), lax.axis_size("tm"), jnp.int32),
        ]
    ).astype(jnp.int32)

    def gather_packed(packed, share):
        full = lax.all_gather(packed, ("rec", "tm"), axis=0, tiled=False)
        if full.shape[0] == 32:
            return full
        parts = packed.shape[0] // share
        full = full.reshape(full.shape[0], parts, -1, WIDTH).transpose(1, 0, 2, 3)
        full = full.reshape(parts, 32, -1, WIDTH).transpose(1, 0, 2, 3)
        return full.reshape(32, -1, WIDTH)

    packed = pack([w_qkv, w_out, w_point_in, w_point_out])
    late = gather_packed(packed, w_out.shape[0])
    if lax.axis_size("rec") == 4 and lax.axis_size("tm") == 8:
        proj = along_rec(behind(w_proj, packed))
        low, high = mel_halos(behind(mel_frames[0], packed))
        patches, taps = prepare(info, mel_frames[0], low, high, w_first, tokens, limit)
        w_second_all, rounds = gather_ordered(behind(w_second, patches, *proj))
        proj = behind(tuple(proj), patches, *rounds[0])
        proj = to_neighbours(jnp.concatenate(proj, axis=0))
        subs = subsample(patches, taps, w_second_all)
        proj_late = relayed(*behind(proj, *subs))
        proj, places = to_other_core(*proj, *proj_late)
    else:
        low, high = mel_halos(mel_frames[0])
        patches, taps = prepare(info, mel_frames[0], low, high, w_first, tokens, limit)
        w_second_all = gather_ordered(w_second)[0]
        subs = subsample(patches, taps, w_second_all)
        proj, places = [lax.all_gather(w_proj, ("rec", "tm"), axis=0, tiled=True)], None
    hidden, normed = project(info, gain_attn[None], subs, proj, places, tokens)
    encoded = conformer_block(
        info,
        hidden,
        normed,
        late,
        gain_conv[None],
        w_depth,
        gain_out[None],
        limit,
    )
    return encoded[None]


def solution(mesh):
    placed = (
        P("rec", "tm", None),
        P("rec", None),
        P(),
        P(("rec", "tm"), None),
        P(("rec", "tm"), None),
        P(),
        P(("rec", "tm"), None),
        P(("rec", "tm"), None),
        P(),
        P(("rec", "tm"), None),
        P(),
        P(("rec", "tm"), None),
        P(),
    )
    return jax.shard_map(
        on_device, mesh=mesh, in_specs=placed, out_specs=P("rec", "tm", None), check_vma=False
    )
```

```python
import functools

import jax
import jax.numpy as jnp
import numpy as np
from jax import lax
from jax.experimental import pallas as pl
from jax.experimental.pallas import tpu as pltpu
from jax.sharding import PartitionSpec as P

WIDTH = 1024
HEADS = 8
HEAD_DIM = 128
KERNEL = 9
WINDOW = 128
CHANNELS = 256
NORM_EPSILON = 1e-05

EDGE = 16
HALO = WINDOW + EDGE
COLS = 256


def segment_of(positions, lengths, limit):
    counted = jnp.zeros(positions.shape, jnp.int32)
    bound = 0
    for k in range(len(lengths) - 1):
        bound = bound + lengths[k]
        counted = counted + (positions >= bound).astype(jnp.int32)
    return jnp.where((positions >= 0) & (positions < limit), counted, -1)


def layer_norm(values, gain):
    row_mean = jnp.mean(values, axis=-1, keepdims=True)
    centred = values - row_mean
    variance = jnp.mean(centred * centred, axis=-1, keepdims=True)
    return centred * lax.rsqrt(variance + NORM_EPSILON) * gain


def exchange(block, axis, distance):
    size = lax.axis_size(axis)
    return lax.ppermute(block, axis, [(i, i ^ distance) for i in range(size)])


def bit_groups():
    groups = []
    for axis, lowest in (("rec", 1), ("tm", 2)):
        bits = []
        bit = lowest
        while bit < lax.axis_size(axis):
            bits.append(bit)
            bit *= 2
        groups += [(axis, bits[k : k + 2]) for k in range(0, len(bits), 2)]
    return groups + [("tm", [1])]


def distances(bits):
    return [0] + [bits[0]] if len(bits) == 1 else [0, bits[0], bits[1], bits[0] + bits[1]]


def can_exchange():
    return all(
        lax.axis_size(axis) & (lax.axis_size(axis) - 1) == 0 and lax.axis_size(axis) > 1
        for axis in ("rec", "tm")
    )


def behind(value, *others):
    return lax.optimization_barrier((value, *others))[0]


def gather_ordered(block, joined=None, hold=None):
    if not can_exchange():
        return lax.all_gather(block, ("rec", "tm"), axis=0, tiled=True)
    names = []
    held = block[None]
    for axis, bits in bit_groups():
        if joined is not None and axis == "rec":
            got = [piece[-32:-8, : 3 * CHANNELS][None] for piece in joined]
        else:
            got = [held] + [exchange(held, axis, d) for d in distances(bits)[1:]]
        if hold is not None and axis == "tm" and bits[0] > 1:
            got = list(behind(tuple(got), hold))
        me = lax.axis_index(axis)
        for at, bit in enumerate(bits):
            high = (me & bit) != 0
            got = [jnp.where(high, got[k ^ (1 << at)], got[k]) for k in range(len(got))]
        held = jnp.concatenate(got, axis=0)
        if joined is not None and axis == "rec":
            held = held.reshape(-1, 24, 3, CHANNELS).transpose(0, 2, 1, 3)
            held = held.reshape((-1,) + block.shape)
        names = [(axis, bit) for bit in reversed(bits)] + names
    wanted = []
    for axis in ("rec", "tm"):
        wanted += sorted((n for n in names if n[0] == axis), key=lambda n: -n[1])
    order = [names.index(n) for n in wanted]
    dims = held.reshape((2,) * len(names) + block.shape)
    dims = jnp.transpose(dims, order + [len(names), len(names) + 1])
    return dims.reshape((-1,) + block.shape[1:])


def along_rec(block):
    return [block] + [exchange(block, "rec", d) for d in (1, 2, 3)]


def to_neighbours(held):
    return held, exchange(held, "tm", 2), exchange(held, "tm", 4)


def relayed(held, beside, above):
    half = held.shape[0] // 2
    return exchange(beside[:half], "tm", 4), exchange(above[half:], "tm", 2)


def to_other_core(held, beside, above, low, high):
    pieces = [(held, 0, 0, 4), (beside, 2, 0, 4), (above, 4, 0, 4), (low, 6, 0, 2), (high, 6, 2, 2)]
    pieces += [(exchange(p, "tm", 1), far ^ 1, slot, n) for p, far, slot, n in pieces]
    return [p[0] for p in pieces], [p[1:] for p in pieces]


def copies_in(info_ref, sources, places, target, sem):
    if places is None:
        pltpu.make_async_copy(sources[0], target, sem).start()
        return
    rec, tm, tm_size = info_ref[5], info_ref[6], info_ref[7]
    for source, (far, first, number) in zip(sources, places):
        rows = source.shape[0] // number
        for slot in range(number):
            owner = (rec ^ (first + slot)) * tm_size + (tm ^ far)
            if len(target.shape) == 3:
                place = target.at[owner]
            else:
                place = target.at[pl.ds(pl.multiple_of(owner * rows, 16), rows), :]
            pltpu.make_async_copy(source.at[pl.ds(slot * rows, rows), :], place, sem).start()


BINS = 41


def prepare_kernel(limit, info_ref, quads_ref, lane_ref, w_ref, patches_ref, taps_ref):
    base = info_ref[0]
    lengths = [info_ref[1 + k] for k in range(4)]
    tokens = quads_ref.shape[0]
    wide = quads_ref.shape[1]
    source = lax.broadcasted_iota(jnp.int32, (wide, COLS), 0)
    token = lax.broadcasted_iota(jnp.int32, (tokens, COLS), 0)
    own = segment_of(base + 4 * (token - HALO), lengths, limit)
    frame = lane_ref[6:7, :]
    for a in range(3):
        middle = segment_of(base + 4 * (token - HALO) + 2 * a - 2, lengths, limit)
        there = segment_of(base + 4 * (token - HALO) + 2 * a - 3 + frame, lengths, limit)
        same = (middle == own) & (there == middle)
        for h in range(2):
            chosen = (source == lane_ref[2 * a + h : 2 * a + h + 1, :]).astype(jnp.float32)
            made = jnp.dot(
                quads_ref[...], chosen.astype(jnp.bfloat16), preferred_element_type=jnp.float32
            )
            patches_ref[a, h] = jnp.where(same, made, 0.0).astype(jnp.bfloat16)

    row = lax.broadcasted_iota(jnp.int32, (COLS, CHANNELS), 0)
    group = jnp.zeros((COLS, CHANNELS), jnp.int32)
    for k in range(1, 7):
        group = group + (row >= BINS * k).astype(jnp.int32)
    at_bin = row - BINS * group
    spread = []
    for b in range(3):
        total = jnp.zeros((COLS, CHANNELS), jnp.float32)
        for a in range(3):
            tap = w_ref[3 * a + b : 3 * a + b + 1, :]
            high = tap.astype(jnp.bfloat16).astype(jnp.float32)
            total = jnp.where(group == a, high, total)
            total = jnp.where(group == 3 + a, tap - high, total)
        spread.append(total)
    for f in range(20):
        total = jnp.zeros((COLS, CHANNELS), jnp.float32)
        for b in range(3):
            total = jnp.where(at_bin == 2 * f + b, spread[b], total)
        taps_ref[:, f * CHANNELS : (f + 1) * CHANNELS] = total.astype(jnp.bfloat16)


def mel_halos(mel):
    reach = 4 * (HALO + EDGE)
    tm = lax.axis_size("tm")
    forward = [(i, i + 1) for i in range(tm - 1)]
    backward = [(i + 1, i) for i in range(tm - 1)]
    low = lax.ppermute(mel[mel.shape[0] - reach :], "tm", forward)
    return low, lax.ppermute(mel[:reach], "tm", backward)


def prepare(info, mel, low, high, w_first, tokens, limit):
    bins = mel.shape[1]
    quads = jnp.concatenate([low, mel, high], axis=0).reshape(-1, 4 * bins)
    count = tokens + 2 * HALO
    quads = jnp.concatenate(
        [quads[EDGE - 1 : EDGE - 1 + count], quads[EDGE : EDGE + count]], axis=1
    )
    lane = np.arange(COLS)
    frame, at_bin = lane // BINS % 3, lane % BINS
    used = lane < 6 * BINS
    picks = np.full((8, COLS), -1, np.int32)
    for a in range(3):
        for h in range(2):
            wanted = at_bin - 1 + 40 * h
            place = bins * (2 * a + frame + 1) + wanted
            picks[2 * a + h] = np.where(used & (wanted >= 0), place, -1)
    picks[6] = frame
    whole = pl.BlockSpec(memory_space=pltpu.VMEM)
    return pl.pallas_call(
        functools.partial(prepare_kernel, limit),
        out_shape=(
            jax.ShapeDtypeStruct((3, 2, count, COLS), jnp.bfloat16),
            jax.ShapeDtypeStruct((COLS, 20 * CHANNELS), jnp.bfloat16),
        ),
        in_specs=[pl.BlockSpec(memory_space=pltpu.SMEM)] + [whole] * 3,
        out_specs=(whole, whole),
        compiler_params=pltpu.CompilerParams(vmem_limit_bytes=24 * 1024 * 1024),
        cost_estimate=pl.CostEstimate(flops=1024, bytes_accessed=1024, transcendentals=0),
        name="prepare",
    )(info, quads, jnp.asarray(picks), w_first.reshape(9, CHANNELS))


def conv_kernel(begin, count, a_ref, b_ref, w_ref, out_ref, first):
    tokens = out_ref.shape[0]
    rows_step = tokens // 2

    @pl.loop(0, 2)
    def _(r):
        rows = pl.ds(pl.multiple_of(r * rows_step, 16), rows_step)
        for a in range(3):
            for i in range(2 * count + 1):
                at = 2 * begin - 1 + i
                place = slice(i * COLS, (i + 1) * COLS)
                if at < 0:
                    first[a, :, place] = jnp.zeros((rows_step, COLS), jnp.bfloat16)
                    continue
                half, col = divmod(at, 20)
                made = jnp.dot(
                    a_ref[a, half, rows, :],
                    b_ref[:, col * COLS : (col + 1) * COLS],
                    preferred_element_type=jnp.float32,
                )
                first[a, :, place] = jnp.maximum(made, 0.0).astype(jnp.bfloat16)
        for t in range(count):
            total = None
            for a in range(3):
                made = jnp.dot(
                    first[a, :, 2 * t * COLS : (2 * t + 3) * COLS],
                    w_ref[a],
                    preferred_element_type=jnp.float32,
                )
                total = made if total is None else total + made
            out_ref[rows, t * COLS : (t + 1) * COLS] = jnp.maximum(total, 0.0).astype(jnp.bfloat16)


def subsample(patches, taps, w_second):
    tokens = patches.shape[2]
    count = 4
    weights = w_second.reshape(3, 3 * COLS, COLS)
    whole = pl.BlockSpec(memory_space=pltpu.VMEM)
    flops = 2 * tokens * COLS * COLS * (3 * (2 * count + 1) + 9 * count)
    pieces = []
    for begin in range(0, 20, count):
        pieces.append(
            pl.pallas_call(
                functools.partial(conv_kernel, begin, count),
                out_shape=jax.ShapeDtypeStruct((tokens, count * CHANNELS), jnp.bfloat16),
                in_specs=[whole] * 3,
                out_specs=whole,
                scratch_shapes=[
                    pltpu.VMEM((3, tokens // 2, (2 * count + 1) * COLS), jnp.bfloat16)
                ],
                compiler_params=pltpu.CompilerParams(vmem_limit_bytes=20 * 1024 * 1024),
                cost_estimate=pl.CostEstimate(flops=1024, bytes_accessed=1024, transcendentals=0),
                name="subsample",
            )(patches, taps, weights)
        )
    return pieces


def project_kernel(places, info_ref, gain_ref, *rest):
    subs = rest[:5]
    sources = rest[5:-5]
    mid_ref, normed_ref, weights, hidden, sem = rest[-5:]
    copies_in(info_ref, sources, places, weights, sem)
    pltpu.make_async_copy(weights, weights, sem).wait()

    depth = weights.shape[0] // len(subs)

    @pl.loop(0, WIDTH // COLS)
    def _(n):
        here = pl.ds(pl.multiple_of(n * COLS, COLS), COLS)
        total = None
        for piece, sub in enumerate(subs):
            made = jnp.dot(
                sub[...],
                weights[piece * depth : (piece + 1) * depth, here],
                preferred_element_type=jnp.float32,
            )
            total = made if total is None else total + made
        hidden[:, here] = total

    gain = gain_ref[...]
    chunk = 160

    @pl.loop(0, hidden.shape[0] // chunk)
    def _(r):
        rows = pl.ds(pl.multiple_of(r * chunk, chunk), chunk)
        normed_ref[rows, :] = layer_norm(hidden[rows, :], gain).astype(jnp.bfloat16)

    mid_ref[...] = hidden[WINDOW : WINDOW + mid_ref.shape[0], :]


def project(info, gain, subs, sources, places, tokens):
    rows_all = tokens + 2 * HALO
    rows_mid = tokens + 2 * EDGE
    whole = pl.BlockSpec(memory_space=pltpu.VMEM)
    depth = sum(sub.shape[1] for sub in subs)
    return pl.pallas_call(
        functools.partial(project_kernel, places),
        out_shape=(
            jax.ShapeDtypeStruct((rows_mid, WIDTH), jnp.float32),
            jax.ShapeDtypeStruct((rows_all, WIDTH), jnp.bfloat16),
        ),
        in_specs=[pl.BlockSpec(memory_space=pltpu.SMEM)]
        + [whole] * 6
        + [pl.BlockSpec(memory_space=pl.ANY)] * len(sources),
        out_specs=(whole, whole),
        scratch_shapes=[
            pltpu.VMEM((depth, WIDTH), jnp.bfloat16),
            pltpu.VMEM((rows_all, WIDTH), jnp.float32),
            pltpu.SemaphoreType.DMA(()),
        ],
        compiler_params=pltpu.CompilerParams(vmem_limit_bytes=34 * 1024 * 1024),
        cost_estimate=pl.CostEstimate(flops=1024, bytes_accessed=1024, transcendentals=0),
        name="project",
    )(info, gain, *subs, *sources)


def join_kernel(proj_ref, second_ref, out_ref):
    rows = proj_ref.shape[0]
    out_ref[0:rows, :] = proj_ref[...]
    second = second_ref[...].astype(jnp.float32)
    spare = jnp.zeros((8, CHANNELS), jnp.float32)
    for k in range(3):
        part = jnp.concatenate([second[24 * k : 24 * k + 24], spare], axis=0)
        out_ref[rows : rows + 32, k * CHANNELS : (k + 1) * CHANNELS] = part.astype(jnp.bfloat16)
    out_ref[rows : rows + 32, 3 * CHANNELS :] = jnp.zeros(
        (32, WIDTH - 3 * CHANNELS), jnp.bfloat16
    )


def join(w_proj, w_second):
    whole = pl.BlockSpec(memory_space=pltpu.VMEM)
    rows = w_proj.shape[0] + 32
    return pl.pallas_call(
        join_kernel,
        out_shape=jax.ShapeDtypeStruct((rows, WIDTH), jnp.bfloat16),
        in_specs=[whole] * 2,
        out_specs=whole,
        compiler_params=pltpu.CompilerParams(vmem_limit_bytes=60 * 1024 * 1024),
        cost_estimate=pl.CostEstimate(flops=1024, bytes_accessed=1024, transcendentals=0),
        name="join",
    )(w_proj, w_second)


def pack_kernel(pieces, *refs):
    *sources, out_ref, held, sems = refs
    at = 0
    copies = []
    for source, first in pieces:
        rows = sources[source].shape[0]
        copies.append(
            pltpu.make_async_copy(
                sources[source].at[:, pl.ds(first, WIDTH)],
                held.at[pl.ds(at, rows), :],
                sems.at[len(copies)],
            )
        )
        at += rows
    for copy in copies:
        copy.start()
    for copy in copies:
        copy.wait()
    out = pltpu.make_async_copy(held, out_ref, sems.at[len(copies)])
    out.start()
    out.wait()


def pack(arrays):
    pieces = [
        (k, first) for k, array in enumerate(arrays) for first in range(0, array.shape[1], WIDTH)
    ]
    if any(array.shape[0] % 16 for array in arrays):
        return jnp.concatenate([arrays[k][:, c : c + WIDTH] for k, c in pieces], axis=0)
    rows = sum(arrays[k].shape[0] for k, _ in pieces)
    far = pl.BlockSpec(memory_space=pltpu.HBM)
    return pl.pallas_call(
        functools.partial(pack_kernel, pieces),
        out_shape=jax.ShapeDtypeStruct((rows, WIDTH), jnp.bfloat16),
        in_specs=[far] * len(arrays),
        out_specs=far,
        scratch_shapes=[
            pltpu.VMEM((rows, WIDTH), jnp.bfloat16),
            pltpu.SemaphoreType.DMA((len(pieces) + 1,)),
        ],
        compiler_params=pltpu.CompilerParams(vmem_limit_bytes=60 * 1024 * 1024),
        cost_estimate=pl.CostEstimate(flops=1024, bytes_accessed=1024, transcendentals=0),
        name="pack",
    )(*arrays)


def columns(weights, part, parts, n):
    rows = weights.shape[1] // parts
    return weights[:, part * rows : (part + 1) * rows, n * COLS : (n + 1) * COLS].reshape(-1, COLS)


def block_kernel(
    tokens,
    limit,
    info_ref,
    normed_ref,
    gain_conv_ref,
    depth_ref,
    gain_out_ref,
    hidden_ref,
    weights_ref,
    out_ref,
    early_w,
    late_w,
    keys,
    values,
    queries,
    context,
    attended,
    gated,
    masks,
    biases,
    sems,
):
    rows_mid = tokens + 2 * EDGE
    share = early_w.shape[1] // 3
    early_copies = []
    for k in range(3):
        part = pl.ds(k * share, share)
        early_copies.append(
            pltpu.make_async_copy(
                weights_ref.at[:, part, :], early_w.at[:, part, :], sems.at[k]
            )
        )
    late_copies = []
    for k in range(4):
        late_copies.append(
            pltpu.make_async_copy(
                weights_ref.at[:, pl.ds((3 + k) * share, share), :],
                late_w.at[:, pl.ds(k * share, share), :],
                sems.at[3 + k],
            )
        )
    hidden_copy = pltpu.make_async_copy(hidden_ref, attended, sems.at[7])
    for copy in early_copies:
        copy.start()
    base = info_ref[0]
    lengths = [info_ref[1 + k] for k in range(4)]

    blocks = []
    at_row = 0
    while at_row < rows_mid:
        size = 128 + (EDGE if at_row == 0 or at_row + 128 + EDGE == rows_mid else 0)
        blocks.append((at_row, size))
        at_row += size

    for at, (start, size) in enumerate(blocks):
        span = size + 2 * WINDOW
        q_row = lax.broadcasted_iota(jnp.int32, (size, 1), 0)
        k_row = lax.broadcasted_iota(jnp.int32, (1, span), 1)
        q_seg = segment_of(base + 4 * (q_row + start - EDGE), lengths, limit)
        k_seg = segment_of(base + 4 * (k_row + start - HALO), lengths, limit)
        apart = k_row - q_row
        allowed = (apart >= 0) & (apart <= 2 * WINDOW) & (q_seg == k_seg)
        biases[at, 0:size, 0:span] = jnp.where(allowed, 0.0, -1e30)
    for head in range(HEADS):
        values[:, (2 * head + 1) * HEAD_DIM : (2 * head + 2) * HEAD_DIM] = jnp.ones(
            (values.shape[0], HEAD_DIM), jnp.bfloat16
        )

    early_copies[0].wait()
    hidden_copy.start()
    for copy in late_copies:
        copy.start()
    for n in range(WIDTH // COLS):
        queries[:, n * COLS : (n + 1) * COLS] = jnp.dot(
            normed_ref[WINDOW : WINDOW + rows_mid, :],
            columns(early_w, 0, 3, n),
            preferred_element_type=jnp.float32,
        ).astype(jnp.bfloat16)
    row = lax.broadcasted_iota(jnp.int32, (tokens, HEAD_DIM), 0)
    own = segment_of(base + 4 * row, lengths, limit)
    for k in range(KERNEL):
        there = segment_of(base + 4 * (row + k - KERNEL // 2), lengths, limit)
        masks[k] = (there == own).astype(jnp.float32)
    early_copies[1].wait()
    for n in range(WIDTH // COLS):
        keys[:, n * COLS : (n + 1) * COLS] = jnp.dot(
            normed_ref[...], columns(early_w, 1, 3, n), preferred_element_type=jnp.float32
        ).astype(jnp.bfloat16)
    early_copies[2].wait()
    for n in range(WIDTH // COLS):
        made = jnp.dot(
            normed_ref[...], columns(early_w, 2, 3, n), preferred_element_type=jnp.float32
        ).astype(jnp.bfloat16)
        for k in range(COLS // HEAD_DIM):
            first = 2 * n * COLS + 2 * k * HEAD_DIM
            values[:, first : first + HEAD_DIM] = made[:, k * HEAD_DIM : (k + 1) * HEAD_DIM]

    scale = HEAD_DIM**-0.5 * 1.4426950408889634

    @pl.loop(0, HEADS // 2)
    def _(pair):
        for at, (start, size) in enumerate(blocks):
            span = size + 2 * WINDOW
            for side in range(2):
                head = 2 * pair + side
                lanes = pl.ds(pl.multiple_of(head * HEAD_DIM, HEAD_DIM), HEAD_DIM)
                wide = pl.ds(pl.multiple_of(head * 2 * HEAD_DIM, 2 * HEAD_DIM), 2 * HEAD_DIM)
                scores = lax.dot_general(
                    queries[start : start + size, lanes],
                    keys[start : start + span, lanes],
                    (((1,), (1,)), ((), ())),
                    preferred_element_type=jnp.float32,
                )
                scores = scores * scale + biases[at, 0:size, 0:span]
                exped = jnp.exp2(scores - jnp.max(scores, axis=-1, keepdims=True))
                mixed = jnp.dot(
                    exped.astype(jnp.bfloat16),
                    values[start : start + span, wide],
                    preferred_element_type=jnp.float32,
                )
                context[start : start + size, lanes] = (
                    mixed[:, :HEAD_DIM] / mixed[:, HEAD_DIM:]
                ).astype(jnp.bfloat16)

    hidden_copy.wait()
    late_copies[0].wait()
    gain_c = gain_conv_ref[...]
    half = rows_mid // 2
    for r in range(2):
        rows = slice(r * half, (r + 1) * half)
        for n in range(WIDTH // COLS):
            attended[rows, n * COLS : (n + 1) * COLS] += jnp.dot(
                context[rows, :], columns(late_w, 0, 4, n), preferred_element_type=jnp.float32
            )
        queries[rows, :] = layer_norm(attended[rows, :], gain_c).astype(jnp.bfloat16)

    late_copies[1].wait()
    late_copies[2].wait()
    for n in range(WIDTH // COLS):
        value = jnp.dot(queries[...], columns(late_w, 1, 4, n), preferred_element_type=jnp.float32)
        gate = jnp.dot(queries[...], columns(late_w, 2, 4, n), preferred_element_type=jnp.float32)
        made = (value * jax.nn.sigmoid(gate)).astype(jnp.bfloat16).astype(jnp.float32)
        for j in range(COLS // HEAD_DIM):
            at = n * (COLS // HEAD_DIM) + j
            gated[at] = made[:, j * HEAD_DIM : (j + 1) * HEAD_DIM]
            lanes = slice(at * HEAD_DIM, (at + 1) * HEAD_DIM)
            total = jnp.zeros((tokens, HEAD_DIM), jnp.float32)
            for k in range(KERNEL):
                begin = EDGE - KERNEL // 2 + k
                tap = gated[at, begin : begin + tokens, :] * depth_ref[k : k + 1, lanes]
                total = total + (tap if k == KERNEL // 2 else tap * masks[k])
            context[0:tokens, lanes] = (total * jax.nn.sigmoid(total)).astype(jnp.bfloat16)

    late_copies[3].wait()
    gain_o = gain_out_ref[...]
    half = tokens // 2
    for r in range(2):
        rows = slice(r * half, (r + 1) * half)
        mid = slice(EDGE + r * half, EDGE + (r + 1) * half)
        for n in range(WIDTH // COLS):
            attended[mid, n * COLS : (n + 1) * COLS] += jnp.dot(
                context[rows, :], columns(late_w, 3, 4, n), preferred_element_type=jnp.float32
            )
        out_ref[rows, :] = layer_norm(attended[mid, :], gain_o).astype(jnp.bfloat16)


def conformer_block(info, hidden, normed, weights, gain_conv, w_depth, gain_out, limit):
    rows_all = normed.shape[0]
    rows_mid = hidden.shape[0]
    tokens = rows_mid - 2 * EDGE
    whole = pl.BlockSpec(memory_space=pltpu.VMEM)
    far = pl.BlockSpec(memory_space=pltpu.HBM)
    flops = 2 * rows_all * WIDTH * 2 * WIDTH + 2 * rows_mid * WIDTH * WIDTH * 5
    return pl.pallas_call(
        functools.partial(block_kernel, tokens, limit),
        out_shape=jax.ShapeDtypeStruct((tokens, WIDTH), jnp.bfloat16),
        in_specs=[pl.BlockSpec(memory_space=pltpu.SMEM)] + [whole] * 4 + [far] * 2,
        out_specs=whole,
        scratch_shapes=[
            pltpu.VMEM((32, 3 * WIDTH // 32, WIDTH), jnp.bfloat16),
            pltpu.VMEM((32, 4 * WIDTH // 32, WIDTH), jnp.bfloat16),
            pltpu.VMEM((rows_all, WIDTH), jnp.bfloat16),
            pltpu.VMEM((rows_all, 2 * WIDTH), jnp.bfloat16),
            pltpu.VMEM((rows_mid, WIDTH), jnp.bfloat16),
            pltpu.VMEM((rows_mid, WIDTH), jnp.bfloat16),
            pltpu.VMEM((rows_mid, WIDTH), jnp.float32),
            pltpu.VMEM((WIDTH // HEAD_DIM, rows_mid, HEAD_DIM), jnp.float32),
            pltpu.VMEM((KERNEL, tokens, HEAD_DIM), jnp.float32),
            pltpu.VMEM((4, 128 + EDGE, 512), jnp.float32),
            pltpu.SemaphoreType.DMA((8,)),
        ],
        compiler_params=pltpu.CompilerParams(vmem_limit_bytes=60 * 1024 * 1024),
        cost_estimate=pl.CostEstimate(flops=1024, bytes_accessed=1024, transcendentals=0),
        name="conformer_block",
    )(info, normed, gain_conv, w_depth, gain_out, hidden, weights)


def on_device(
    mel_frames,
    lengths,
    w_first,
    w_second,
    w_proj,
    gain_attn,
    w_qkv,
    w_out,
    gain_conv,
    w_point_in,
    w_depth,
    w_point_out,
    gain_out,
):
    tokens = mel_frames.shape[1] // 4
    limit = mel_frames.shape[1] * lax.axis_size("tm")
    base = lax.axis_index("tm") * mel_frames.shape[1]
    info = jnp.concatenate(
        [
            jnp.reshape(base, (1,)),
            lengths[0],
            jnp.stack([lax.axis_index("rec"), lax.axis_index("tm")]),
            jnp.full((1,), lax.axis_size("tm"), jnp.int32),
        ]
    ).astype(jnp.int32)

    def gather_packed(packed, share):
        full = lax.all_gather(packed, ("rec", "tm"), axis=0, tiled=False)
        if full.shape[0] == 32:
            return full
        parts = packed.shape[0] // share
        full = full.reshape(full.shape[0], parts, -1, WIDTH).transpose(1, 0, 2, 3)
        full = full.reshape(parts, 32, -1, WIDTH).transpose(1, 0, 2, 3)
        return full.reshape(32, -1, WIDTH)

    packed = pack([w_qkv, w_out, w_point_in, w_point_out])
    late = gather_packed(packed, w_out.shape[0])
    if lax.axis_size("rec") == 4 and lax.axis_size("tm") == 8 and w_proj.shape[0] == 160:
        joined = along_rec(join(behind(w_proj, packed), w_second))
        low, high = mel_halos(behind(mel_frames[0], joined[0]))
        patches, taps = prepare(info, mel_frames[0], low, high, w_first, tokens, limit)
        joined = behind(tuple(joined), patches)
        proj = jnp.concatenate([piece[:-32] for piece in joined], axis=0)
        subs = subsample(patches, taps, gather_ordered(w_second, joined, proj))
        proj = to_neighbours(proj)
        proj_late = relayed(*behind(proj, *subs))
        proj, places = to_other_core(*proj, *proj_late)
    else:
        low, high = mel_halos(mel_frames[0])
        patches, taps = prepare(info, mel_frames[0], low, high, w_first, tokens, limit)
        subs = subsample(patches, taps, gather_ordered(w_second))
        proj, places = [lax.all_gather(w_proj, ("rec", "tm"), axis=0, tiled=True)], None
    hidden, normed = project(info, gain_attn[None], subs, proj, places, tokens)
    encoded = conformer_block(
        info,
        hidden,
        normed,
        late,
        gain_conv[None],
        w_depth,
        gain_out[None],
        limit,
    )
    return encoded[None]


def solution(mesh):
    placed = (
        P("rec", "tm", None),
        P("rec", None),
        P(),
        P(("rec", "tm"), None),
        P(("rec", "tm"), None),
        P(),
        P(("rec", "tm"), None),
        P(("rec", "tm"), None),
        P(),
        P(("rec", "tm"), None),
        P(),
        P(("rec", "tm"), None),
        P(),
    )
    return jax.shard_map(
        on_device, mesh=mesh, in_specs=placed, out_specs=P("rec", "tm", None), check_vma=False
    )
```

```python
import functools

import jax
import jax.numpy as jnp
import numpy as np
from jax import lax
from jax.experimental import pallas as pl
from jax.experimental.pallas import tpu as pltpu
from jax.sharding import PartitionSpec as P

WIDTH = 1024
HEADS = 8
HEAD_DIM = 128
KERNEL = 9
WINDOW = 128
CHANNELS = 256
NORM_EPSILON = 1e-05

EDGE = 16
HALO = WINDOW + EDGE
COLS = 256


def segment_of(positions, lengths, limit):
    counted = jnp.zeros(positions.shape, jnp.int32)
    bound = 0
    for k in range(len(lengths) - 1):
        bound = bound + lengths[k]
        counted = counted + (positions >= bound).astype(jnp.int32)
    return jnp.where((positions >= 0) & (positions < limit), counted, -1)


def layer_norm(values, gain):
    row_mean = jnp.mean(values, axis=-1, keepdims=True)
    centred = values - row_mean
    variance = jnp.mean(centred * centred, axis=-1, keepdims=True)
    return centred * lax.rsqrt(variance + NORM_EPSILON) * gain


def exchange(block, axis, distance):
    size = lax.axis_size(axis)
    return lax.ppermute(block, axis, [(i, i ^ distance) for i in range(size)])


def bit_groups():
    groups = []
    for axis, lowest in (("rec", 1), ("tm", 2)):
        bits = []
        bit = lowest
        while bit < lax.axis_size(axis):
            bits.append(bit)
            bit *= 2
        groups += [(axis, bits[k : k + 2]) for k in range(0, len(bits), 2)]
    return groups + [("tm", [1])]


def distances(bits):
    return [0] + [bits[0]] if len(bits) == 1 else [0, bits[0], bits[1], bits[0] + bits[1]]


def can_exchange():
    return all(
        lax.axis_size(axis) & (lax.axis_size(axis) - 1) == 0 and lax.axis_size(axis) > 1
        for axis in ("rec", "tm")
    )


def behind(value, *others):
    return lax.optimization_barrier((value, *others))[0]


def gather_ordered(block):
    if not can_exchange():
        return lax.all_gather(block, ("rec", "tm"), axis=0, tiled=True), []
    names = []
    held = block[None]
    rounds = []
    for axis, bits in bit_groups():
        got = [held] + [exchange(held, axis, d) for d in distances(bits)[1:]]
        rounds.append(got[1:])
        me = lax.axis_index(axis)
        for at, bit in enumerate(bits):
            high = (me & bit) != 0
            got = [jnp.where(high, got[k ^ (1 << at)], got[k]) for k in range(len(got))]
        held = jnp.concatenate(got, axis=0)
        names = [(axis, bit) for bit in reversed(bits)] + names
    wanted = []
    for axis in ("rec", "tm"):
        wanted += sorted((n for n in names if n[0] == axis), key=lambda n: -n[1])
    order = [names.index(n) for n in wanted]
    dims = held.reshape((2,) * len(names) + block.shape)
    dims = jnp.transpose(dims, order + [len(names), len(names) + 1])
    return dims.reshape((-1,) + block.shape[1:]), rounds


def along_rec(block):
    return [block] + [exchange(block, "rec", d) for d in (1, 2, 3)]


def to_neighbours(held):
    return held, exchange(held, "tm", 2), exchange(held, "tm", 4)


def relayed(held, beside, above):
    half = held.shape[0] // 2
    return exchange(beside[:half], "tm", 4), exchange(above[half:], "tm", 2)


def to_other_core(held, beside, above, low, high):
    pieces = [(held, 0, 0, 4), (beside, 2, 0, 4), (above, 4, 0, 4), (low, 6, 0, 2), (high, 6, 2, 2)]
    pieces += [(exchange(p, "tm", 1), far ^ 1, slot, n) for p, far, slot, n in pieces]
    return [p[0] for p in pieces], [p[1:] for p in pieces]


def copies_in(info_ref, sources, places, target, sem):
    if places is None:
        pltpu.make_async_copy(sources[0], target, sem).start()
        return
    rec, tm, tm_size = info_ref[5], info_ref[6], info_ref[7]
    for source, (far, first, number) in zip(sources, places):
        rows = source.shape[0] // number
        for slot in range(number):
            owner = (rec ^ (first + slot)) * tm_size + (tm ^ far)
            if len(target.shape) == 3:
                place = target.at[owner]
            else:
                place = target.at[pl.ds(pl.multiple_of(owner * rows, 16), rows), :]
            pltpu.make_async_copy(source.at[pl.ds(slot * rows, rows), :], place, sem).start()


BINS = 41


def prepare_kernel(limit, info_ref, quads_ref, lane_ref, w_ref, patches_ref, taps_ref):
    base = info_ref[0]
    lengths = [info_ref[1 + k] for k in range(4)]
    tokens = quads_ref.shape[0]
    wide = quads_ref.shape[1]
    source = lax.broadcasted_iota(jnp.int32, (wide, COLS), 0)
    token = lax.broadcasted_iota(jnp.int32, (tokens, COLS), 0)
    own = segment_of(base + 4 * (token - HALO), lengths, limit)
    frame = lane_ref[6:7, :]
    for a in range(3):
        middle = segment_of(base + 4 * (token - HALO) + 2 * a - 2, lengths, limit)
        there = segment_of(base + 4 * (token - HALO) + 2 * a - 3 + frame, lengths, limit)
        same = (middle == own) & (there == middle)
        for h in range(2):
            chosen = (source == lane_ref[2 * a + h : 2 * a + h + 1, :]).astype(jnp.float32)
            made = jnp.dot(
                quads_ref[...], chosen.astype(jnp.bfloat16), preferred_element_type=jnp.float32
            )
            patches_ref[a, h] = jnp.where(same, made, 0.0).astype(jnp.bfloat16)

    row = lax.broadcasted_iota(jnp.int32, (COLS, CHANNELS), 0)
    group = jnp.zeros((COLS, CHANNELS), jnp.int32)
    for k in range(1, 7):
        group = group + (row >= BINS * k).astype(jnp.int32)
    at_bin = row - BINS * group
    spread = []
    for b in range(3):
        total = jnp.zeros((COLS, CHANNELS), jnp.float32)
        for a in range(3):
            tap = w_ref[3 * a + b : 3 * a + b + 1, :]
            high = tap.astype(jnp.bfloat16).astype(jnp.float32)
            total = jnp.where(group == a, high, total)
            total = jnp.where(group == 3 + a, tap - high, total)
        spread.append(total)
    for f in range(20):
        total = jnp.zeros((COLS, CHANNELS), jnp.float32)
        for b in range(3):
            total = jnp.where(at_bin == 2 * f + b, spread[b], total)
        taps_ref[:, f * CHANNELS : (f + 1) * CHANNELS] = total.astype(jnp.bfloat16)


def prepare(info, mel, w_first, tokens, limit):
    bins = mel.shape[1]
    reach = 4 * (HALO + EDGE)
    tm = lax.axis_size("tm")
    forward = [(i, i + 1) for i in range(tm - 1)]
    backward = [(i + 1, i) for i in range(tm - 1)]
    low = lax.ppermute(mel[mel.shape[0] - reach :], "tm", forward)
    high = lax.ppermute(mel[:reach], "tm", backward)
    quads = jnp.concatenate([low, mel, high], axis=0).reshape(-1, 4 * bins)
    count = tokens + 2 * HALO
    quads = jnp.concatenate(
        [quads[EDGE - 1 : EDGE - 1 + count], quads[EDGE : EDGE + count]], axis=1
    )
    lane = np.arange(COLS)
    frame, at_bin = lane // BINS % 3, lane % BINS
    used = lane < 6 * BINS
    picks = np.full((8, COLS), -1, np.int32)
    for a in range(3):
        for h in range(2):
            wanted = at_bin - 1 + 40 * h
            place = bins * (2 * a + frame + 1) + wanted
            picks[2 * a + h] = np.where(used & (wanted >= 0), place, -1)
    picks[6] = frame
    whole = pl.BlockSpec(memory_space=pltpu.VMEM)
    return pl.pallas_call(
        functools.partial(prepare_kernel, limit),
        out_shape=(
            jax.ShapeDtypeStruct((3, 2, count, COLS), jnp.bfloat16),
            jax.ShapeDtypeStruct((COLS, 20 * CHANNELS), jnp.bfloat16),
        ),
        in_specs=[pl.BlockSpec(memory_space=pltpu.SMEM)] + [whole] * 3,
        out_specs=(whole, whole),
        compiler_params=pltpu.CompilerParams(vmem_limit_bytes=24 * 1024 * 1024),
        cost_estimate=pl.CostEstimate(
            flops=12 * count * 768 * COLS, bytes_accessed=6 * 1024 * 1024, transcendentals=0
        ),
        name="prepare",
    )(info, quads, jnp.asarray(picks), w_first.reshape(9, CHANNELS))


def conv_kernel(begin, count, a_ref, b_ref, w_ref, out_ref, first):
    tokens = out_ref.shape[0]
    rows_step = tokens // 2

    @pl.loop(0, 2)
    def _(r):
        rows = pl.ds(pl.multiple_of(r * rows_step, 16), rows_step)
        for a in range(3):
            for i in range(2 * count + 1):
                at = 2 * begin - 1 + i
                place = slice(i * COLS, (i + 1) * COLS)
                if at < 0:
                    first[a, :, place] = jnp.zeros((rows_step, COLS), jnp.bfloat16)
                    continue
                half, col = divmod(at, 20)
                made = jnp.dot(
                    a_ref[a, half, rows, :],
                    b_ref[:, col * COLS : (col + 1) * COLS],
                    preferred_element_type=jnp.float32,
                )
                first[a, :, place] = jnp.maximum(made, 0.0).astype(jnp.bfloat16)
        for t in range(count):
            total = None
            for a in range(3):
                made = jnp.dot(
                    first[a, :, 2 * t * COLS : (2 * t + 3) * COLS],
                    w_ref[a],
                    preferred_element_type=jnp.float32,
                )
                total = made if total is None else total + made
            out_ref[rows, t * COLS : (t + 1) * COLS] = jnp.maximum(total, 0.0).astype(jnp.bfloat16)


def subsample(patches, taps, w_second):
    tokens = patches.shape[2]
    count = 4
    weights = w_second.reshape(3, 3 * COLS, COLS)
    whole = pl.BlockSpec(memory_space=pltpu.VMEM)
    flops = 2 * tokens * COLS * COLS * (3 * (2 * count + 1) + 9 * count)
    pieces = []
    for begin in range(0, 20, count):
        pieces.append(
            pl.pallas_call(
                functools.partial(conv_kernel, begin, count),
                out_shape=jax.ShapeDtypeStruct((tokens, count * CHANNELS), jnp.bfloat16),
                in_specs=[whole] * 3,
                out_specs=whole,
                scratch_shapes=[
                    pltpu.VMEM((3, tokens // 2, (2 * count + 1) * COLS), jnp.bfloat16)
                ],
                compiler_params=pltpu.CompilerParams(vmem_limit_bytes=20 * 1024 * 1024),
                cost_estimate=pl.CostEstimate(
                    flops=flops, bytes_accessed=8 * 1024 * 1024, transcendentals=0
                ),
                name="subsample",
            )(patches, taps, weights)
        )
    return pieces


def project_kernel(places, info_ref, gain_ref, *rest):
    subs = rest[:5]
    sources = rest[5:-5]
    mid_ref, normed_ref, weights, hidden, sem = rest[-5:]
    copies_in(info_ref, sources, places, weights, sem)
    pltpu.make_async_copy(weights, weights, sem).wait()

    depth = weights.shape[0] // len(subs)

    @pl.loop(0, WIDTH // COLS)
    def _(n):
        here = pl.ds(pl.multiple_of(n * COLS, COLS), COLS)
        total = None
        for piece, sub in enumerate(subs):
            made = jnp.dot(
                sub[...],
                weights[piece * depth : (piece + 1) * depth, here],
                preferred_element_type=jnp.float32,
            )
            total = made if total is None else total + made
        hidden[:, here] = total

    gain = gain_ref[...]
    chunk = 160

    @pl.loop(0, hidden.shape[0] // chunk)
    def _(r):
        rows = pl.ds(pl.multiple_of(r * chunk, chunk), chunk)
        normed_ref[rows, :] = layer_norm(hidden[rows, :], gain).astype(jnp.bfloat16)

    mid_ref[...] = hidden[WINDOW : WINDOW + mid_ref.shape[0], :]


def project(info, gain, subs, sources, places, tokens):
    rows_all = tokens + 2 * HALO
    rows_mid = tokens + 2 * EDGE
    whole = pl.BlockSpec(memory_space=pltpu.VMEM)
    depth = sum(sub.shape[1] for sub in subs)
    return pl.pallas_call(
        functools.partial(project_kernel, places),
        out_shape=(
            jax.ShapeDtypeStruct((rows_mid, WIDTH), jnp.float32),
            jax.ShapeDtypeStruct((rows_all, WIDTH), jnp.bfloat16),
        ),
        in_specs=[pl.BlockSpec(memory_space=pltpu.SMEM)]
        + [whole] * 6
        + [pl.BlockSpec(memory_space=pl.ANY)] * len(sources),
        out_specs=(whole, whole),
        scratch_shapes=[
            pltpu.VMEM((depth, WIDTH), jnp.bfloat16),
            pltpu.VMEM((rows_all, WIDTH), jnp.float32),
            pltpu.SemaphoreType.DMA(()),
        ],
        compiler_params=pltpu.CompilerParams(vmem_limit_bytes=34 * 1024 * 1024),
        cost_estimate=pl.CostEstimate(
            flops=2 * rows_all * depth * WIDTH, bytes_accessed=24 * 1024 * 1024, transcendentals=0
        ),
        name="project",
    )(info, gain, *subs, *sources)


def pack_kernel(pieces, *refs):
    *sources, out_ref, held, sems = refs
    at = 0
    copies = []
    for source, first in pieces:
        rows = sources[source].shape[0]
        copies.append(
            pltpu.make_async_copy(
                sources[source].at[:, pl.ds(first, WIDTH)],
                held.at[pl.ds(at, rows), :],
                sems.at[len(copies)],
            )
        )
        at += rows
    for copy in copies:
        copy.start()
    for copy in copies:
        copy.wait()
    out = pltpu.make_async_copy(held, out_ref, sems.at[len(copies)])
    out.start()
    out.wait()


def pack(arrays):
    pieces = [
        (k, first) for k, array in enumerate(arrays) for first in range(0, array.shape[1], WIDTH)
    ]
    if any(array.shape[0] % 16 for array in arrays):
        return jnp.concatenate([arrays[k][:, c : c + WIDTH] for k, c in pieces], axis=0)
    rows = sum(arrays[k].shape[0] for k, _ in pieces)
    far = pl.BlockSpec(memory_space=pltpu.HBM)
    return pl.pallas_call(
        functools.partial(pack_kernel, pieces),
        out_shape=jax.ShapeDtypeStruct((rows, WIDTH), jnp.bfloat16),
        in_specs=[far] * len(arrays),
        out_specs=far,
        scratch_shapes=[
            pltpu.VMEM((rows, WIDTH), jnp.bfloat16),
            pltpu.SemaphoreType.DMA((len(pieces) + 1,)),
        ],
        compiler_params=pltpu.CompilerParams(vmem_limit_bytes=60 * 1024 * 1024),
        cost_estimate=pl.CostEstimate(
            flops=0, bytes_accessed=4 * rows * WIDTH, transcendentals=0
        ),
        name="pack",
    )(*arrays)


def columns(weights, part, parts, n):
    rows = weights.shape[1] // parts
    return weights[:, part * rows : (part + 1) * rows, n * COLS : (n + 1) * COLS].reshape(-1, COLS)


def block_kernel(
    tokens,
    limit,
    info_ref,
    normed_ref,
    gain_conv_ref,
    depth_ref,
    gain_out_ref,
    hidden_ref,
    weights_ref,
    out_ref,
    early_w,
    late_w,
    keys,
    values,
    queries,
    context,
    attended,
    gated,
    masks,
    biases,
    sems,
):
    rows_mid = tokens + 2 * EDGE
    share = early_w.shape[1] // 3
    early_copies = []
    for k in range(3):
        part = pl.ds(k * share, share)
        early_copies.append(
            pltpu.make_async_copy(
                weights_ref.at[:, part, :], early_w.at[:, part, :], sems.at[k]
            )
        )
    late_copies = []
    for k in range(4):
        late_copies.append(
            pltpu.make_async_copy(
                weights_ref.at[:, pl.ds((3 + k) * share, share), :],
                late_w.at[:, pl.ds(k * share, share), :],
                sems.at[3 + k],
            )
        )
    hidden_copy = pltpu.make_async_copy(hidden_ref, attended, sems.at[7])
    for copy in early_copies:
        copy.start()
    base = info_ref[0]
    lengths = [info_ref[1 + k] for k in range(4)]

    blocks = []
    at_row = 0
    while at_row < rows_mid:
        size = 128 + (EDGE if at_row == 0 or at_row + 128 + EDGE == rows_mid else 0)
        blocks.append((at_row, size))
        at_row += size

    for at, (start, size) in enumerate(blocks):
        span = size + 2 * WINDOW
        q_row = lax.broadcasted_iota(jnp.int32, (size, 1), 0)
        k_row = lax.broadcasted_iota(jnp.int32, (1, span), 1)
        q_seg = segment_of(base + 4 * (q_row + start - EDGE), lengths, limit)
        k_seg = segment_of(base + 4 * (k_row + start - HALO), lengths, limit)
        apart = k_row - q_row
        allowed = (apart >= 0) & (apart <= 2 * WINDOW) & (q_seg == k_seg)
        biases[at, 0:size, 0:span] = jnp.where(allowed, 0.0, -1e30)
    for head in range(HEADS):
        values[:, (2 * head + 1) * HEAD_DIM : (2 * head + 2) * HEAD_DIM] = jnp.ones(
            (values.shape[0], HEAD_DIM), jnp.bfloat16
        )

    early_copies[0].wait()
    hidden_copy.start()
    for copy in late_copies:
        copy.start()
    for n in range(WIDTH // COLS):
        queries[:, n * COLS : (n + 1) * COLS] = jnp.dot(
            normed_ref[WINDOW : WINDOW + rows_mid, :],
            columns(early_w, 0, 3, n),
            preferred_element_type=jnp.float32,
        ).astype(jnp.bfloat16)
    row = lax.broadcasted_iota(jnp.int32, (tokens, HEAD_DIM), 0)
    own = segment_of(base + 4 * row, lengths, limit)
    for k in range(KERNEL):
        there = segment_of(base + 4 * (row + k - KERNEL // 2), lengths, limit)
        masks[k] = (there == own).astype(jnp.float32)
    early_copies[1].wait()
    for n in range(WIDTH // COLS):
        keys[:, n * COLS : (n + 1) * COLS] = jnp.dot(
            normed_ref[...], columns(early_w, 1, 3, n), preferred_element_type=jnp.float32
        ).astype(jnp.bfloat16)
    early_copies[2].wait()
    for n in range(WIDTH // COLS):
        made = jnp.dot(
            normed_ref[...], columns(early_w, 2, 3, n), preferred_element_type=jnp.float32
        ).astype(jnp.bfloat16)
        for k in range(COLS // HEAD_DIM):
            first = 2 * n * COLS + 2 * k * HEAD_DIM
            values[:, first : first + HEAD_DIM] = made[:, k * HEAD_DIM : (k + 1) * HEAD_DIM]

    scale = HEAD_DIM**-0.5 * 1.4426950408889634

    @pl.loop(0, HEADS // 4)
    def _(four):
        for at, (start, size) in enumerate(blocks):
            span = size + 2 * WINDOW
            for side in range(4):
                head = 4 * four + side
                lanes = pl.ds(pl.multiple_of(head * HEAD_DIM, HEAD_DIM), HEAD_DIM)
                wide = pl.ds(pl.multiple_of(head * 2 * HEAD_DIM, 2 * HEAD_DIM), 2 * HEAD_DIM)
                scores = lax.dot_general(
                    queries[start : start + size, lanes],
                    keys[start : start + span, lanes],
                    (((1,), (1,)), ((), ())),
                    preferred_element_type=jnp.float32,
                )
                scores = scores * scale + biases[at, 0:size, 0:span]
                exped = jnp.exp2(scores - jnp.max(scores, axis=-1, keepdims=True))
                mixed = jnp.dot(
                    exped.astype(jnp.bfloat16),
                    values[start : start + span, wide],
                    preferred_element_type=jnp.float32,
                )
                context[start : start + size, lanes] = (
                    mixed[:, :HEAD_DIM] / mixed[:, HEAD_DIM:]
                ).astype(jnp.bfloat16)

    hidden_copy.wait()
    late_copies[0].wait()
    gain_c = gain_conv_ref[...]
    half = rows_mid // 2
    for r in range(2):
        rows = slice(r * half, (r + 1) * half)
        for n in range(WIDTH // COLS):
            attended[rows, n * COLS : (n + 1) * COLS] += jnp.dot(
                context[rows, :], columns(late_w, 0, 4, n), preferred_element_type=jnp.float32
            )
        queries[rows, :] = layer_norm(attended[rows, :], gain_c).astype(jnp.bfloat16)

    late_copies[1].wait()
    late_copies[2].wait()
    for n in range(WIDTH // COLS):
        value = jnp.dot(queries[...], columns(late_w, 1, 4, n), preferred_element_type=jnp.float32)
        gate = jnp.dot(queries[...], columns(late_w, 2, 4, n), preferred_element_type=jnp.float32)
        made = (value * jax.nn.sigmoid(gate)).astype(jnp.bfloat16).astype(jnp.float32)
        for j in range(COLS // HEAD_DIM):
            at = n * (COLS // HEAD_DIM) + j
            gated[at] = made[:, j * HEAD_DIM : (j + 1) * HEAD_DIM]
            lanes = slice(at * HEAD_DIM, (at + 1) * HEAD_DIM)
            total = jnp.zeros((tokens, HEAD_DIM), jnp.float32)
            for k in range(KERNEL):
                begin = EDGE - KERNEL // 2 + k
                tap = gated[at, begin : begin + tokens, :] * depth_ref[k : k + 1, lanes]
                total = total + (tap if k == KERNEL // 2 else tap * masks[k])
            context[0:tokens, lanes] = (total * jax.nn.sigmoid(total)).astype(jnp.bfloat16)

    late_copies[3].wait()
    gain_o = gain_out_ref[...]
    half = tokens // 2
    for r in range(2):
        rows = slice(r * half, (r + 1) * half)
        mid = slice(EDGE + r * half, EDGE + (r + 1) * half)
        for n in range(WIDTH // COLS):
            attended[mid, n * COLS : (n + 1) * COLS] += jnp.dot(
                context[rows, :], columns(late_w, 3, 4, n), preferred_element_type=jnp.float32
            )
        out_ref[rows, :] = layer_norm(attended[mid, :], gain_o).astype(jnp.bfloat16)


def conformer_block(info, hidden, normed, weights, gain_conv, w_depth, gain_out, limit):
    rows_all = normed.shape[0]
    rows_mid = hidden.shape[0]
    tokens = rows_mid - 2 * EDGE
    whole = pl.BlockSpec(memory_space=pltpu.VMEM)
    far = pl.BlockSpec(memory_space=pltpu.HBM)
    flops = 2 * rows_all * WIDTH * 2 * WIDTH + 2 * rows_mid * WIDTH * WIDTH * 5
    return pl.pallas_call(
        functools.partial(block_kernel, tokens, limit),
        out_shape=jax.ShapeDtypeStruct((tokens, WIDTH), jnp.bfloat16),
        in_specs=[pl.BlockSpec(memory_space=pltpu.SMEM)] + [whole] * 4 + [far] * 2,
        out_specs=whole,
        scratch_shapes=[
            pltpu.VMEM((32, 3 * WIDTH // 32, WIDTH), jnp.bfloat16),
            pltpu.VMEM((32, 4 * WIDTH // 32, WIDTH), jnp.bfloat16),
            pltpu.VMEM((rows_all, WIDTH), jnp.bfloat16),
            pltpu.VMEM((rows_all, 2 * WIDTH), jnp.bfloat16),
            pltpu.VMEM((rows_mid, WIDTH), jnp.bfloat16),
            pltpu.VMEM((rows_mid, WIDTH), jnp.bfloat16),
            pltpu.VMEM((rows_mid, WIDTH), jnp.float32),
            pltpu.VMEM((WIDTH // HEAD_DIM, rows_mid, HEAD_DIM), jnp.float32),
            pltpu.VMEM((KERNEL, tokens, HEAD_DIM), jnp.float32),
            pltpu.VMEM((4, 128 + EDGE, 512), jnp.float32),
            pltpu.SemaphoreType.DMA((8,)),
        ],
        compiler_params=pltpu.CompilerParams(vmem_limit_bytes=60 * 1024 * 1024),
        cost_estimate=pl.CostEstimate(
            flops=flops, bytes_accessed=24 * 1024 * 1024, transcendentals=4 * 1024 * 1024
        ),
        name="conformer_block",
    )(info, normed, gain_conv, w_depth, gain_out, hidden, weights)


def on_device(
    mel_frames,
    lengths,
    w_first,
    w_second,
    w_proj,
    gain_attn,
    w_qkv,
    w_out,
    gain_conv,
    w_point_in,
    w_depth,
    w_point_out,
    gain_out,
):
    tokens = mel_frames.shape[1] // 4
    limit = mel_frames.shape[1] * lax.axis_size("tm")
    base = lax.axis_index("tm") * mel_frames.shape[1]
    info = jnp.concatenate(
        [
            jnp.reshape(base, (1,)),
            lengths[0],
            jnp.stack([lax.axis_index("rec"), lax.axis_index("tm")]),
            jnp.full((1,), lax.axis_size("tm"), jnp.int32),
        ]
    ).astype(jnp.int32)

    def gather_packed(arrays):
        packed = pack(arrays)
        full = lax.all_gather(packed, ("rec", "tm"), axis=0, tiled=False)
        if full.shape[0] == 32:
            return full
        parts = packed.shape[0] // w_out.shape[0]
        full = full.reshape(full.shape[0], parts, -1, WIDTH).transpose(1, 0, 2, 3)
        full = full.reshape(parts, 32, -1, WIDTH).transpose(1, 0, 2, 3)
        return full.reshape(32, -1, WIDTH)

    late = gather_packed([w_qkv, w_out, w_point_in, w_point_out])
    w_second_all, rounds = gather_ordered(w_second)
    patches, taps = prepare(info, mel_frames[0], w_first, tokens, limit)
    subs = subsample(patches, taps, w_second_all)
    if lax.axis_size("rec") == 4 and lax.axis_size("tm") == 8:
        proj = along_rec(behind(w_proj, *rounds[0]))
        proj = behind(tuple(proj), patches, *rounds[1], *subs[:2])
        proj = to_neighbours(jnp.concatenate(proj, axis=0))
        proj_late = relayed(*behind(proj, *subs))
        proj, places = to_other_core(*proj, *proj_late)
    else:
        proj, places = [lax.all_gather(w_proj, ("rec", "tm"), axis=0, tiled=True)], None
    hidden, normed = project(info, gain_attn[None], subs, proj, places, tokens)
    encoded = conformer_block(
        info,
        hidden,
        normed,
        late,
        gain_conv[None],
        w_depth,
        gain_out[None],
        limit,
    )
    return encoded[None]


def solution(mesh):
    placed = (
        P("rec", "tm", None),
        P("rec", None),
        P(),
        P(("rec", "tm"), None),
        P(("rec", "tm"), None),
        P(),
        P(("rec", "tm"), None),
        P(("rec", "tm"), None),
        P(),
        P(("rec", "tm"), None),
        P(),
        P(("rec", "tm"), None),
        P(),
    )
    return jax.shard_map(
        on_device, mesh=mesh, in_specs=placed, out_specs=P("rec", "tm", None), check_vma=False
    )
```
